32 devices in a mesh: ckpt: 4 (over y, x), vocab: 8 (over z, core).
Axes of the slice: x: 2, y: 2, z: 4, core: 2. Of those that a mesh axis runs over, the one named last changes fastest.
Arguments:
- token_ids: int32 [1024], P('vocab'), may hold values from 0 to 1023, as said below
- grad_values: bfloat16 [4, 1024, 8192], P('ckpt', 'vocab'), may hold values from -6 to 6
- grad_scales: float32 [4, 64, 1024], P('ckpt', None, 'vocab'), may hold values from 0.3 to 3
- tables: bfloat16 [4, 1024, 8192], P('ckpt', 'vocab'), may hold values from -6 to 6
Outputs:
- merged: bfloat16 [1024, 8192], P('vocab', 'ckpt')
The draws below stay inside these ranges and needn't reach their ends.
Inputs may be any that keep to these rules, and one draw needn't show every extreme that they name: The owner of a token is token_ids // 128. Among the 128 tokens of each index of vocab, exactly 4 owners appear, each with exactly 32 tokens; one owner appears in every index's tokens. Ids repeat and some owners are far more frequent than others.
All inputs are finite; a program needn't handle non-finite values.
Results may differ from the reference program's by a relative error of at most 0.018.
Values may be sent and summed in bfloat16 or wider, within the bound.
A program may use at most 64 MiB of HBM per device.

```python
import math
import jax
import jax.numpy as jnp
from jax import lax

D = 8192
BLK = 128
R_DEV = 128
TOK_DEV = 128
CKPT = 4
CAP = 32
VOCAB = 1024
TOKENS = 1024


def draw_token_ids(key, part):
    owners_all = VOCAB // R_DEV
    chosen = TOK_DEV // CAP
    hotness = jax.random.randint(jax.random.fold_in(key, 1), (owners_all,), 1, 9)
    starred = jax.random.randint(jax.random.fold_in(key, 2), (), 0, owners_all)
    keys = jax.random.split(jax.random.fold_in(key, 3), owners_all)
    positions = jnp.arange(owners_all, dtype=jnp.int32)

    def one_device(dkey):
        noise = jax.random.randint(jax.random.fold_in(dkey, 1), (owners_all,), 0, 4096)
        score = noise * hotness * owners_all + positions
        score = jnp.where(positions == starred, 2 ** 28, score)
        picked = lax.top_k(score, chosen)[1].astype(jnp.int32)
        repeated = jnp.repeat(picked, CAP)
        first = jax.random.randint(jax.random.fold_in(dkey, 2), (TOK_DEV,), 0, R_DEV)
        second = jax.random.randint(jax.random.fold_in(dkey, 3), (TOK_DEV,), 0, R_DEV)
        rows = jnp.minimum(first, second)
        ids = repeated * R_DEV + rows
        order = jax.random.permutation(jax.random.fold_in(dkey, 4), TOK_DEV)
        return ids[order].astype(jnp.int32)
    return jax.vmap(one_device)(keys).reshape(TOKENS)


def block_scale(stream_key, shape, cuts, smallest, top_value):
    level, own = 1.0, jax.random.fold_in(stream_key, 6)
    for axis_at, shards_of in cuts:
        heights = jnp.exp(jax.random.uniform(jax.random.fold_in(own, axis_at), (shards_of,), jnp.float32, smallest / len(cuts), top_value / len(cuts)))
        level = level * jnp.repeat(heights, shape[axis_at] // shards_of).reshape([-1 if axis == axis_at else 1 for axis in range(len(shape))])
    return level


def centred(key, dims, spread, limit, pieces=(), kind=jnp.bfloat16):
    factor_of = block_scale(key, dims, pieces, -0.22, 0.18) if pieces else 1.0
    drawn = jax.random.normal(key, dims, jnp.float32) * spread * factor_of
    return jnp.minimum(jnp.maximum(drawn, -limit), limit).astype(kind)


def setup_inputs(seed: int = 0) -> dict:
    seeds = jax.random.split(jax.random.key(seed), 5)
    token_ids = draw_token_ids(jax.random.fold_in(seeds[4], 71), 0)
    grad_values = centred(seeds[1], (CKPT, TOKENS, D), 1.0, 6.0, ((0, 4), (1, 8)))
    grad_scales = jnp.clip(jnp.exp(math.log(3.0) - 2.3025851 * jax.random.uniform(seeds[2], (CKPT, D // BLK, TOKENS), jnp.float32) ** block_scale(seeds[2], (CKPT, D // BLK, TOKENS), ((0, 4), (2, 8)), -0.2, 0.2)), 0.3, 3.0)
    tables = centred(seeds[3], (CKPT, VOCAB, D), 1.0, 6.0, ((0, 4), (1, 8)))
    return dict(token_ids=token_ids, grad_values=grad_values, grad_scales=grad_scales, tables=tables)


prior_weight = 1.0


def reference(token_ids, grad_values, grad_scales, tables):
    numer = jnp.zeros((VOCAB, D), jnp.float32)
    denom = jnp.zeros((VOCAB, D), jnp.float32)
    for index in range(CKPT):
        scales = grad_scales[index].T
        grads = grad_values[index].astype(jnp.float32).reshape(TOKENS, D // BLK, BLK) * scales[:, :, None]
        squares = (grads * grads).reshape(TOKENS, D).astype(jnp.bfloat16)
        fisher = jax.ops.segment_sum(squares.astype(jnp.float32), token_ids, num_segments=VOCAB)
        weight = (fisher + prior_weight).astype(jnp.bfloat16)
        term = (weight.astype(jnp.float32) * tables[index].astype(jnp.float32)).astype(jnp.bfloat16)
        numer = numer + term.astype(jnp.float32)
        denom = denom + weight.astype(jnp.float32)
    return (numer / denom).astype(jnp.bfloat16)
```

```python
import functools

import jax
import jax.numpy as jnp
from jax import lax
from jax.experimental import pallas as pl
from jax.experimental.pallas import tpu as pltpu
from jax.sharding import PartitionSpec as P

BLK = 128
CHUNKS = 8
MESH = pl.DeviceIdType.MESH


prior_weight = 1.0


def merge_kernel(
    groups,
    ckpts,
    chunks,
    ids_row_ref,
    ids_col_ref,
    grads_ref,
    scales_ref,
    tables_ref,
    out_ref,
    grads,
    tables,
    match_ref,
    select_ref,
    tag_send,
    tag_recv,
    send,
    recv,
    part_send,
    part_recv,
    load_sem,
    tag_send_sem,
    tag_recv_sem,
    send_sem,
    recv_sem,
    part_send_sem,
    part_recv_sem,
):
    c = lax.axis_index("ckpt")
    v = lax.axis_index("vocab")
    rows = tables.shape[0]
    count = grads.shape[0]
    width = grads.shape[1]
    slots = match_ref.shape[0]
    capacity = slots // groups
    quarter = width // ckpts
    piece = quarter // chunks
    blocks = piece // BLK

    def vocab_peer(j):
        return (c, lax.rem(v + j, groups))

    def ckpt_peer(j):
        return (lax.rem(c + j, ckpts), v)

    barrier = pltpu.get_barrier_semaphore()
    for j in range(1, groups):
        pl.semaphore_signal(barrier, inc=1, device_id=vocab_peer(j), device_id_type=MESH)
    for j in range(1, ckpts):
        pl.semaphore_signal(barrier, inc=1, device_id=ckpt_peer(j), device_id_type=MESH)

    load_grads = pltpu.make_async_copy(grads_ref, grads, load_sem.at[0])
    load_tables = pltpu.make_async_copy(tables_ref, tables, load_sem.at[1])
    load_grads.start()
    load_tables.start()

    ids_row = ids_row_ref[...]
    ids_col = ids_col_ref[...]
    near_row = lax.rem(ids_row // rows - v + groups, groups)
    near_col = lax.rem(ids_col // rows - v + groups, groups)
    same = near_row == near_col
    at0 = lax.broadcasted_iota(jnp.int32, (count, count), 0)
    at1 = lax.broadcasted_iota(jnp.int32, (count, count), 1)
    rank_row = jnp.sum(jnp.where(same & (at0 < at1), 1, 0), axis=0, keepdims=True)
    rank_col = jnp.sum(jnp.where(same & (at1 < at0), 1, 0), axis=1, keepdims=True)
    slot_row = near_row * capacity + rank_row
    slot_col = near_col * capacity + rank_col
    match_ref[...] = jnp.where(
        lax.broadcasted_iota(jnp.int32, (slots, count), 0) == slot_row, 1.0, 0.0
    ).astype(jnp.bfloat16)
    tags = jnp.sum(
        jnp.where(
            lax.broadcasted_iota(jnp.int32, (count, slots), 1) == slot_col,
            lax.rem(ids_col, rows),
            0,
        ),
        axis=0,
        keepdims=True,
    )
    tag_send[...] = jnp.broadcast_to(tags, tag_send.shape)

    def tag_copy(j):
        return pltpu.make_async_remote_copy(
            src_ref=tag_send,
            dst_ref=tag_recv.at[j],
            send_sem=tag_send_sem.at[j],
            recv_sem=tag_recv_sem.at[j],
            device_id=vocab_peer(j),
            device_id_type=MESH,
        )

    def row_copy(k, j):
        return pltpu.make_async_remote_copy(
            src_ref=send.at[k, j],
            dst_ref=recv.at[k, j],
            send_sem=send_sem.at[k, j],
            recv_sem=recv_sem.at[k, j],
            device_id=vocab_peer(j),
            device_id_type=MESH,
        )

    def part_copy(k, j):
        return pltpu.make_async_remote_copy(
            src_ref=part_send.at[k, j],
            dst_ref=part_recv.at[k, j],
            send_sem=part_send_sem.at[k, j],
            recv_sem=part_recv_sem.at[k, j],
            device_id=ckpt_peer(j),
            device_id_type=MESH,
        )

    order = sorted(range(1, groups), key=lambda j: -min(j, groups - j))

    load_grads.wait()
    pl.semaphore_wait(barrier, groups + ckpts - 2)
    for j in order:
        tag_copy(j).start()

    def place(k, carry):
        block_scales = jnp.concatenate(
            [
                scales_ref[pl.ds(q * (quarter // BLK) + k * blocks, blocks), :]
                for q in range(ckpts)
            ],
            axis=0,
        ).T
        squares = []
        for q in range(ckpts):
            for b in range(blocks):
                at = pl.multiple_of(q * quarter + k * piece + b * BLK, BLK)
                i = q * blocks + b
                g = grads[:, pl.ds(at, BLK)].astype(jnp.float32) * block_scales[:, i : i + 1]
                squares.append((g * g).astype(jnp.bfloat16))
        placed = jnp.dot(
            match_ref[...],
            jnp.concatenate(squares, axis=1),
            preferred_element_type=jnp.float32,
        ).astype(jnp.bfloat16)
        placed = placed.reshape(groups, capacity, ckpts * piece)
        recv[k, 0] = placed[0]
        for j in range(1, groups):
            send[k, j] = placed[j]
        for j in order:
            row_copy(k, j).start()
        return carry

    lax.fori_loop(0, chunks, place, 0)

    lane = lax.broadcasted_iota(jnp.int32, (1, slots), 1) // capacity
    arrived_tags = jnp.where(lane == 0, tags, 0)
    for j in range(1, groups):
        tag_copy(j).wait()
        arrived_tags = jnp.where(lane == j, tag_recv[j, 0:1, :], arrived_tags)
    select_ref[...] = jnp.where(
        lax.broadcasted_iota(jnp.int32, (rows, slots), 0) == arrived_tags, 1.0, 0.0
    ).astype(jnp.bfloat16)
    load_tables.wait()

    def weigh_chunk(k):
        for j in range(1, groups):
            row_copy(k, j).wait_recv()
        fisher = jnp.dot(
            select_ref[...],
            recv[k].reshape(slots, ckpts * piece),
            preferred_element_type=jnp.float32,
        )
        weight = (fisher + prior_weight).astype(jnp.bfloat16)
        for q in range(ckpts):
            own = weight[:, q * piece : (q + 1) * piece]
            at = pl.multiple_of(q * quarter + k * piece, BLK)
            table = tables[:, pl.ds(at, piece)].astype(jnp.float32)
            j = lax.rem(q - c + ckpts, ckpts)
            part_send[k, j, 0] = (own.astype(jnp.float32) * table).astype(jnp.bfloat16)
            part_send[k, j, 1] = own
        for j in range(1, ckpts):
            part_copy(k, j).start()

    def finish_chunk(k):
        numer = part_send[k, 0, 0].astype(jnp.float32)
        denom = part_send[k, 0, 1].astype(jnp.float32)
        for j in range(1, ckpts):
            part_copy(k, j).wait_recv()
            numer += part_recv[k, j, 0].astype(jnp.float32)
            denom += part_recv[k, j, 1].astype(jnp.float32)
        at = pl.multiple_of(k * piece, BLK)
        out_ref[:, pl.ds(at, piece)] = (numer / denom).astype(jnp.bfloat16)

    weigh_chunk(0)

    def step(k, carry):
        weigh_chunk(k)
        finish_chunk(k - 1)
        return carry

    lax.fori_loop(1, chunks, step, 0)
    finish_chunk(chunks - 1)

    def drain(k, carry):
        for j in range(1, groups):
            row_copy(k, j).wait_send()
        for j in range(1, ckpts):
            part_copy(k, j).wait_send()
        return carry

    lax.fori_loop(0, chunks, drain, 0)


def merge_rows(token_ids, grad_values, grad_scales, tables):
    groups = lax.axis_size("vocab")
    ckpts = lax.axis_size("ckpt")
    rows, width = tables.shape[1:]
    count = token_ids.shape[0]
    slots = 2 * count
    capacity = slots // groups
    chunk_width = width // CHUNKS
    vmem = pl.BlockSpec(memory_space=pltpu.VMEM)
    hbm = pl.BlockSpec(memory_space=pl.ANY)
    bf16 = jnp.bfloat16
    dma = pltpu.SemaphoreType.DMA
    return pl.pallas_call(
        functools.partial(merge_kernel, groups, ckpts, CHUNKS),
        out_shape=jax.ShapeDtypeStruct((rows, width // ckpts), bf16),
        in_specs=[vmem, vmem, hbm, vmem, hbm],
        out_specs=vmem,
        scratch_shapes=[
            pltpu.VMEM((count, width), bf16),
            pltpu.VMEM((rows, width), bf16),
            pltpu.VMEM((slots, count), bf16),
            pltpu.VMEM((rows, slots), bf16),
            pltpu.VMEM((8, slots), jnp.int32),
            pltpu.VMEM((groups, 8, slots), jnp.int32),
            pltpu.VMEM((CHUNKS, groups, capacity, chunk_width), bf16),
            pltpu.VMEM((CHUNKS, groups, capacity, chunk_width), bf16),
            pltpu.VMEM((CHUNKS, ckpts, 2, rows, chunk_width // ckpts), bf16),
            pltpu.VMEM((CHUNKS, ckpts, 2, rows, chunk_width // ckpts), bf16),
            dma((2,)),
            dma((groups,)),
            dma((groups,)),
            dma((CHUNKS, groups)),
            dma((CHUNKS, groups)),
            dma((CHUNKS, ckpts)),
            dma((CHUNKS, ckpts)),
        ],
        compiler_params=pltpu.CompilerParams(
            collective_id=0, has_side_effects=True, vmem_limit_bytes=48 * 1024 * 1024
        ),
        cost_estimate=pl.CostEstimate(
            flops=4 * slots * count * width,
            bytes_accessed=5 * rows * width,
            transcendentals=0,
        ),
    )(
        token_ids.reshape(1, count),
        token_ids.reshape(count, 1),
        grad_values[0],
        grad_scales[0],
        tables[0],
    )


def merge_small_slots(token_ids, grad_values, grad_scales, tables):
    groups = lax.axis_size("vocab")
    rows = tables.shape[1]
    width = tables.shape[2]
    count = token_ids.shape[0]
    capacity = 2 * count // groups
    owner = token_ids // rows
    same = owner[:, None] == owner[None, :]
    before = lax.broadcasted_iota(jnp.int32, (count, count), 0) < lax.broadcasted_iota(
        jnp.int32, (count, count), 1
    )
    rank = jnp.sum((same & before).astype(jnp.int32), axis=0)
    slot = owner * capacity + rank
    match = lax.broadcasted_iota(jnp.int32, (groups * capacity, count), 0) == slot[None, :]
    scales = grad_scales[0].T
    grads = (
        grad_values[0].astype(jnp.float32).reshape(count, width // BLK, BLK) * scales[:, :, None]
    )
    squares = (grads * grads).reshape(count, width).astype(jnp.bfloat16)
    placed = jnp.dot(match.astype(jnp.bfloat16), squares, preferred_element_type=jnp.float32)
    buffer = placed.astype(jnp.bfloat16).reshape(groups, capacity, width)
    local_rows = token_ids % rows
    row_tags = (
        jnp.sum(jnp.where(match, local_rows[None, :], 0), axis=1)
        .astype(jnp.bfloat16)
        .reshape(groups, capacity)
    )
    arrived, arrived_rows = (
        lax.all_to_all(buffer, "vocab", split_axis=0, concat_axis=0, tiled=True),
        lax.all_to_all(row_tags, "vocab", split_axis=0, concat_axis=0, tiled=True),
    )
    flat_rows = arrived_rows.reshape(groups * capacity).astype(jnp.int32)
    selector = (
        lax.broadcasted_iota(jnp.int32, (rows, groups * capacity), 0) == flat_rows[None, :]
    ).astype(jnp.bfloat16)
    fisher = jnp.dot(
        selector, arrived.reshape(groups * capacity, width), preferred_element_type=jnp.float32
    )
    weight = (fisher + prior_weight).astype(jnp.bfloat16)
    term = (weight.astype(jnp.float32) * tables[0].astype(jnp.float32)).astype(jnp.bfloat16)
    numer, denom = (
        lax.psum_scatter(term, "ckpt", scatter_dimension=1, tiled=True).astype(jnp.float32),
        lax.psum_scatter(weight, "ckpt", scatter_dimension=1, tiled=True).astype(jnp.float32),
    )
    return (numer / denom).astype(jnp.bfloat16)


def per_device(token_ids, grad_values, grad_scales, tables):
    groups = lax.axis_size("vocab")
    ckpts = lax.axis_size("ckpt")
    count = token_ids.shape[0]
    width = tables.shape[2]
    capacity = 2 * count // groups
    if capacity % 16 == 0 and width % (ckpts * CHUNKS * BLK) == 0:
        return merge_rows(token_ids, grad_values, grad_scales, tables)
    return merge_small_slots(token_ids, grad_values, grad_scales, tables)


def solution(mesh):
    return jax.shard_map(
        per_device,
        mesh=mesh,
        in_specs=(
            P("vocab"),
            P("ckpt", "vocab", None),
            P("ckpt", None, "vocab"),
            P("ckpt", "vocab", None),
        ),
        out_specs=P("vocab", "ckpt"),
        check_vma=False,
    )
```

```python
import functools

import jax
import jax.numpy as jnp
from jax import lax
from jax.experimental import pallas as pl
from jax.experimental.pallas import tpu as pltpu
from jax.sharding import PartitionSpec as P

BLK = 128
CHUNKS = 16
MESH = pl.DeviceIdType.MESH


prior_weight = 1.0


def merge_kernel(
    groups,
    ckpts,
    chunks,
    ids_ref,
    grads_ref,
    all_scales_ref,
    tables_ref,
    out_ref,
    grads,
    tables,
    scales_ref,
    match_ref,
    select_ref,
    tag_send,
    tag_recv,
    send,
    recv,
    part_send,
    part_recv,
    load_sem,
    tag_send_sem,
    tag_recv_sem,
    send_sem,
    recv_sem,
    part_send_sem,
    part_recv_sem,
):
    c = lax.axis_index("ckpt")
    v = lax.axis_index("vocab")
    rows = tables.shape[0]
    count = grads.shape[0]
    width = grads.shape[1]
    slots = match_ref.shape[0]
    capacity = slots // groups
    quarter = width // ckpts
    piece = quarter // chunks
    blocks = piece // BLK

    def vocab_peer(j):
        return (c, lax.rem(v + j, groups))

    def ckpt_peer(j):
        return (lax.rem(c + j, ckpts), v)

    barrier = pltpu.get_barrier_semaphore()
    for j in range(1, groups):
        pl.semaphore_signal(barrier, inc=1, device_id=vocab_peer(j), device_id_type=MESH)
    for j in range(1, ckpts):
        pl.semaphore_signal(barrier, inc=1, device_id=ckpt_peer(j), device_id_type=MESH)

    load_grads = pltpu.make_async_copy(grads_ref, grads, load_sem.at[0])
    load_tables = pltpu.make_async_copy(tables_ref, tables, load_sem.at[1])
    load_scales = pltpu.make_async_copy(all_scales_ref, scales_ref, load_sem.at[2])
    load_grads.start()
    load_scales.start()
    load_tables.start()

    ids_row = ids_ref[...]
    ids_col = jnp.broadcast_to(ids_row, (count, count)).T
    near_row = lax.rem(ids_row // rows - v + groups, groups)
    near_col = lax.rem(ids_col // rows - v + groups, groups)
    same = near_row == near_col
    at0 = lax.broadcasted_iota(jnp.int32, (count, count), 0)
    at1 = lax.broadcasted_iota(jnp.int32, (count, count), 1)
    rank_row = jnp.sum(jnp.where(same & (at0 < at1), 1, 0), axis=0, keepdims=True)
    rank_col = jnp.sum(jnp.where(same & (at1 < at0), 1, 0), axis=1, keepdims=True)
    slot_row = near_row * capacity + rank_row
    slot_col = near_col * capacity + rank_col
    match_ref[...] = jnp.where(
        lax.broadcasted_iota(jnp.int32, (slots, count), 0) == slot_row, 1.0, 0.0
    ).astype(jnp.bfloat16)
    tags = jnp.sum(
        jnp.where(
            lax.broadcasted_iota(jnp.int32, (count, slots), 1) == slot_col[:, 0:1],
            lax.rem(ids_col[:, 0:1], rows),
            0,
        ),
        axis=0,
        keepdims=True,
    )
    tag_send[...] = jnp.broadcast_to(tags, tag_send.shape)

    def tag_copy(j):
        return pltpu.make_async_remote_copy(
            src_ref=tag_send,
            dst_ref=tag_recv.at[j],
            send_sem=tag_send_sem.at[j],
            recv_sem=tag_recv_sem.at[j],
            device_id=vocab_peer(j),
            device_id_type=MESH,
        )

    def row_copy(k, j):
        return pltpu.make_async_remote_copy(
            src_ref=send.at[k, j],
            dst_ref=recv.at[k, j],
            send_sem=send_sem.at[k, j],
            recv_sem=recv_sem.at[k, j],
            device_id=vocab_peer(j),
            device_id_type=MESH,
        )

    def part_copy(k, j):
        return pltpu.make_async_remote_copy(
            src_ref=part_send.at[k, j],
            dst_ref=part_recv.at[k, j],
            send_sem=part_send_sem.at[k, j],
            recv_sem=part_recv_sem.at[k, j],
            device_id=ckpt_peer(j),
            device_id_type=MESH,
        )

    order = sorted(range(1, groups), key=lambda j: -min(j, groups - j))

    def place(k):
        block_scales = jnp.concatenate(
            [
                scales_ref[pl.ds(q * (quarter // BLK) + k * blocks, blocks), :]
                for q in range(ckpts)
            ],
            axis=0,
        ).T
        squares = []
        for q in range(ckpts):
            for b in range(blocks):
                at = pl.multiple_of(q * quarter + k * piece + b * BLK, BLK)
                i = q * blocks + b
                g = grads[:, pl.ds(at, BLK)].astype(jnp.float32) * block_scales[:, i : i + 1]
                squares.append((g * g).astype(jnp.bfloat16))
        placed = jnp.dot(
            match_ref[...],
            jnp.concatenate(squares, axis=1),
            preferred_element_type=jnp.float32,
        ).astype(jnp.bfloat16)
        placed = placed.reshape(groups, capacity, ckpts * piece)
        recv[k, 0] = placed[0]
        for j in range(1, groups):
            send[k, j] = placed[j]

    def start_rows(k):
        for j in order:
            row_copy(k, j).start()

    load_grads.wait()
    load_scales.wait()
    place(0)
    pl.semaphore_wait(barrier, groups + ckpts - 2)
    for j in order:
        tag_copy(j).start()
    start_rows(0)

    def place_next(k, carry):
        place(k)
        start_rows(k)
        return carry

    lax.fori_loop(1, chunks, place_next, 0)

    lane = lax.broadcasted_iota(jnp.int32, (1, slots), 1) // capacity
    arrived_tags = jnp.where(lane == 0, tags, 0)
    for j in range(1, groups):
        tag_copy(j).wait()
        arrived_tags = jnp.where(lane == j, tag_recv[j, 0:1, :], arrived_tags)
    select_ref[...] = jnp.where(
        lax.broadcasted_iota(jnp.int32, (rows, slots), 0) == arrived_tags, 1.0, 0.0
    ).astype(jnp.bfloat16)
    load_tables.wait()

    def weigh_chunk(k):
        for j in range(1, groups):
            row_copy(k, j).wait_recv()
        fisher = jnp.dot(
            select_ref[...],
            recv[k].reshape(slots, ckpts * piece),
            preferred_element_type=jnp.float32,
        )
        weight = (fisher + prior_weight).astype(jnp.bfloat16)
        for q in range(ckpts):
            own = weight[:, q * piece : (q + 1) * piece]
            at = pl.multiple_of(q * quarter + k * piece, BLK)
            table = tables[:, pl.ds(at, piece)].astype(jnp.float32)
            j = lax.rem(q - c + ckpts, ckpts)
            part_send[k, j, 0] = (own.astype(jnp.float32) * table).astype(jnp.bfloat16)
            part_send[k, j, 1] = own
        for j in range(1, ckpts):
            part_copy(k, j).start()

    def finish_chunk(k):
        numer = part_send[k, 0, 0].astype(jnp.float32)
        denom = part_send[k, 0, 1].astype(jnp.float32)
        for j in range(1, ckpts):
            part_copy(k, j).wait_recv()
            numer += part_recv[k, j, 0].astype(jnp.float32)
            denom += part_recv[k, j, 1].astype(jnp.float32)
        at = pl.multiple_of(k * piece, BLK)
        out_ref[:, pl.ds(at, piece)] = (numer / denom).astype(jnp.bfloat16)

    weigh_chunk(0)

    def step(k, carry):
        weigh_chunk(k)
        finish_chunk(k - 1)
        return carry

    lax.fori_loop(1, chunks, step, 0)
    finish_chunk(chunks - 1)

    def drain(k, carry):
        for j in range(1, groups):
            row_copy(k, j).wait_send()
        for j in range(1, ckpts):
            part_copy(k, j).wait_send()
        return carry

    lax.fori_loop(0, chunks, drain, 0)


def merge_rows(token_ids, grad_values, grad_scales, tables):
    groups = lax.axis_size("vocab")
    ckpts = lax.axis_size("ckpt")
    rows, width = tables.shape[1:]
    count = token_ids.shape[0]
    slots = 2 * count
    capacity = slots // groups
    chunk_width = width // CHUNKS
    vmem = pl.BlockSpec(memory_space=pltpu.VMEM)
    hbm = pl.BlockSpec(memory_space=pl.ANY)
    bf16 = jnp.bfloat16
    dma = pltpu.SemaphoreType.DMA
    return pl.pallas_call(
        functools.partial(merge_kernel, groups, ckpts, CHUNKS),
        out_shape=jax.ShapeDtypeStruct((rows, width // ckpts), bf16),
        in_specs=[vmem, hbm, hbm, hbm],
        out_specs=vmem,
        scratch_shapes=[
            pltpu.VMEM((count, width), bf16),
            pltpu.VMEM((rows, width), bf16),
            pltpu.VMEM((width // BLK, count), jnp.float32),
            pltpu.VMEM((slots, count), bf16),
            pltpu.VMEM((rows, slots), bf16),
            pltpu.VMEM((8, slots), jnp.int32),
            pltpu.VMEM((groups, 8, slots), jnp.int32),
            pltpu.VMEM((CHUNKS, groups, capacity, chunk_width), bf16),
            pltpu.VMEM((CHUNKS, groups, capacity, chunk_width), bf16),
            pltpu.VMEM((CHUNKS, ckpts, 2, rows, chunk_width // ckpts), bf16),
            pltpu.VMEM((CHUNKS, ckpts, 2, rows, chunk_width // ckpts), bf16),
            dma((3,)),
            dma((groups,)),
            dma((groups,)),
            dma((CHUNKS, groups)),
            dma((CHUNKS, groups)),
            dma((CHUNKS, ckpts)),
            dma((CHUNKS, ckpts)),
        ],
        compiler_params=pltpu.CompilerParams(
            collective_id=0, has_side_effects=True, vmem_limit_bytes=60 * 1024 * 1024
        ),
        cost_estimate=pl.CostEstimate(
            flops=4 * slots * count * width,
            bytes_accessed=5 * rows * width,
            transcendentals=0,
        ),
    )(
        token_ids.reshape(1, count),
        grad_values[0],
        grad_scales[0],
        tables[0],
    )


def merge_small_slots(token_ids, grad_values, grad_scales, tables):
    groups = lax.axis_size("vocab")
    rows = tables.shape[1]
    width = tables.shape[2]
    count = token_ids.shape[0]
    capacity = 2 * count // groups
    owner = token_ids // rows
    same = owner[:, None] == owner[None, :]
    before = lax.broadcasted_iota(jnp.int32, (count, count), 0) < lax.broadcasted_iota(
        jnp.int32, (count, count), 1
    )
    rank = jnp.sum((same & before).astype(jnp.int32), axis=0)
    slot = owner * capacity + rank
    match = lax.broadcasted_iota(jnp.int32, (groups * capacity, count), 0) == slot[None, :]
    scales = grad_scales[0].T
    grads = (
        grad_values[0].astype(jnp.float32).reshape(count, width // BLK, BLK) * scales[:, :, None]
    )
    squares = (grads * grads).reshape(count, width).astype(jnp.bfloat16)
    placed = jnp.dot(match.astype(jnp.bfloat16), squares, preferred_element_type=jnp.float32)
    buffer = placed.astype(jnp.bfloat16).reshape(groups, capacity, width)
    local_rows = token_ids % rows
    row_tags = (
        jnp.sum(jnp.where(match, local_rows[None, :], 0), axis=1)
        .astype(jnp.bfloat16)
        .reshape(groups, capacity)
    )
    arrived, arrived_rows = (
        lax.all_to_all(buffer, "vocab", split_axis=0, concat_axis=0, tiled=True),
        lax.all_to_all(row_tags, "vocab", split_axis=0, concat_axis=0, tiled=True),
    )
    flat_rows = arrived_rows.reshape(groups * capacity).astype(jnp.int32)
    selector = (
        lax.broadcasted_iota(jnp.int32, (rows, groups * capacity), 0) == flat_rows[None, :]
    ).astype(jnp.bfloat16)
    fisher = jnp.dot(
        selector, arrived.reshape(groups * capacity, width), preferred_element_type=jnp.float32
    )
    weight = (fisher + prior_weight).astype(jnp.bfloat16)
    term = (weight.astype(jnp.float32) * tables[0].astype(jnp.float32)).astype(jnp.bfloat16)
    numer, denom = (
        lax.psum_scatter(term, "ckpt", scatter_dimension=1, tiled=True).astype(jnp.float32),
        lax.psum_scatter(weight, "ckpt", scatter_dimension=1, tiled=True).astype(jnp.float32),
    )
    return (numer / denom).astype(jnp.bfloat16)


def per_device(token_ids, grad_values, grad_scales, tables):
    groups = lax.axis_size("vocab")
    ckpts = lax.axis_size("ckpt")
    count = token_ids.shape[0]
    width = tables.shape[2]
    capacity = 2 * count // groups
    if capacity % 16 == 0 and width % (ckpts * CHUNKS * BLK) == 0:
        return merge_rows(token_ids, grad_values, grad_scales, tables)
    return merge_small_slots(token_ids, grad_values, grad_scales, tables)


def solution(mesh):
    return jax.shard_map(
        per_device,
        mesh=mesh,
        in_specs=(
            P("vocab"),
            P("ckpt", "vocab", None),
            P("ckpt", None, "vocab"),
            P("ckpt", "vocab", None),
        ),
        out_specs=P("vocab", "ckpt"),
        check_vma=False,
    )
```

```python
import functools

import jax
import jax.numpy as jnp
from jax import lax
from jax.experimental import pallas as pl
from jax.experimental.pallas import tpu as pltpu
from jax.sharding import PartitionSpec as P

BLK = 128
CHUNKS = 16
LAG = 4
HALVES = (5, 6)
MESH = pl.DeviceIdType.MESH


prior_weight = 1.0


def merge_kernel(
    groups,
    ckpts,
    chunks,
    ids_ref,
    grads_ref,
    all_scales_ref,
    tables_ref,
    out_ref,
    grads,
    tables,
    scales_ref,
    match_ref,
    select_ref,
    tag_send,
    tag_recv,
    send,
    recv,
    part_send,
    part_recv,
    load_sem,
    tag_send_sem,
    tag_recv_sem,
    send_sem,
    recv_sem,
    part_send_sem,
    part_recv_sem,
):
    c = lax.axis_index("ckpt")
    v = lax.axis_index("vocab")
    rows = tables.shape[0]
    count = grads.shape[0]
    width = grads.shape[1]
    slots = match_ref.shape[0]
    capacity = slots // groups
    quarter = width // ckpts
    piece = quarter // chunks
    blocks = piece // BLK

    def vocab_peer(j):
        return (c, lax.rem(v + j, groups))

    def ckpt_peer(j):
        return (lax.rem(c + j, ckpts), v)

    barrier = pltpu.get_barrier_semaphore()
    for j in range(1, groups):
        pl.semaphore_signal(barrier, inc=1, device_id=vocab_peer(j), device_id_type=MESH)
    for j in range(1, ckpts):
        pl.semaphore_signal(barrier, inc=1, device_id=ckpt_peer(j), device_id_type=MESH)

    load_grads = pltpu.make_async_copy(grads_ref, grads, load_sem.at[0])
    load_tables = pltpu.make_async_copy(tables_ref, tables, load_sem.at[1])
    load_scales = pltpu.make_async_copy(all_scales_ref, scales_ref, load_sem.at[2])
    load_grads.start()
    load_scales.start()
    load_tables.start()

    ids_row = ids_ref[...]
    ids_col = jnp.broadcast_to(ids_row, (count, count)).T
    near_row = lax.rem(ids_row // rows - v + groups, groups)
    near_col = lax.rem(ids_col // rows - v + groups, groups)
    same = near_row == near_col
    at0 = lax.broadcasted_iota(jnp.int32, (count, count), 0)
    at1 = lax.broadcasted_iota(jnp.int32, (count, count), 1)
    rank_row = jnp.sum(jnp.where(same & (at0 < at1), 1, 0), axis=0, keepdims=True)
    rank_col = jnp.sum(jnp.where(same & (at1 < at0), 1, 0), axis=1, keepdims=True)
    slot_row = near_row * capacity + rank_row
    slot_col = near_col * capacity + rank_col
    match_ref[...] = jnp.where(
        lax.broadcasted_iota(jnp.int32, (slots, count), 0) == slot_row, 1.0, 0.0
    ).astype(jnp.bfloat16)
    tags = jnp.sum(
        jnp.where(
            lax.broadcasted_iota(jnp.int32, (count, slots), 1) == slot_col[:, 0:1],
            lax.rem(ids_col[:, 0:1], rows),
            0,
        ),
        axis=0,
        keepdims=True,
    )
    tag_send[...] = jnp.broadcast_to(tags, tag_send.shape)

    def tag_copy(j):
        return pltpu.make_async_remote_copy(
            src_ref=tag_send,
            dst_ref=tag_recv.at[j],
            send_sem=tag_send_sem.at[j],
            recv_sem=tag_recv_sem.at[j],
            device_id=vocab_peer(j),
            device_id_type=MESH,
        )

    def row_copy(k, j):
        return pltpu.make_async_remote_copy(
            src_ref=send.at[k, j],
            dst_ref=recv.at[k, j],
            send_sem=send_sem.at[k, j],
            recv_sem=recv_sem.at[k, j],
            device_id=vocab_peer(j),
            device_id_type=MESH,
        )

    def part_copy(k, j):
        return pltpu.make_async_remote_copy(
            src_ref=part_send.at[k, j],
            dst_ref=part_recv.at[k, j],
            send_sem=part_send_sem.at[k, j],
            recv_sem=part_recv_sem.at[k, j],
            device_id=ckpt_peer(j),
            device_id_type=MESH,
        )

    order = sorted(range(1, groups), key=lambda j: -min(j, groups - j))

    def place(k):
        block_scales = jnp.concatenate(
            [
                scales_ref[pl.ds(q * (quarter // BLK) + k * blocks, blocks), :]
                for q in range(ckpts)
            ],
            axis=0,
        ).T
        squares = []
        for q in range(ckpts):
            for b in range(blocks):
                at = pl.multiple_of(q * quarter + k * piece + b * BLK, BLK)
                i = q * blocks + b
                g = grads[:, pl.ds(at, BLK)].astype(jnp.float32) * block_scales[:, i : i + 1]
                squares.append((g * g).astype(jnp.bfloat16))
        placed = jnp.dot(
            match_ref[...],
            jnp.concatenate(squares, axis=1),
            preferred_element_type=jnp.float32,
        ).astype(jnp.bfloat16)
        placed = placed.reshape(groups, capacity, ckpts * piece)
        recv[k, 0] = placed[0]
        for j in range(1, groups):
            send[k, j] = placed[j]

    def start_rows(k):
        for j in order:
            row_copy(k, j).start()

    load_grads.wait()
    load_scales.wait()
    place(0)
    pl.semaphore_wait(barrier, groups + ckpts - 2)
    for j in order:
        tag_copy(j).start()
    start_rows(0)

    def place_next(k, carry):
        place(k)
        start_rows(k)
        return carry

    lax.fori_loop(1, chunks, place_next, 0)

    lane = lax.broadcasted_iota(jnp.int32, (1, slots), 1) // capacity
    arrived_tags = jnp.where(lane == 0, tags, 0)
    for j in range(1, groups):
        tag_copy(j).wait()
        arrived_tags = jnp.where(lane == j, tag_recv[j, 0:1, :], arrived_tags)
    select_ref[...] = jnp.where(
        lax.broadcasted_iota(jnp.int32, (rows, slots), 0) == arrived_tags, 1.0, 0.0
    ).astype(jnp.bfloat16)
    load_tables.wait()

    def weigh_chunk(k):
        for j in range(1, groups):
            row_copy(k, j).wait_recv()
        fisher = jnp.dot(
            select_ref[...],
            recv[k].reshape(slots, ckpts * piece),
            preferred_element_type=jnp.float32,
        )
        weight = (fisher + prior_weight).astype(jnp.bfloat16)
        for q in range(ckpts):
            own = weight[:, q * piece : (q + 1) * piece]
            at = pl.multiple_of(q * quarter + k * piece, BLK)
            table = tables[:, pl.ds(at, piece)].astype(jnp.float32)
            j = lax.rem(q - c + ckpts, ckpts)
            part_send[k, j, 0] = (own.astype(jnp.float32) * table).astype(jnp.bfloat16)
            part_send[k, j, 1] = own
        for j in range(1, ckpts):
            part_copy(k, j).start()

    def finish_chunk(k):
        numer = part_send[k, 0, 0].astype(jnp.float32)
        denom = part_send[k, 0, 1].astype(jnp.float32)
        for j in range(1, ckpts):
            part_copy(k, j).wait_recv()
            numer += part_recv[k, j, 0].astype(jnp.float32)
            denom += part_recv[k, j, 1].astype(jnp.float32)
        at = pl.multiple_of(k * piece, BLK)
        out_ref[:, pl.ds(at, piece)] = (numer / denom).astype(jnp.bfloat16)

    weigh_chunk(0)

    def step(k, carry):
        weigh_chunk(k)
        finish_chunk(k - 1)
        return carry

    lax.fori_loop(1, chunks, step, 0)
    finish_chunk(chunks - 1)

    def drain(k, carry):
        for j in range(1, groups):
            row_copy(k, j).wait_send()
        for j in range(1, ckpts):
            part_copy(k, j).wait_send()
        return carry

    lax.fori_loop(0, chunks, drain, 0)


def merge_rows(token_ids, grad_values, grad_scales, tables):
    groups = lax.axis_size("vocab")
    ckpts = lax.axis_size("ckpt")
    rows, width = tables.shape[1:]
    count = token_ids.shape[0]
    slots = 2 * count
    capacity = slots // groups
    chunk_width = width // CHUNKS
    vmem = pl.BlockSpec(memory_space=pltpu.VMEM)
    hbm = pl.BlockSpec(memory_space=pl.ANY)
    bf16 = jnp.bfloat16
    dma = pltpu.SemaphoreType.DMA
    return pl.pallas_call(
        functools.partial(merge_kernel, groups, ckpts, CHUNKS),
        out_shape=jax.ShapeDtypeStruct((rows, width // ckpts), bf16),
        in_specs=[vmem, hbm, hbm, hbm],
        out_specs=vmem,
        scratch_shapes=[
            pltpu.VMEM((count, width), bf16),
            pltpu.VMEM((rows, width), bf16),
            pltpu.VMEM((width // BLK, count), jnp.float32),
            pltpu.VMEM((slots, count), bf16),
            pltpu.VMEM((rows, slots), bf16),
            pltpu.VMEM((8, slots), jnp.int32),
            pltpu.VMEM((groups, 8, slots), jnp.int32),
            pltpu.VMEM((CHUNKS, groups, capacity, chunk_width), bf16),
            pltpu.VMEM((CHUNKS, groups, capacity, chunk_width), bf16),
            pltpu.VMEM((CHUNKS, ckpts, 2, rows, chunk_width // ckpts), bf16),
            pltpu.VMEM((CHUNKS, ckpts, 2, rows, chunk_width // ckpts), bf16),
            dma((3,)),
            dma((groups,)),
            dma((groups,)),
            dma((CHUNKS, groups)),
            dma((CHUNKS, groups)),
            dma((CHUNKS, ckpts)),
            dma((CHUNKS, ckpts)),
        ],
        compiler_params=pltpu.CompilerParams(
            collective_id=7, has_side_effects=True, vmem_limit_bytes=60 * 1024 * 1024
        ),
        cost_estimate=pl.CostEstimate(
            flops=4 * slots * count * width,
            bytes_accessed=5 * rows * width,
            transcendentals=0,
        ),
    )(
        token_ids.reshape(1, count),
        grad_values[0],
        grad_scales[0],
        tables[0],
    )


def sort_positions(ids_row, rows):
    count = ids_row.shape[1]
    ids_col = jnp.broadcast_to(ids_row, (count, count)).T
    own_row = ids_row // rows
    own_col = ids_col // rows
    at0 = lax.broadcasted_iota(jnp.int32, (count, count), 0)
    at1 = lax.broadcasted_iota(jnp.int32, (count, count), 1)
    same = own_row == own_col
    first0 = (own_col < own_row) | (same & (at0 < at1))
    first1 = (own_row < own_col) | (same & (at1 < at0))
    pos_row = jnp.sum(jnp.where(first0, 1, 0), axis=0, keepdims=True)
    pos_col = jnp.sum(jnp.where(first1, 1, 0), axis=1, keepdims=True)
    return pos_row, pos_col, ids_col[:, 0:1]


def gather_kernel(groups, rows, capacity, ids_ref, ids_out, load_out, mine, theirs, send_sem, recv_sem):
    c = lax.axis_index("ckpt")
    v = lax.axis_index("vocab")
    count = ids_ref.shape[1]

    def peer(j):
        return (c, lax.rem(v + j, groups))

    barrier = pltpu.get_barrier_semaphore()
    for j in range(1, groups):
        pl.semaphore_signal(barrier, inc=1, device_id=peer(j), device_id_type=MESH)
    _, pos_col, ids_col = sort_positions(ids_ref[...], rows)
    at1 = lax.broadcasted_iota(jnp.int32, (count, count), 1)
    ordered = jnp.sum(jnp.where(at1 == pos_col, ids_col, 0), axis=0, keepdims=True)
    mine[...] = jnp.broadcast_to(ordered, mine.shape)
    theirs[v] = mine[...]

    def copy(j):
        return pltpu.make_async_remote_copy(
            src_ref=mine,
            dst_ref=theirs.at[v],
            send_sem=send_sem.at[j],
            recv_sem=recv_sem.at[j],
            device_id=peer(j),
            device_id_type=MESH,
        )

    pl.semaphore_wait(barrier, groups - 1)
    for j in range(1, groups):
        copy(j).start()
    for j in range(1, groups):
        copy(j).wait()
    ids_all = jnp.concatenate([theirs[d, 0:1, :] for d in range(groups)], axis=0)
    ids_out[...] = ids_all
    layer = lax.broadcasted_iota(jnp.int32, (groups, count), 0) // 2
    owner_layer = ids_all // (2 * rows)
    most = jnp.zeros((1, 1), jnp.int32)
    for cut in range(groups // 2 - 1):
        up = jnp.where((layer <= cut) & (owner_layer > cut), 1, 0)
        down = jnp.where((layer > cut) & (owner_layer <= cut), 1, 0)
        for flow in (up, down):
            total = jnp.sum(jnp.sum(flow, axis=1, keepdims=True), axis=0, keepdims=True)
            most = jnp.maximum(most, total)
    load_out[...] = jnp.broadcast_to(most, load_out.shape)


def chain_kernel(
    groups,
    ckpts,
    chunks,
    half,
    capacity,
    ids_ref,
    ids_all_ref,
    grads_ref,
    all_scales_ref,
    tables_ref,
    out_ref,
    grads,
    tables,
    scales_ref,
    match_ref,
    up_pool_sel,
    up_in_sel,
    down_pool_sel,
    down_in_sel,
    rows_pool_sel,
    rows_up_sel,
    rows_down_sel,
    pool,
    up_in,
    down_in,
    up_out,
    down_out,
    part_send,
    part_recv,
    load_sem,
    pool_sems,
    up_sems,
    up_mate_sems,
    down_sems,
    down_mate_sems,
    part_send_sem,
    part_recv_sem,
):
    c = lax.axis_index("ckpt")
    v = lax.axis_index("vocab")
    layers = groups // 2
    z = v // 2
    core = v % 2
    mate = v + 1 - 2 * core
    rows = tables.shape[0]
    count = grads.shape[0]
    width = grads.shape[1]
    quarter = width // ckpts
    piece = quarter // chunks
    blocks = piece // BLK
    span = half * capacity
    bf16 = jnp.bfloat16
    has_up = z < layers - 1
    has_down = z > 0

    def ckpt_peer(j):
        return (lax.rem(c + j, ckpts), v)

    def greet(device):
        pl.semaphore_signal(barrier, inc=1, device_id=device, device_id_type=MESH)

    barrier = pltpu.get_barrier_semaphore()
    greet((c, mate))
    for j in range(1, ckpts):
        greet(ckpt_peer(j))

    @pl.when(has_up)
    def _():
        greet((c, v + 2))

    @pl.when(has_down)
    def _():
        greet((c, v - 2))

    load_grads = pltpu.make_async_copy(grads_ref, grads, load_sem.at[0])
    load_tables = pltpu.make_async_copy(tables_ref, tables, load_sem.at[1])
    load_scales = pltpu.make_async_copy(all_scales_ref, scales_ref, load_sem.at[2])
    load_grads.start()
    load_scales.start()
    load_tables.start()

    pos_row, _, _ = sort_positions(ids_ref[...], rows)
    at0 = lax.broadcasted_iota(jnp.int32, (count, count), 0)
    at1 = lax.broadcasted_iota(jnp.int32, (count, count), 1)
    match_ref[...] = jnp.where(at0 == pos_row, 1.0, 0.0).astype(bf16)

    ids_all = ids_all_ref[...]
    layer = lax.broadcasted_iota(jnp.int32, (groups, count), 0) // 2
    owner_layer = ids_all // (2 * rows)
    before = jnp.where(at0 < at1, 1.0, 0.0).astype(bf16)

    def places(mask):
        flags = jnp.where(mask, 1.0, 0.0)
        inner = jnp.dot(flags.astype(bf16), before, preferred_element_type=jnp.float32)
        totals = jnp.sum(flags, axis=1, keepdims=True)
        offset = jnp.zeros((1, 1), jnp.float32)
        offsets = []
        for d in range(groups):
            offsets.append(offset)
            offset = offset + totals[d : d + 1]
        place = (inner + jnp.concatenate(offsets, axis=0)).astype(jnp.int32)
        return jnp.where(mask, place, -1)

    up_from = places((layer <= z - 1) & (owner_layer > z - 1))
    up_to = places((layer <= z) & (owner_layer > z))
    down_from = places((layer >= z + 1) & (owner_layer < z + 1))
    down_to = places((layer >= z) & (owner_layer < z))

    def one_hot(size, values):
        shape = (size, count)
        return jnp.where(
            lax.broadcasted_iota(jnp.int32, shape, 0) == values, 1.0, 0.0
        ).astype(bf16)

    def meet(a, b):
        return lax.dot_general(
            a, b, (((1,), (1,)), ((), ())), preferred_element_type=jnp.float32
        )

    up_sum = down_sum = rows_up = rows_down = 0.0
    pools = [[0.0, 0.0] for _ in range(3)]
    for d in range(groups):
        take_up = one_hot(span, up_to[d : d + 1] - core * span)
        take_down = one_hot(span, down_to[d : d + 1] - core * span)
        take_rows = one_hot(rows, ids_all[d : d + 1] - v * rows)
        at_up = one_hot(2 * span, up_from[d : d + 1])
        at_down = one_hot(2 * span, down_from[d : d + 1])
        up_sum += meet(take_up, at_up)
        down_sum += meet(take_down, at_down)
        rows_up += meet(take_rows, at_up)
        rows_down += meet(take_rows, at_down)
        here = jnp.where(z == d // 2, 1.0, 0.0).astype(bf16)
        for i, take in enumerate((take_up, take_down, take_rows)):
            pools[i][d % 2] += take * here
    up_in_sel[...] = up_sum.astype(bf16)
    down_in_sel[...] = down_sum.astype(bf16)
    rows_up_sel[...] = rows_up.astype(bf16)
    rows_down_sel[...] = rows_down.astype(bf16)
    for ref, pair in zip((up_pool_sel, down_pool_sel, rows_pool_sel), pools):
        ref[...] = jnp.concatenate(pair, axis=1).astype(bf16)

    @pl.when(z == 0)
    def _():
        def clear(k, carry):
            up_in[k] = jnp.zeros(up_in.shape[1:], bf16)
            return carry

        lax.fori_loop(0, chunks, clear, 0)

    @pl.when(z == layers - 1)
    def _():
        def clear(k, carry):
            down_in[k] = jnp.zeros(down_in.shape[1:], bf16)
            return carry

        lax.fori_loop(0, chunks, clear, 0)

    def remote(src, dst, sems, k, device):
        return pltpu.make_async_remote_copy(
            src_ref=src,
            dst_ref=dst,
            send_sem=sems.at[0, k],
            recv_sem=sems.at[1, k],
            device_id=device,
            device_id_type=MESH,
        )

    def pool_copy(k):
        return remote(pool.at[k, core], pool.at[k, core], pool_sems, k, (c, mate))

    def up_copy(k):
        return remote(up_out.at[k], up_in.at[k, core], up_sems, k, (c, lax.rem(v + 2, groups)))

    def down_copy(k):
        device = (c, lax.rem(v + groups - 2, groups))
        return remote(down_out.at[k], down_in.at[k, core], down_sems, k, device)

    def up_mate(k):
        return remote(up_in.at[k, core], up_in.at[k, core], up_mate_sems, k, (c, mate))

    def down_mate(k):
        return remote(down_in.at[k, core], down_in.at[k, core], down_mate_sems, k, (c, mate))

    def part_copy(k, j):
        return pltpu.make_async_remote_copy(
            src_ref=part_send.at[k, j],
            dst_ref=part_recv.at[k, j],
            send_sem=part_send_sem.at[k, j],
            recv_sem=part_recv_sem.at[k, j],
            device_id=ckpt_peer(j),
            device_id_type=MESH,
        )

    def place(k):
        block_scales = jnp.concatenate(
            [
                scales_ref[pl.ds(q * (quarter // BLK) + k * blocks, blocks), :]
                for q in range(ckpts)
            ],
            axis=0,
        ).T
        squares = []
        for q in range(ckpts):
            for b in range(blocks):
                at = pl.multiple_of(q * quarter + k * piece + b * BLK, BLK)
                i = q * blocks + b
                g = grads[:, pl.ds(at, BLK)].astype(jnp.float32) * block_scales[:, i : i + 1]
                squares.append((g * g).astype(bf16))
        pool[k, core] = jnp.dot(
            match_ref[...],
            jnp.concatenate(squares, axis=1),
            preferred_element_type=jnp.float32,
        ).astype(bf16)

    def pooled(k):
        return pool[k].reshape(2 * count, ckpts * piece)

    def arrived(ref, k):
        return ref[k].reshape(2 * span, ckpts * piece)

    def dot(a, b):
        return jnp.dot(a, b, preferred_element_type=jnp.float32)

    def weigh_chunk(k):
        fisher = (
            dot(rows_pool_sel[...], pooled(k))
            + dot(rows_up_sel[...], arrived(up_in, k))
            + dot(rows_down_sel[...], arrived(down_in, k))
        )
        weight = (fisher + prior_weight).astype(bf16)
        for q in range(ckpts):
            own = weight[:, q * piece : (q + 1) * piece]
            at = pl.multiple_of(q * quarter + k * piece, BLK)
            table = tables[:, pl.ds(at, piece)].astype(jnp.float32)
            j = lax.rem(q - c + ckpts, ckpts)
            part_send[k, j, 0] = (own.astype(jnp.float32) * table).astype(bf16)
            part_send[k, j, 1] = own
        for j in range(1, ckpts):
            part_copy(k, j).start()

    def finish_chunk(k):
        numer = part_send[k, 0, 0].astype(jnp.float32)
        denom = part_send[k, 0, 1].astype(jnp.float32)
        for j in range(1, ckpts):
            part_copy(k, j).wait_recv()
            numer += part_recv[k, j, 0].astype(jnp.float32)
            denom += part_recv[k, j, 1].astype(jnp.float32)
        at = pl.multiple_of(k * piece, BLK)
        out_ref[:, pl.ds(at, piece)] = (numer / denom).astype(bf16)

    load_grads.wait()
    load_scales.wait()
    load_tables.wait()
    greetings = ckpts + jnp.where(has_up, 1, 0) + jnp.where(has_down, 1, 0)
    pl.semaphore_wait(barrier, greetings)

    def inside(k):
        return (k >= 0) & (k < chunks)

    def step(s, carry):
        up = s - LAG * z
        down = s - LAG * (layers - 1 - z)

        @pl.when(s < chunks)
        def _():
            place(s)
            pool_copy(s).start()

        @pl.when(inside(up) & has_down)
        def _():
            up_copy(up).wait_recv()
            up_mate(up).start()

        @pl.when(inside(down) & has_up)
        def _():
            down_copy(down).wait_recv()
            down_mate(down).start()

        @pl.when(inside(s - 1))
        def _():
            pool_copy(s - 1).wait_recv()

        @pl.when(inside(up - 1) & has_down)
        def _():
            up_mate(up - 1).wait_recv()

        @pl.when(inside(up - 1) & has_up)
        def _():
            k = up - 1
            up_out[k] = (
                dot(up_pool_sel[...], pooled(k)) + dot(up_in_sel[...], arrived(up_in, k))
            ).astype(bf16)
            up_copy(k).start()

        @pl.when(inside(down - 1) & has_up)
        def _():
            down_mate(down - 1).wait_recv()

        @pl.when(inside(down - 1) & has_down)
        def _():
            k = down - 1
            down_out[k] = (
                dot(down_pool_sel[...], pooled(k)) + dot(down_in_sel[...], arrived(down_in, k))
            ).astype(bf16)
            down_copy(k).start()

        ready = jnp.minimum(up, down) - 1

        @pl.when(inside(ready))
        def _():
            weigh_chunk(ready)

        @pl.when(inside(ready - 1))
        def _():
            finish_chunk(ready - 1)

        return carry

    lax.fori_loop(0, chunks + 2 + LAG * (layers - 1), step, 0)

    def drain(k, carry):
        pool_copy(k).wait_send()

        @pl.when(has_up)
        def _():
            up_copy(k).wait_send()
            down_mate(k).wait_send()

        @pl.when(has_down)
        def _():
            down_copy(k).wait_send()
            up_mate(k).wait_send()

        for j in range(1, ckpts):
            part_copy(k, j).wait_send()
        return carry

    lax.fori_loop(0, chunks, drain, 0)


def merge_chain(half, collective, token_ids, ids_all, grad_values, grad_scales, tables):
    groups = lax.axis_size("vocab")
    ckpts = lax.axis_size("ckpt")
    rows, width = tables.shape[1:]
    count = token_ids.shape[0]
    capacity = 2 * count // groups
    chunk_width = width // CHUNKS
    span = half * capacity
    vmem = pl.BlockSpec(memory_space=pltpu.VMEM)
    hbm = pl.BlockSpec(memory_space=pl.ANY)
    bf16 = jnp.bfloat16
    dma = pltpu.SemaphoreType.DMA
    return pl.pallas_call(
        functools.partial(chain_kernel, groups, ckpts, CHUNKS, half, capacity),
        out_shape=jax.ShapeDtypeStruct((rows, width // ckpts), bf16),
        in_specs=[vmem, vmem, hbm, hbm, hbm],
        out_specs=vmem,
        scratch_shapes=[
            pltpu.VMEM((count, width), bf16),
            pltpu.VMEM((rows, width), bf16),
            pltpu.VMEM((width // BLK, count), jnp.float32),
            pltpu.VMEM((count, count), bf16),
            pltpu.VMEM((span, 2 * count), bf16),
            pltpu.VMEM((span, 2 * span), bf16),
            pltpu.VMEM((span, 2 * count), bf16),
            pltpu.VMEM((span, 2 * span), bf16),
            pltpu.VMEM((rows, 2 * count), bf16),
            pltpu.VMEM((rows, 2 * span), bf16),
            pltpu.VMEM((rows, 2 * span), bf16),
            pltpu.VMEM((CHUNKS, 2, count, chunk_width), bf16),
            pltpu.VMEM((CHUNKS, 2, span, chunk_width), bf16),
            pltpu.VMEM((CHUNKS, 2, span, chunk_width), bf16),
            pltpu.VMEM((CHUNKS, span, chunk_width), bf16),
            pltpu.VMEM((CHUNKS, span, chunk_width), bf16),
            pltpu.VMEM((CHUNKS, ckpts, 2, rows, chunk_width // ckpts), bf16),
            pltpu.VMEM((CHUNKS, ckpts, 2, rows, chunk_width // ckpts), bf16),
            dma((3,)),
            dma((2, CHUNKS)),
            dma((2, CHUNKS)),
            dma((2, CHUNKS)),
            dma((2, CHUNKS)),
            dma((2, CHUNKS)),
            dma((CHUNKS, ckpts)),
            dma((CHUNKS, ckpts)),
        ],
        compiler_params=pltpu.CompilerParams(
            collective_id=collective, has_side_effects=True, vmem_limit_bytes=60 * 1024 * 1024
        ),
    )(token_ids.reshape(1, count), ids_all, grad_values[0], grad_scales[0], tables[0])


def merge_by_load(token_ids, grad_values, grad_scales, tables):
    groups = lax.axis_size("vocab")
    rows = tables.shape[1]
    count = token_ids.shape[0]
    capacity = 2 * count // groups
    vmem = pl.BlockSpec(memory_space=pltpu.VMEM)
    dma = pltpu.SemaphoreType.DMA
    ids_all, load = pl.pallas_call(
        functools.partial(gather_kernel, groups, rows, capacity),
        out_shape=[
            jax.ShapeDtypeStruct((groups, count), jnp.int32),
            jax.ShapeDtypeStruct((8, 128), jnp.int32),
        ],
        in_specs=[vmem],
        out_specs=[vmem, vmem],
        scratch_shapes=[
            pltpu.VMEM((8, count), jnp.int32),
            pltpu.VMEM((groups, 8, count), jnp.int32),
            dma((groups,)),
            dma((groups,)),
        ],
        compiler_params=pltpu.CompilerParams(collective_id=0, has_side_effects=True),
    )(token_ids.reshape(1, count))
    load = load[0, 0]
    args = (token_ids, ids_all, grad_values, grad_scales, tables)
    branches = [functools.partial(merge_chain, half, i + 1) for i, half in enumerate(HALVES)]
    branches.append(lambda ids, _, values, scales, rows: merge_rows(ids, values, scales, rows))
    index = sum((load > 2 * half * capacity).astype(jnp.int32) for half in HALVES)
    return lax.switch(index, branches, *args)


def merge_small_slots(token_ids, grad_values, grad_scales, tables):
    groups = lax.axis_size("vocab")
    rows = tables.shape[1]
    width = tables.shape[2]
    count = token_ids.shape[0]
    capacity = 2 * count // groups
    owner = token_ids // rows
    same = owner[:, None] == owner[None, :]
    before = lax.broadcasted_iota(jnp.int32, (count, count), 0) < lax.broadcasted_iota(
        jnp.int32, (count, count), 1
    )
    rank = jnp.sum((same & before).astype(jnp.int32), axis=0)
    slot = owner * capacity + rank
    match = lax.broadcasted_iota(jnp.int32, (groups * capacity, count), 0) == slot[None, :]
    scales = grad_scales[0].T
    grads = (
        grad_values[0].astype(jnp.float32).reshape(count, width // BLK, BLK) * scales[:, :, None]
    )
    squares = (grads * grads).reshape(count, width).astype(jnp.bfloat16)
    placed = jnp.dot(match.astype(jnp.bfloat16), squares, preferred_element_type=jnp.float32)
    buffer = placed.astype(jnp.bfloat16).reshape(groups, capacity, width)
    local_rows = token_ids % rows
    row_tags = (
        jnp.sum(jnp.where(match, local_rows[None, :], 0), axis=1)
        .astype(jnp.bfloat16)
        .reshape(groups, capacity)
    )
    arrived, arrived_rows = (
        lax.all_to_all(buffer, "vocab", split_axis=0, concat_axis=0, tiled=True),
        lax.all_to_all(row_tags, "vocab", split_axis=0, concat_axis=0, tiled=True),
    )
    flat_rows = arrived_rows.reshape(groups * capacity).astype(jnp.int32)
    selector = (
        lax.broadcasted_iota(jnp.int32, (rows, groups * capacity), 0) == flat_rows[None, :]
    ).astype(jnp.bfloat16)
    fisher = jnp.dot(
        selector, arrived.reshape(groups * capacity, width), preferred_element_type=jnp.float32
    )
    weight = (fisher + prior_weight).astype(jnp.bfloat16)
    term = (weight.astype(jnp.float32) * tables[0].astype(jnp.float32)).astype(jnp.bfloat16)
    numer, denom = (
        lax.psum_scatter(term, "ckpt", scatter_dimension=1, tiled=True).astype(jnp.float32),
        lax.psum_scatter(weight, "ckpt", scatter_dimension=1, tiled=True).astype(jnp.float32),
    )
    return (numer / denom).astype(jnp.bfloat16)


def per_device(token_ids, grad_values, grad_scales, tables):
    groups = lax.axis_size("vocab")
    ckpts = lax.axis_size("ckpt")
    count = token_ids.shape[0]
    width = tables.shape[2]
    capacity = 2 * count // groups
    if capacity % 16 == 0 and width % (ckpts * CHUNKS * BLK) == 0:
        if groups == 8:
            return merge_by_load(token_ids, grad_values, grad_scales, tables)
        return merge_rows(token_ids, grad_values, grad_scales, tables)
    return merge_small_slots(token_ids, grad_values, grad_scales, tables)


def solution(mesh):
    return jax.shard_map(
        per_device,
        mesh=mesh,
        in_specs=(
            P("vocab"),
            P("ckpt", "vocab", None),
            P("ckpt", None, "vocab"),
            P("ckpt", "vocab", None),
        ),
        out_specs=P("vocab", "ckpt"),
        check_vma=False,
    )
```

```python
import functools

import jax
import jax.numpy as jnp
from jax import lax
from jax.experimental import pallas as pl
from jax.experimental.pallas import tpu as pltpu
from jax.sharding import PartitionSpec as P

BLK = 128
CHUNKS = 16
LAG = 4
SETTLE = 3
HALVES = (5, 6)
MESH = pl.DeviceIdType.MESH


prior_weight = 1.0


def merge_kernel(
    groups,
    ckpts,
    chunks,
    ids_ref,
    grads_ref,
    all_scales_ref,
    tables_ref,
    out_ref,
    grads,
    tables,
    scales_ref,
    match_ref,
    select_ref,
    tag_send,
    tag_recv,
    send,
    recv,
    part_send,
    part_recv,
    load_sem,
    tag_send_sem,
    tag_recv_sem,
    send_sem,
    recv_sem,
    part_send_sem,
    part_recv_sem,
):
    c = lax.axis_index("ckpt")
    v = lax.axis_index("vocab")
    rows = tables.shape[0]
    count = grads.shape[0]
    width = grads.shape[1]
    slots = match_ref.shape[0]
    capacity = slots // groups
    quarter = width // ckpts
    piece = quarter // chunks
    blocks = piece // BLK

    def vocab_peer(j):
        return (c, lax.rem(v + j, groups))

    def ckpt_peer(j):
        return (lax.rem(c + j, ckpts), v)

    barrier = pltpu.get_barrier_semaphore()
    for j in range(1, groups):
        pl.semaphore_signal(barrier, inc=1, device_id=vocab_peer(j), device_id_type=MESH)
    for j in range(1, ckpts):
        pl.semaphore_signal(barrier, inc=1, device_id=ckpt_peer(j), device_id_type=MESH)

    load_grads = pltpu.make_async_copy(grads_ref, grads, load_sem.at[0])
    load_tables = pltpu.make_async_copy(tables_ref, tables, load_sem.at[1])
    load_scales = pltpu.make_async_copy(all_scales_ref, scales_ref, load_sem.at[2])
    load_grads.start()
    load_scales.start()
    load_tables.start()

    ids_row = ids_ref[...]
    ids_col = jnp.broadcast_to(ids_row, (count, count)).T
    near_row = lax.rem(ids_row // rows - v + groups, groups)
    near_col = lax.rem(ids_col // rows - v + groups, groups)
    same = near_row == near_col
    at0 = lax.broadcasted_iota(jnp.int32, (count, count), 0)
    at1 = lax.broadcasted_iota(jnp.int32, (count, count), 1)
    rank_row = jnp.sum(jnp.where(same & (at0 < at1), 1, 0), axis=0, keepdims=True)
    rank_col = jnp.sum(jnp.where(same & (at1 < at0), 1, 0), axis=1, keepdims=True)
    slot_row = near_row * capacity + rank_row
    slot_col = near_col * capacity + rank_col
    match_ref[...] = jnp.where(
        lax.broadcasted_iota(jnp.int32, (slots, count), 0) == slot_row, 1.0, 0.0
    ).astype(jnp.bfloat16)
    tags = jnp.sum(
        jnp.where(
            lax.broadcasted_iota(jnp.int32, (count, slots), 1) == slot_col[:, 0:1],
            lax.rem(ids_col[:, 0:1], rows),
            0,
        ),
        axis=0,
        keepdims=True,
    )
    tag_send[...] = jnp.broadcast_to(tags, tag_send.shape)

    def tag_copy(j):
        return pltpu.make_async_remote_copy(
            src_ref=tag_send,
            dst_ref=tag_recv.at[j],
            send_sem=tag_send_sem.at[j],
            recv_sem=tag_recv_sem.at[j],
            device_id=vocab_peer(j),
            device_id_type=MESH,
        )

    def row_copy(k, j):
        return pltpu.make_async_remote_copy(
            src_ref=send.at[k, j],
            dst_ref=recv.at[k, j],
            send_sem=send_sem.at[k, j],
            recv_sem=recv_sem.at[k, j],
            device_id=vocab_peer(j),
            device_id_type=MESH,
        )

    def part_copy(k, j):
        return pltpu.make_async_remote_copy(
            src_ref=part_send.at[k, j],
            dst_ref=part_recv.at[k, j],
            send_sem=part_send_sem.at[k, j],
            recv_sem=part_recv_sem.at[k, j],
            device_id=ckpt_peer(j),
            device_id_type=MESH,
        )

    order = sorted(range(1, groups), key=lambda j: -min(j, groups - j))

    def place(k):
        block_scales = jnp.concatenate(
            [
                scales_ref[pl.ds(q * (quarter // BLK) + k * blocks, blocks), :]
                for q in range(ckpts)
            ],
            axis=0,
        ).T
        squares = []
        for q in range(ckpts):
            for b in range(blocks):
                at = pl.multiple_of(q * quarter + k * piece + b * BLK, BLK)
                i = q * blocks + b
                g = grads[:, pl.ds(at, BLK)].astype(jnp.float32) * block_scales[:, i : i + 1]
                squares.append((g * g).astype(jnp.bfloat16))
        placed = jnp.dot(
            match_ref[...],
            jnp.concatenate(squares, axis=1),
            preferred_element_type=jnp.float32,
        ).astype(jnp.bfloat16)
        placed = placed.reshape(groups, capacity, ckpts * piece)
        recv[k, 0] = placed[0]
        for j in range(1, groups):
            send[k, j] = placed[j]

    def start_rows(k):
        for j in order:
            row_copy(k, j).start()

    load_grads.wait()
    load_scales.wait()
    place(0)
    pl.semaphore_wait(barrier, groups + ckpts - 2)
    for j in order:
        tag_copy(j).start()
    start_rows(0)

    def place_next(k, carry):
        place(k)
        start_rows(k)
        return carry

    lax.fori_loop(1, chunks, place_next, 0)

    lane = lax.broadcasted_iota(jnp.int32, (1, slots), 1) // capacity
    arrived_tags = jnp.where(lane == 0, tags, 0)
    for j in range(1, groups):
        tag_copy(j).wait()
        arrived_tags = jnp.where(lane == j, tag_recv[j, 0:1, :], arrived_tags)
    select_ref[...] = jnp.where(
        lax.broadcasted_iota(jnp.int32, (rows, slots), 0) == arrived_tags, 1.0, 0.0
    ).astype(jnp.bfloat16)
    load_tables.wait()

    def weigh_chunk(k):
        for j in range(1, groups):
            row_copy(k, j).wait_recv()
        fisher = jnp.dot(
            select_ref[...],
            recv[k].reshape(slots, ckpts * piece),
            preferred_element_type=jnp.float32,
        )
        weight = (fisher + prior_weight).astype(jnp.bfloat16)
        for q in range(ckpts):
            own = weight[:, q * piece : (q + 1) * piece]
            at = pl.multiple_of(q * quarter + k * piece, BLK)
            table = tables[:, pl.ds(at, piece)].astype(jnp.float32)
            j = lax.rem(q - c + ckpts, ckpts)
            part_send[k, j, 0] = (own.astype(jnp.float32) * table).astype(jnp.bfloat16)
            part_send[k, j, 1] = own
        for j in range(1, ckpts):
            part_copy(k, j).start()

    def finish_chunk(k):
        numer = part_send[k, 0, 0].astype(jnp.float32)
        denom = part_send[k, 0, 1].astype(jnp.float32)
        for j in range(1, ckpts):
            part_copy(k, j).wait_recv()
            numer += part_recv[k, j, 0].astype(jnp.float32)
            denom += part_recv[k, j, 1].astype(jnp.float32)
        at = pl.multiple_of(k * piece, BLK)
        out_ref[:, pl.ds(at, piece)] = (numer / denom).astype(jnp.bfloat16)

    weigh_chunk(0)

    def step(k, carry):
        weigh_chunk(k)
        finish_chunk(k - 1)
        return carry

    lax.fori_loop(1, chunks, step, 0)
    finish_chunk(chunks - 1)

    def drain(k, carry):
        for j in range(1, groups):
            row_copy(k, j).wait_send()
        for j in range(1, ckpts):
            part_copy(k, j).wait_send()
        return carry

    lax.fori_loop(0, chunks, drain, 0)


def merge_rows(token_ids, grad_values, grad_scales, tables):
    groups = lax.axis_size("vocab")
    ckpts = lax.axis_size("ckpt")
    rows, width = tables.shape[1:]
    count = token_ids.shape[0]
    slots = 2 * count
    capacity = slots // groups
    chunk_width = width // CHUNKS
    vmem = pl.BlockSpec(memory_space=pltpu.VMEM)
    hbm = pl.BlockSpec(memory_space=pl.ANY)
    bf16 = jnp.bfloat16
    dma = pltpu.SemaphoreType.DMA
    return pl.pallas_call(
        functools.partial(merge_kernel, groups, ckpts, CHUNKS),
        out_shape=jax.ShapeDtypeStruct((rows, width // ckpts), bf16),
        in_specs=[vmem, hbm, hbm, hbm],
        out_specs=vmem,
        scratch_shapes=[
            pltpu.VMEM((count, width), bf16),
            pltpu.VMEM((rows, width), bf16),
            pltpu.VMEM((width // BLK, count), jnp.float32),
            pltpu.VMEM((slots, count), bf16),
            pltpu.VMEM((rows, slots), bf16),
            pltpu.VMEM((8, slots), jnp.int32),
            pltpu.VMEM((groups, 8, slots), jnp.int32),
            pltpu.VMEM((CHUNKS, groups, capacity, chunk_width), bf16),
            pltpu.VMEM((CHUNKS, groups, capacity, chunk_width), bf16),
            pltpu.VMEM((CHUNKS, ckpts, 2, rows, chunk_width // ckpts), bf16),
            pltpu.VMEM((CHUNKS, ckpts, 2, rows, chunk_width // ckpts), bf16),
            dma((3,)),
            dma((groups,)),
            dma((groups,)),
            dma((CHUNKS, groups)),
            dma((CHUNKS, groups)),
            dma((CHUNKS, ckpts)),
            dma((CHUNKS, ckpts)),
        ],
        compiler_params=pltpu.CompilerParams(
            collective_id=7, has_side_effects=True, vmem_limit_bytes=60 * 1024 * 1024
        ),
        cost_estimate=pl.CostEstimate(
            flops=4 * slots * count * width,
            bytes_accessed=5 * rows * width,
            transcendentals=0,
        ),
    )(
        token_ids.reshape(1, count),
        grad_values[0],
        grad_scales[0],
        tables[0],
    )


def sort_positions(ids_row, rows):
    count = ids_row.shape[1]
    ids_col = jnp.broadcast_to(ids_row, (count, count)).T
    own_row = ids_row // rows
    own_col = ids_col // rows
    at0 = lax.broadcasted_iota(jnp.int32, (count, count), 0)
    at1 = lax.broadcasted_iota(jnp.int32, (count, count), 1)
    same = own_row == own_col
    first0 = (own_col < own_row) | (same & (at0 < at1))
    first1 = (own_row < own_col) | (same & (at1 < at0))
    pos_row = jnp.sum(jnp.where(first0, 1, 0), axis=0, keepdims=True)
    pos_col = jnp.sum(jnp.where(first1, 1, 0), axis=1, keepdims=True)
    return pos_row, pos_col, ids_col[:, 0:1]


def gather_kernel(groups, rows, capacity, ids_ref, ids_out, branch_out, mine, theirs, send_sem, recv_sem):
    c = lax.axis_index("ckpt")
    v = lax.axis_index("vocab")
    count = ids_ref.shape[1]

    def peer(j):
        return (c, lax.rem(v + j, groups))

    barrier = pltpu.get_barrier_semaphore()
    for j in range(1, groups):
        pl.semaphore_signal(barrier, inc=1, device_id=peer(j), device_id_type=MESH)
    _, pos_col, ids_col = sort_positions(ids_ref[...], rows)
    at1 = lax.broadcasted_iota(jnp.int32, (count, count), 1)
    ordered = jnp.sum(jnp.where(at1 == pos_col, ids_col, 0), axis=0, keepdims=True)
    mine[...] = jnp.broadcast_to(ordered, mine.shape)
    theirs[v] = mine[...]

    def copy(j):
        return pltpu.make_async_remote_copy(
            src_ref=mine,
            dst_ref=theirs.at[v],
            send_sem=send_sem.at[j],
            recv_sem=recv_sem.at[j],
            device_id=peer(j),
            device_id_type=MESH,
        )

    pl.semaphore_wait(barrier, groups - 1)
    for j in range(1, groups):
        copy(j).start()
    for j in range(1, groups):
        copy(j).wait()
    ids_all = jnp.concatenate([theirs[d, 0:1, :] for d in range(groups)], axis=0)
    ids_out[...] = ids_all
    layer = lax.broadcasted_iota(jnp.int32, (groups, count), 0) // 2
    owner_layer = ids_all // (2 * rows)
    most = jnp.zeros((1, 1), jnp.int32)
    for cut in range(groups // 2 - 1):
        up = jnp.where((layer <= cut) & (owner_layer > cut), 1, 0)
        down = jnp.where((layer > cut) & (owner_layer <= cut), 1, 0)
        for flow in (up, down):
            total = jnp.sum(jnp.sum(flow, axis=1, keepdims=True), axis=0, keepdims=True)
            most = jnp.maximum(most, total)
    most = jnp.max(most)
    branch_out[0] = sum(jnp.where(most > 2 * half * capacity, 1, 0) for half in HALVES)


def chain_kernel(
    groups,
    ckpts,
    chunks,
    half,
    capacity,
    ids_ref,
    ids_all_ref,
    grads_ref,
    all_scales_ref,
    tables_ref,
    out_ref,
    grads,
    tables,
    scales_ref,
    match_ref,
    up_pool_sel,
    up_in_sel,
    down_pool_sel,
    down_in_sel,
    rows_pool_sel,
    rows_up_sel,
    rows_down_sel,
    pool,
    up_in,
    down_in,
    up_out,
    down_out,
    part_send,
    part_recv,
    load_sem,
    pool_sems,
    up_sems,
    up_mate_sems,
    down_sems,
    down_mate_sems,
    part_send_sem,
    part_recv_sem,
):
    c = lax.axis_index("ckpt")
    v = lax.axis_index("vocab")
    layers = groups // 2
    z = v // 2
    core = v % 2
    mate = v + 1 - 2 * core
    rows = tables.shape[0]
    count = grads.shape[0]
    width = grads.shape[1]
    quarter = width // ckpts
    piece = quarter // chunks
    blocks = piece // BLK
    span = half * capacity
    bf16 = jnp.bfloat16
    has_up = z < layers - 1
    has_down = z > 0

    def ckpt_peer(j):
        return (lax.rem(c + j, ckpts), v)

    def greet(device):
        pl.semaphore_signal(barrier, inc=1, device_id=device, device_id_type=MESH)

    barrier = pltpu.get_barrier_semaphore()
    greet((c, mate))
    for j in range(1, ckpts):
        greet(ckpt_peer(j))

    @pl.when(has_up)
    def _():
        greet((c, v + 2))

    @pl.when(has_down)
    def _():
        greet((c, v - 2))

    load_grads = pltpu.make_async_copy(grads_ref, grads, load_sem.at[0])
    load_tables = pltpu.make_async_copy(tables_ref, tables, load_sem.at[1])
    load_scales = pltpu.make_async_copy(all_scales_ref, scales_ref, load_sem.at[2])
    load_grads.start()
    load_scales.start()
    load_tables.start()

    pos_row, _, _ = sort_positions(ids_ref[...], rows)
    at0 = lax.broadcasted_iota(jnp.int32, (count, count), 0)
    at1 = lax.broadcasted_iota(jnp.int32, (count, count), 1)
    match_ref[...] = jnp.where(at0 == pos_row, 1.0, 0.0).astype(bf16)

    ids_all = ids_all_ref[...]
    layer = lax.broadcasted_iota(jnp.int32, (groups, count), 0) // 2
    owner_layer = ids_all // (2 * rows)
    before = jnp.where(at0 < at1, 1.0, 0.0).astype(bf16)

    def places(mask):
        flags = jnp.where(mask, 1.0, 0.0)
        inner = jnp.dot(flags.astype(bf16), before, preferred_element_type=jnp.float32)
        totals = jnp.sum(flags, axis=1, keepdims=True)
        offset = jnp.zeros((1, 1), jnp.float32)
        offsets = []
        for d in range(groups):
            offsets.append(offset)
            offset = offset + totals[d : d + 1]
        place = (inner + jnp.concatenate(offsets, axis=0)).astype(jnp.int32)
        return jnp.where(mask, place, -1)

    up_from = places((layer <= z - 1) & (owner_layer > z - 1))
    up_to = places((layer <= z) & (owner_layer > z))
    down_from = places((layer >= z + 1) & (owner_layer < z + 1))
    down_to = places((layer >= z) & (owner_layer < z))

    def one_hot(size, values):
        shape = (size, count)
        return jnp.where(
            lax.broadcasted_iota(jnp.int32, shape, 0) == values, 1.0, 0.0
        ).astype(bf16)

    def meet(a, b):
        return lax.dot_general(
            a, b, (((1,), (1,)), ((), ())), preferred_element_type=jnp.float32
        )

    up_sum = down_sum = rows_up = rows_down = 0.0
    pools = [[0.0, 0.0] for _ in range(3)]
    for d in range(groups):
        take_up = one_hot(span, up_to[d : d + 1] - core * span)
        take_down = one_hot(span, down_to[d : d + 1] - core * span)
        take_rows = one_hot(rows, ids_all[d : d + 1] - v * rows)
        at_up = one_hot(2 * span, up_from[d : d + 1])
        at_down = one_hot(2 * span, down_from[d : d + 1])
        up_sum += meet(take_up, at_up)
        down_sum += meet(take_down, at_down)
        rows_up += meet(take_rows, at_up)
        rows_down += meet(take_rows, at_down)
        here = jnp.where(z == d // 2, 1.0, 0.0).astype(bf16)
        for i, take in enumerate((take_up, take_down, take_rows)):
            pools[i][d % 2] += take * here
    up_in_sel[...] = up_sum.astype(bf16)
    down_in_sel[...] = down_sum.astype(bf16)
    rows_up_sel[...] = rows_up.astype(bf16)
    rows_down_sel[...] = rows_down.astype(bf16)
    for ref, pair in zip((up_pool_sel, down_pool_sel, rows_pool_sel), pools):
        ref[...] = jnp.concatenate(pair, axis=1).astype(bf16)

    @pl.when(z == 0)
    def _():
        def clear(k, carry):
            up_in[k] = jnp.zeros(up_in.shape[1:], bf16)
            return carry

        lax.fori_loop(0, chunks, clear, 0)

    @pl.when(z == layers - 1)
    def _():
        def clear(k, carry):
            down_in[k] = jnp.zeros(down_in.shape[1:], bf16)
            return carry

        lax.fori_loop(0, chunks, clear, 0)

    def remote(src, dst, sems, k, device):
        return pltpu.make_async_remote_copy(
            src_ref=src,
            dst_ref=dst,
            send_sem=sems.at[0, k],
            recv_sem=sems.at[1, k],
            device_id=device,
            device_id_type=MESH,
        )

    def pool_copy(k):
        return remote(pool.at[k, core], pool.at[k, core], pool_sems, k, (c, mate))

    def up_copy(k):
        return remote(up_out.at[k], up_in.at[k, core], up_sems, k, (c, lax.rem(v + 2, groups)))

    def down_copy(k):
        device = (c, lax.rem(v + groups - 2, groups))
        return remote(down_out.at[k], down_in.at[k, core], down_sems, k, device)

    def up_mate(k):
        return remote(up_in.at[k, core], up_in.at[k, core], up_mate_sems, k, (c, mate))

    def down_mate(k):
        return remote(down_in.at[k, core], down_in.at[k, core], down_mate_sems, k, (c, mate))

    def part_copy(k, j):
        return pltpu.make_async_remote_copy(
            src_ref=part_send.at[k, j],
            dst_ref=part_recv.at[k, j],
            send_sem=part_send_sem.at[k, j],
            recv_sem=part_recv_sem.at[k, j],
            device_id=ckpt_peer(j),
            device_id_type=MESH,
        )

    def place(k):
        block_scales = jnp.concatenate(
            [
                scales_ref[pl.ds(q * (quarter // BLK) + k * blocks, blocks), :]
                for q in range(ckpts)
            ],
            axis=0,
        ).T
        squares = []
        for q in range(ckpts):
            for b in range(blocks):
                at = pl.multiple_of(q * quarter + k * piece + b * BLK, BLK)
                i = q * blocks + b
                g = grads[:, pl.ds(at, BLK)].astype(jnp.float32) * block_scales[:, i : i + 1]
                squares.append((g * g).astype(bf16))
        pool[k, core] = jnp.dot(
            match_ref[...],
            jnp.concatenate(squares, axis=1),
            preferred_element_type=jnp.float32,
        ).astype(bf16)

    def pooled(k):
        return pool[k].reshape(2 * count, ckpts * piece)

    def arrived(ref, k):
        return ref[k].reshape(2 * span, ckpts * piece)

    def dot(a, b):
        return jnp.dot(a, b, preferred_element_type=jnp.float32)

    def weigh_chunk(k):
        fisher = (
            dot(rows_pool_sel[...], pooled(k))
            + dot(rows_up_sel[...], arrived(up_in, k))
            + dot(rows_down_sel[...], arrived(down_in, k))
        )
        weight = (fisher + prior_weight).astype(bf16)
        for q in range(ckpts):
            own = weight[:, q * piece : (q + 1) * piece]
            at = pl.multiple_of(q * quarter + k * piece, BLK)
            table = tables[:, pl.ds(at, piece)].astype(jnp.float32)
            j = lax.rem(q - c + ckpts, ckpts)
            part_send[k, j, 0] = (own.astype(jnp.float32) * table).astype(bf16)
            part_send[k, j, 1] = own
        for j in range(1, ckpts):
            part_copy(k, j).start()

    def finish_chunk(k):
        numer = part_send[k, 0, 0].astype(jnp.float32)
        denom = part_send[k, 0, 1].astype(jnp.float32)
        for j in range(1, ckpts):
            part_copy(k, j).wait_recv()
            numer += part_recv[k, j, 0].astype(jnp.float32)
            denom += part_recv[k, j, 1].astype(jnp.float32)
        at = pl.multiple_of(k * piece, BLK)
        out_ref[:, pl.ds(at, piece)] = (numer / denom).astype(bf16)

    load_grads.wait()
    load_scales.wait()
    load_tables.wait()
    greetings = ckpts + jnp.where(has_up, 1, 0) + jnp.where(has_down, 1, 0)
    pl.semaphore_wait(barrier, greetings)

    def inside(k):
        return (k >= 0) & (k < chunks)

    def step(s, carry):
        up = s - LAG * z
        down = s - LAG * (layers - 1 - z)

        @pl.when(inside(s - 1))
        def _():
            pool_copy(s - 1).wait_recv()

        @pl.when(inside(up - 1) & has_down)
        def _():
            up_mate(up - 1).wait_recv()

        @pl.when(inside(up - 1) & has_up)
        def _():
            k = up - 1
            up_out[k] = (
                dot(up_pool_sel[...], pooled(k)) + dot(up_in_sel[...], arrived(up_in, k))
            ).astype(bf16)
            up_copy(k).start()

        @pl.when(inside(down - 1) & has_up)
        def _():
            down_mate(down - 1).wait_recv()

        @pl.when(inside(down - 1) & has_down)
        def _():
            k = down - 1
            down_out[k] = (
                dot(down_pool_sel[...], pooled(k)) + dot(down_in_sel[...], arrived(down_in, k))
            ).astype(bf16)
            down_copy(k).start()

        @pl.when(s < chunks)
        def _():
            place(s)
            pool_copy(s).start()

        @pl.when(inside(up) & has_down)
        def _():
            up_copy(up).wait_recv()
            up_mate(up).start()

        @pl.when(inside(down) & has_up)
        def _():
            down_copy(down).wait_recv()
            down_mate(down).start()

        ready = jnp.minimum(up, down) - 1

        @pl.when(inside(ready))
        def _():
            weigh_chunk(ready)

        @pl.when(inside(ready - SETTLE))
        def _():
            finish_chunk(ready - SETTLE)

        return carry

    lax.fori_loop(0, chunks + 1 + SETTLE + LAG * (layers - 1), step, 0)

    def drain(k, carry):
        pool_copy(k).wait_send()

        @pl.when(has_up)
        def _():
            up_copy(k).wait_send()
            down_mate(k).wait_send()

        @pl.when(has_down)
        def _():
            down_copy(k).wait_send()
            up_mate(k).wait_send()

        for j in range(1, ckpts):
            part_copy(k, j).wait_send()
        return carry

    lax.fori_loop(0, chunks, drain, 0)


def merge_chain(half, collective, token_ids, ids_all, grad_values, grad_scales, tables):
    groups = lax.axis_size("vocab")
    ckpts = lax.axis_size("ckpt")
    rows, width = tables.shape[1:]
    count = token_ids.shape[0]
    capacity = 2 * count // groups
    chunk_width = width // CHUNKS
    span = half * capacity
    vmem = pl.BlockSpec(memory_space=pltpu.VMEM)
    hbm = pl.BlockSpec(memory_space=pl.ANY)
    bf16 = jnp.bfloat16
    dma = pltpu.SemaphoreType.DMA
    return pl.pallas_call(
        functools.partial(chain_kernel, groups, ckpts, CHUNKS, half, capacity),
        out_shape=jax.ShapeDtypeStruct((rows, width // ckpts), bf16),
        in_specs=[vmem, vmem, hbm, hbm, hbm],
        out_specs=vmem,
        scratch_shapes=[
            pltpu.VMEM((count, width), bf16),
            pltpu.VMEM((rows, width), bf16),
            pltpu.VMEM((width // BLK, count), jnp.float32),
            pltpu.VMEM((count, count), bf16),
            pltpu.VMEM((span, 2 * count), bf16),
            pltpu.VMEM((span, 2 * span), bf16),
            pltpu.VMEM((span, 2 * count), bf16),
            pltpu.VMEM((span, 2 * span), bf16),
            pltpu.VMEM((rows, 2 * count), bf16),
            pltpu.VMEM((rows, 2 * span), bf16),
            pltpu.VMEM((rows, 2 * span), bf16),
            pltpu.VMEM((CHUNKS, 2, count, chunk_width), bf16),
            pltpu.VMEM((CHUNKS, 2, span, chunk_width), bf16),
            pltpu.VMEM((CHUNKS, 2, span, chunk_width), bf16),
            pltpu.VMEM((CHUNKS, span, chunk_width), bf16),
            pltpu.VMEM((CHUNKS, span, chunk_width), bf16),
            pltpu.VMEM((CHUNKS, ckpts, 2, rows, chunk_width // ckpts), bf16),
            pltpu.VMEM((CHUNKS, ckpts, 2, rows, chunk_width // ckpts), bf16),
            dma((3,)),
            dma((2, CHUNKS)),
            dma((2, CHUNKS)),
            dma((2, CHUNKS)),
            dma((2, CHUNKS)),
            dma((2, CHUNKS)),
            dma((CHUNKS, ckpts)),
            dma((CHUNKS, ckpts)),
        ],
        compiler_params=pltpu.CompilerParams(
            collective_id=collective, has_side_effects=True, vmem_limit_bytes=60 * 1024 * 1024
        ),
    )(token_ids.reshape(1, count), ids_all, grad_values[0], grad_scales[0], tables[0])


def merge_by_load(token_ids, grad_values, grad_scales, tables):
    groups = lax.axis_size("vocab")
    rows = tables.shape[1]
    count = token_ids.shape[0]
    capacity = 2 * count // groups
    vmem = pl.BlockSpec(memory_space=pltpu.VMEM)
    dma = pltpu.SemaphoreType.DMA
    ids_all, branch = pl.pallas_call(
        functools.partial(gather_kernel, groups, rows, capacity),
        out_shape=[
            jax.ShapeDtypeStruct((groups, count), jnp.int32),
            jax.ShapeDtypeStruct((1,), jnp.int32),
        ],
        in_specs=[vmem],
        out_specs=[vmem, pl.BlockSpec(memory_space=pltpu.SMEM)],
        scratch_shapes=[
            pltpu.VMEM((8, count), jnp.int32),
            pltpu.VMEM((groups, 8, count), jnp.int32),
            dma((groups,)),
            dma((groups,)),
        ],
        compiler_params=pltpu.CompilerParams(collective_id=0, has_side_effects=True),
    )(token_ids.reshape(1, count))
    args = (token_ids, ids_all, grad_values, grad_scales, tables)
    branches = [functools.partial(merge_chain, half, i + 1) for i, half in enumerate(HALVES)]
    branches.append(lambda ids, _, values, scales, rows: merge_rows(ids, values, scales, rows))
    return lax.switch(branch[0], branches, *args)


def merge_small_slots(token_ids, grad_values, grad_scales, tables):
    groups = lax.axis_size("vocab")
    rows = tables.shape[1]
    width = tables.shape[2]
    count = token_ids.shape[0]
    capacity = 2 * count // groups
    owner = token_ids // rows
    same = owner[:, None] == owner[None, :]
    before = lax.broadcasted_iota(jnp.int32, (count, count), 0) < lax.broadcasted_iota(
        jnp.int32, (count, count), 1
    )
    rank = jnp.sum((same & before).astype(jnp.int32), axis=0)
    slot = owner * capacity + rank
    match = lax.broadcasted_iota(jnp.int32, (groups * capacity, count), 0) == slot[None, :]
    scales = grad_scales[0].T
    grads = (
        grad_values[0].astype(jnp.float32).reshape(count, width // BLK, BLK) * scales[:, :, None]
    )
    squares = (grads * grads).reshape(count, width).astype(jnp.bfloat16)
    placed = jnp.dot(match.astype(jnp.bfloat16), squares, preferred_element_type=jnp.float32)
    buffer = placed.astype(jnp.bfloat16).reshape(groups, capacity, width)
    local_rows = token_ids % rows
    row_tags = (
        jnp.sum(jnp.where(match, local_rows[None, :], 0), axis=1)
        .astype(jnp.bfloat16)
        .reshape(groups, capacity)
    )
    arrived, arrived_rows = (
        lax.all_to_all(buffer, "vocab", split_axis=0, concat_axis=0, tiled=True),
        lax.all_to_all(row_tags, "vocab", split_axis=0, concat_axis=0, tiled=True),
    )
    flat_rows = arrived_rows.reshape(groups * capacity).astype(jnp.int32)
    selector = (
        lax.broadcasted_iota(jnp.int32, (rows, groups * capacity), 0) == flat_rows[None, :]
    ).astype(jnp.bfloat16)
    fisher = jnp.dot(
        selector, arrived.reshape(groups * capacity, width), preferred_element_type=jnp.float32
    )
    weight = (fisher + prior_weight).astype(jnp.bfloat16)
    term = (weight.astype(jnp.float32) * tables[0].astype(jnp.float32)).astype(jnp.bfloat16)
    numer, denom = (
        lax.psum_scatter(term, "ckpt", scatter_dimension=1, tiled=True).astype(jnp.float32),
        lax.psum_scatter(weight, "ckpt", scatter_dimension=1, tiled=True).astype(jnp.float32),
    )
    return (numer / denom).astype(jnp.bfloat16)


def per_device(token_ids, grad_values, grad_scales, tables):
    groups = lax.axis_size("vocab")
    ckpts = lax.axis_size("ckpt")
    count = token_ids.shape[0]
    width = tables.shape[2]
    capacity = 2 * count // groups
    if capacity % 16 == 0 and width % (ckpts * CHUNKS * BLK) == 0:
        if groups == 8:
            return merge_by_load(token_ids, grad_values, grad_scales, tables)
        return merge_rows(token_ids, grad_values, grad_scales, tables)
    return merge_small_slots(token_ids, grad_values, grad_scales, tables)


def solution(mesh):
    return jax.shard_map(
        per_device,
        mesh=mesh,
        in_specs=(
            P("vocab"),
            P("ckpt", "vocab", None),
            P("ckpt", None, "vocab"),
            P("ckpt", "vocab", None),
        ),
        out_specs=P("vocab", "ckpt"),
        check_vma=False,
    )
```

```python
import functools

import jax
import jax.numpy as jnp
from jax import lax
from jax.experimental import pallas as pl
from jax.experimental.pallas import tpu as pltpu
from jax.sharding import PartitionSpec as P

BLK = 128
CHUNKS = 16
LAG = 4
SETTLE = 2
LOADS = (8, 9, 10, 11, 12)
MESH = pl.DeviceIdType.MESH


prior_weight = 1.0


def merge_kernel(
    groups,
    ckpts,
    chunks,
    ids_ref,
    grads_ref,
    all_scales_ref,
    tables_ref,
    out_ref,
    grads,
    tables,
    scales_ref,
    match_ref,
    select_ref,
    tag_send,
    tag_recv,
    send,
    recv,
    part_send,
    part_recv,
    load_sem,
    tag_send_sem,
    tag_recv_sem,
    send_sem,
    recv_sem,
    part_send_sem,
    part_recv_sem,
):
    c = lax.axis_index("ckpt")
    v = lax.axis_index("vocab")
    rows = tables.shape[0]
    count = grads.shape[0]
    width = grads.shape[1]
    slots = match_ref.shape[0]
    capacity = slots // groups
    quarter = width // ckpts
    piece = quarter // chunks
    blocks = piece // BLK

    def vocab_peer(j):
        return (c, lax.rem(v + j, groups))

    def ckpt_peer(j):
        return (lax.rem(c + j, ckpts), v)

    barrier = pltpu.get_barrier_semaphore()
    for j in range(1, groups):
        pl.semaphore_signal(barrier, inc=1, device_id=vocab_peer(j), device_id_type=MESH)
    for j in range(1, ckpts):
        pl.semaphore_signal(barrier, inc=1, device_id=ckpt_peer(j), device_id_type=MESH)

    load_grads = pltpu.make_async_copy(grads_ref, grads, load_sem.at[0])
    load_tables = pltpu.make_async_copy(tables_ref, tables, load_sem.at[1])
    load_scales = pltpu.make_async_copy(all_scales_ref, scales_ref, load_sem.at[2])
    load_grads.start()
    load_scales.start()
    load_tables.start()

    ids_row = ids_ref[...]
    ids_col = jnp.broadcast_to(ids_row, (count, count)).T
    near_row = lax.rem(ids_row // rows - v + groups, groups)
    near_col = lax.rem(ids_col // rows - v + groups, groups)
    same = near_row == near_col
    at0 = lax.broadcasted_iota(jnp.int32, (count, count), 0)
    at1 = lax.broadcasted_iota(jnp.int32, (count, count), 1)
    rank_row = jnp.sum(jnp.where(same & (at0 < at1), 1, 0), axis=0, keepdims=True)
    rank_col = jnp.sum(jnp.where(same & (at1 < at0), 1, 0), axis=1, keepdims=True)
    slot_row = near_row * capacity + rank_row
    slot_col = near_col * capacity + rank_col
    match_ref[...] = jnp.where(
        lax.broadcasted_iota(jnp.int32, (slots, count), 0) == slot_row, 1.0, 0.0
    ).astype(jnp.bfloat16)
    tags = jnp.sum(
        jnp.where(
            lax.broadcasted_iota(jnp.int32, (count, slots), 1) == slot_col[:, 0:1],
            lax.rem(ids_col[:, 0:1], rows),
            0,
        ),
        axis=0,
        keepdims=True,
    )
    tag_send[...] = jnp.broadcast_to(tags, tag_send.shape)

    def tag_copy(j):
        return pltpu.make_async_remote_copy(
            src_ref=tag_send,
            dst_ref=tag_recv.at[j],
            send_sem=tag_send_sem.at[j],
            recv_sem=tag_recv_sem.at[j],
            device_id=vocab_peer(j),
            device_id_type=MESH,
        )

    def row_copy(k, j):
        return pltpu.make_async_remote_copy(
            src_ref=send.at[k, j],
            dst_ref=recv.at[k, j],
            send_sem=send_sem.at[k, j],
            recv_sem=recv_sem.at[k, j],
            device_id=vocab_peer(j),
            device_id_type=MESH,
        )

    def part_copy(k, j):
        return pltpu.make_async_remote_copy(
            src_ref=part_send.at[k, j],
            dst_ref=part_recv.at[k, j],
            send_sem=part_send_sem.at[k, j],
            recv_sem=part_recv_sem.at[k, j],
            device_id=ckpt_peer(j),
            device_id_type=MESH,
        )

    order = sorted(range(1, groups), key=lambda j: -min(j, groups - j))

    def place(k):
        block_scales = jnp.concatenate(
            [
                scales_ref[pl.ds(q * (quarter // BLK) + k * blocks, blocks), :]
                for q in range(ckpts)
            ],
            axis=0,
        ).T
        squares = []
        for q in range(ckpts):
            for b in range(blocks):
                at = pl.multiple_of(q * quarter + k * piece + b * BLK, BLK)
                i = q * blocks + b
                g = grads[:, pl.ds(at, BLK)].astype(jnp.float32) * block_scales[:, i : i + 1]
                squares.append((g * g).astype(jnp.bfloat16))
        placed = jnp.dot(
            match_ref[...],
            jnp.concatenate(squares, axis=1),
            preferred_element_type=jnp.float32,
        ).astype(jnp.bfloat16)
        placed = placed.reshape(groups, capacity, ckpts * piece)
        recv[k, 0] = placed[0]
        for j in range(1, groups):
            send[k, j] = placed[j]

    def start_rows(k):
        for j in order:
            row_copy(k, j).start()

    load_grads.wait()
    load_scales.wait()
    place(0)
    pl.semaphore_wait(barrier, groups + ckpts - 2)
    for j in order:
        tag_copy(j).start()
    start_rows(0)

    def place_next(k, carry):
        place(k)
        start_rows(k)
        return carry

    lax.fori_loop(1, chunks, place_next, 0)

    lane = lax.broadcasted_iota(jnp.int32, (1, slots), 1) // capacity
    arrived_tags = jnp.where(lane == 0, tags, 0)
    for j in range(1, groups):
        tag_copy(j).wait()
        arrived_tags = jnp.where(lane == j, tag_recv[j, 0:1, :], arrived_tags)
    select_ref[...] = jnp.where(
        lax.broadcasted_iota(jnp.int32, (rows, slots), 0) == arrived_tags, 1.0, 0.0
    ).astype(jnp.bfloat16)
    load_tables.wait()

    def weigh_chunk(k):
        for j in range(1, groups):
            row_copy(k, j).wait_recv()
        fisher = jnp.dot(
            select_ref[...],
            recv[k].reshape(slots, ckpts * piece),
            preferred_element_type=jnp.float32,
        )
        weight = (fisher + prior_weight).astype(jnp.bfloat16)
        for q in range(ckpts):
            own = weight[:, q * piece : (q + 1) * piece]
            at = pl.multiple_of(q * quarter + k * piece, BLK)
            table = tables[:, pl.ds(at, piece)].astype(jnp.float32)
            j = lax.rem(q - c + ckpts, ckpts)
            part_send[k, j, 0] = (own.astype(jnp.float32) * table).astype(jnp.bfloat16)
            part_send[k, j, 1] = own
        for j in range(1, ckpts):
            part_copy(k, j).start()

    def finish_chunk(k):
        numer = part_send[k, 0, 0].astype(jnp.float32)
        denom = part_send[k, 0, 1].astype(jnp.float32)
        for j in range(1, ckpts):
            part_copy(k, j).wait_recv()
            numer += part_recv[k, j, 0].astype(jnp.float32)
            denom += part_recv[k, j, 1].astype(jnp.float32)
        at = pl.multiple_of(k * piece, BLK)
        out_ref[:, pl.ds(at, piece)] = (numer / denom).astype(jnp.bfloat16)

    weigh_chunk(0)

    def step(k, carry):
        weigh_chunk(k)
        finish_chunk(k - 1)
        return carry

    lax.fori_loop(1, chunks, step, 0)
    finish_chunk(chunks - 1)

    def drain(k, carry):
        for j in range(1, groups):
            row_copy(k, j).wait_send()
        for j in range(1, ckpts):
            part_copy(k, j).wait_send()
        return carry

    lax.fori_loop(0, chunks, drain, 0)


def merge_rows(token_ids, grad_values, grad_scales, tables):
    groups = lax.axis_size("vocab")
    ckpts = lax.axis_size("ckpt")
    rows, width = tables.shape[1:]
    count = token_ids.shape[0]
    slots = 2 * count
    capacity = slots // groups
    chunk_width = width // CHUNKS
    vmem = pl.BlockSpec(memory_space=pltpu.VMEM)
    hbm = pl.BlockSpec(memory_space=pl.ANY)
    bf16 = jnp.bfloat16
    dma = pltpu.SemaphoreType.DMA
    return pl.pallas_call(
        functools.partial(merge_kernel, groups, ckpts, CHUNKS),
        out_shape=jax.ShapeDtypeStruct((rows, width // ckpts), bf16),
        in_specs=[vmem, hbm, hbm, hbm],
        out_specs=vmem,
        scratch_shapes=[
            pltpu.VMEM((count, width), bf16),
            pltpu.VMEM((rows, width), bf16),
            pltpu.VMEM((width // BLK, count), jnp.float32),
            pltpu.VMEM((slots, count), bf16),
            pltpu.VMEM((rows, slots), bf16),
            pltpu.VMEM((8, slots), jnp.int32),
            pltpu.VMEM((groups, 8, slots), jnp.int32),
            pltpu.VMEM((CHUNKS, groups, capacity, chunk_width), bf16),
            pltpu.VMEM((CHUNKS, groups, capacity, chunk_width), bf16),
            pltpu.VMEM((CHUNKS, ckpts, 2, rows, chunk_width // ckpts), bf16),
            pltpu.VMEM((CHUNKS, ckpts, 2, rows, chunk_width // ckpts), bf16),
            dma((3,)),
            dma((groups,)),
            dma((groups,)),
            dma((CHUNKS, groups)),
            dma((CHUNKS, groups)),
            dma((CHUNKS, ckpts)),
            dma((CHUNKS, ckpts)),
        ],
        compiler_params=pltpu.CompilerParams(
            collective_id=9, has_side_effects=True, vmem_limit_bytes=60 * 1024 * 1024
        ),
        cost_estimate=pl.CostEstimate(
            flops=4 * slots * count * width,
            bytes_accessed=5 * rows * width,
            transcendentals=0,
        ),
    )(
        token_ids.reshape(1, count),
        grad_values[0],
        grad_scales[0],
        tables[0],
    )


def sort_positions(ids_row, rows):
    count = ids_row.shape[1]
    ids_col = jnp.broadcast_to(ids_row, (count, count)).T
    own_row = ids_row // rows
    own_col = ids_col // rows
    at0 = lax.broadcasted_iota(jnp.int32, (count, count), 0)
    at1 = lax.broadcasted_iota(jnp.int32, (count, count), 1)
    same = own_row == own_col
    first0 = (own_col < own_row) | (same & (at0 < at1))
    first1 = (own_row < own_col) | (same & (at1 < at0))
    pos_row = jnp.sum(jnp.where(first0, 1, 0), axis=0, keepdims=True)
    pos_col = jnp.sum(jnp.where(first1, 1, 0), axis=1, keepdims=True)
    return pos_row, pos_col, ids_col[:, 0:1]


def gather_kernel(groups, rows, capacity, ids_ref, ids_out, branch_out, mine, theirs, send_sem, recv_sem):
    c = lax.axis_index("ckpt")
    v = lax.axis_index("vocab")
    count = ids_ref.shape[1]

    def peer(j):
        return (c, lax.rem(v + j, groups))

    barrier = pltpu.get_barrier_semaphore()
    for j in range(1, groups):
        pl.semaphore_signal(barrier, inc=1, device_id=peer(j), device_id_type=MESH)
    _, pos_col, ids_col = sort_positions(ids_ref[...], rows)
    at1 = lax.broadcasted_iota(jnp.int32, (count, count), 1)
    ordered = jnp.sum(jnp.where(at1 == pos_col, ids_col, 0), axis=0, keepdims=True)
    mine[...] = jnp.broadcast_to(ordered, mine.shape)
    theirs[v] = mine[...]

    def copy(j):
        return pltpu.make_async_remote_copy(
            src_ref=mine,
            dst_ref=theirs.at[v],
            send_sem=send_sem.at[j],
            recv_sem=recv_sem.at[j],
            device_id=peer(j),
            device_id_type=MESH,
        )

    pl.semaphore_wait(barrier, groups - 1)
    for j in range(1, groups):
        copy(j).start()
    for j in range(1, groups):
        copy(j).wait()
    ids_all = jnp.concatenate([theirs[d, 0:1, :] for d in range(groups)], axis=0)
    ids_out[...] = ids_all
    layer = lax.broadcasted_iota(jnp.int32, (groups, count), 0) // 2
    owner_layer = ids_all // (2 * rows)
    most = jnp.zeros((1, 1), jnp.int32)
    for cut in range(groups // 2 - 1):
        up = jnp.where((layer <= cut) & (owner_layer > cut), 1, 0)
        down = jnp.where((layer > cut) & (owner_layer <= cut), 1, 0)
        for flow in (up, down):
            total = jnp.sum(jnp.sum(flow, axis=1, keepdims=True), axis=0, keepdims=True)
            most = jnp.maximum(most, total)
    most = jnp.max(most)
    branch_out[0] = sum(jnp.where(most > load * capacity, 1, 0) for load in LOADS)


def chain_kernel(
    groups,
    ckpts,
    chunks,
    span,
    ids_ref,
    ids_all_ref,
    grads_ref,
    all_scales_ref,
    tables_ref,
    out_ref,
    grads,
    tables,
    scales_ref,
    match_ref,
    up_pool_sel,
    up_in_sel,
    down_pool_sel,
    down_in_sel,
    rows_pool_sel,
    rows_up_sel,
    rows_down_sel,
    pool,
    up_in,
    down_in,
    up_out,
    down_out,
    part,
    part_x,
    sum_send,
    sum_recv,
    load_sem,
    pool_sems,
    up_sems,
    up_mate_sems,
    down_sems,
    down_mate_sems,
    x_sems,
    y_sems,
):
    c = lax.axis_index("ckpt")
    v = lax.axis_index("vocab")
    layers = groups // 2
    z = v // 2
    core = v % 2
    mate = v + 1 - 2 * core
    rows = tables.shape[0]
    count = grads.shape[0]
    width = grads.shape[1]
    quarter = width // ckpts
    piece = quarter // chunks
    blocks = piece // BLK
    bf16 = jnp.bfloat16
    has_up = z < layers - 1
    has_down = z > 0

    y, x = c // 2, c % 2
    x_peer = (y * 2 + 1 - x, v)
    y_peer = ((1 - y) * 2 + x, v)

    def greet(device):
        pl.semaphore_signal(barrier, inc=1, device_id=device, device_id_type=MESH)

    barrier = pltpu.get_barrier_semaphore()
    greet((c, mate))
    greet(x_peer)
    greet(y_peer)

    @pl.when(has_up)
    def _():
        greet((c, v + 2))

    @pl.when(has_down)
    def _():
        greet((c, v - 2))

    load_grads = pltpu.make_async_copy(grads_ref, grads, load_sem.at[0])
    load_tables = pltpu.make_async_copy(tables_ref, tables, load_sem.at[1])
    load_scales = pltpu.make_async_copy(all_scales_ref, scales_ref, load_sem.at[2])
    load_grads.start()
    load_scales.start()
    load_tables.start()

    pos_row, _, _ = sort_positions(ids_ref[...], rows)
    at0 = lax.broadcasted_iota(jnp.int32, (count, count), 0)
    at1 = lax.broadcasted_iota(jnp.int32, (count, count), 1)
    match_ref[...] = jnp.where(at0 == pos_row, 1.0, 0.0).astype(bf16)

    ids_all = ids_all_ref[...]
    layer = lax.broadcasted_iota(jnp.int32, (groups, count), 0) // 2
    owner_layer = ids_all // (2 * rows)
    before = jnp.where(at0 < at1, 1.0, 0.0).astype(bf16)

    def places(mask):
        flags = jnp.where(mask, 1.0, 0.0)
        inner = jnp.dot(flags.astype(bf16), before, preferred_element_type=jnp.float32)
        totals = jnp.sum(flags, axis=1, keepdims=True)
        offset = jnp.zeros((1, 1), jnp.float32)
        offsets = []
        for d in range(groups):
            offsets.append(offset)
            offset = offset + totals[d : d + 1]
        place = (inner + jnp.concatenate(offsets, axis=0)).astype(jnp.int32)
        return jnp.where(mask, place, -1)

    up_from = places((layer <= z - 1) & (owner_layer > z - 1))
    up_to = places((layer <= z) & (owner_layer > z))
    down_from = places((layer >= z + 1) & (owner_layer < z + 1))
    down_to = places((layer >= z) & (owner_layer < z))

    def one_hot(size, values):
        shape = (size, count)
        return jnp.where(
            lax.broadcasted_iota(jnp.int32, shape, 0) == values, 1.0, 0.0
        ).astype(bf16)

    def meet(a, b):
        return lax.dot_general(
            a, b, (((1,), (1,)), ((), ())), preferred_element_type=jnp.float32
        )

    up_sum = down_sum = rows_up = rows_down = 0.0
    pools = [[0.0, 0.0] for _ in range(3)]
    for d in range(groups):
        take_up = one_hot(span, up_to[d : d + 1] - core * span)
        take_down = one_hot(span, down_to[d : d + 1] - core * span)
        take_rows = one_hot(rows, ids_all[d : d + 1] - v * rows)
        at_up = one_hot(2 * span, up_from[d : d + 1])
        at_down = one_hot(2 * span, down_from[d : d + 1])
        up_sum += meet(take_up, at_up)
        down_sum += meet(take_down, at_down)
        rows_up += meet(take_rows, at_up)
        rows_down += meet(take_rows, at_down)
        here = jnp.where(z == d // 2, 1.0, 0.0).astype(bf16)
        for i, take in enumerate((take_up, take_down, take_rows)):
            pools[i][d % 2] += take * here
    up_in_sel[...] = up_sum.astype(bf16)
    down_in_sel[...] = down_sum.astype(bf16)
    rows_up_sel[...] = rows_up.astype(bf16)
    rows_down_sel[...] = rows_down.astype(bf16)
    for ref, pair in zip((up_pool_sel, down_pool_sel, rows_pool_sel), pools):
        ref[...] = jnp.concatenate(pair, axis=1).astype(bf16)

    @pl.when(z == 0)
    def _():
        def clear(k, carry):
            up_in[k] = jnp.zeros(up_in.shape[1:], bf16)
            return carry

        lax.fori_loop(0, chunks, clear, 0)

    @pl.when(z == layers - 1)
    def _():
        def clear(k, carry):
            down_in[k] = jnp.zeros(down_in.shape[1:], bf16)
            return carry

        lax.fori_loop(0, chunks, clear, 0)

    def remote(src, dst, sems, k, device):
        return pltpu.make_async_remote_copy(
            src_ref=src,
            dst_ref=dst,
            send_sem=sems.at[0, k],
            recv_sem=sems.at[1, k],
            device_id=device,
            device_id_type=MESH,
        )

    def pool_copy(k):
        return remote(pool.at[k, core], pool.at[k, core], pool_sems, k, (c, mate))

    def up_copy(k):
        return remote(up_out.at[k], up_in.at[k, core], up_sems, k, (c, lax.rem(v + 2, groups)))

    def down_copy(k):
        device = (c, lax.rem(v + groups - 2, groups))
        return remote(down_out.at[k], down_in.at[k, core], down_sems, k, device)

    def up_mate(k):
        return remote(up_in.at[k, core], up_in.at[k, core], up_mate_sems, k, (c, mate))

    def down_mate(k):
        return remote(down_in.at[k, core], down_in.at[k, core], down_mate_sems, k, (c, mate))

    def x_copy(k):
        return remote(part.at[k, 1], part_x.at[k], x_sems, k, x_peer)

    def y_copy(k):
        return remote(sum_send.at[k], sum_recv.at[k], y_sems, k, y_peer)

    def place(k):
        block_scales = jnp.concatenate(
            [
                scales_ref[pl.ds(q * (quarter // BLK) + k * blocks, blocks), :]
                for q in range(ckpts)
            ],
            axis=0,
        ).T
        squares = []
        for q in range(ckpts):
            for b in range(blocks):
                at = pl.multiple_of(q * quarter + k * piece + b * BLK, BLK)
                i = q * blocks + b
                g = grads[:, pl.ds(at, BLK)].astype(jnp.float32) * block_scales[:, i : i + 1]
                squares.append((g * g).astype(bf16))
        pool[k, core] = jnp.dot(
            match_ref[...],
            jnp.concatenate(squares, axis=1),
            preferred_element_type=jnp.float32,
        ).astype(bf16)

    def pooled(k):
        return pool[k].reshape(2 * count, ckpts * piece)

    def arrived(ref, k):
        return ref[k].reshape(2 * span, ckpts * piece)

    def dot(a, b):
        return jnp.dot(a, b, preferred_element_type=jnp.float32)

    def weigh_chunk(k):
        fisher = (
            dot(rows_pool_sel[...], pooled(k))
            + dot(rows_up_sel[...], arrived(up_in, k))
            + dot(rows_down_sel[...], arrived(down_in, k))
        )
        weight = (fisher + prior_weight).astype(bf16)
        for q in range(ckpts):
            own = weight[:, q * piece : (q + 1) * piece]
            at = pl.multiple_of(q * quarter + k * piece, BLK)
            table = tables[:, pl.ds(at, piece)].astype(jnp.float32)
            to_y = (q // 2 + y) % 2
            to_x = (q % 2 + x) % 2
            part[k, to_x, to_y, 0] = (own.astype(jnp.float32) * table).astype(bf16)
            part[k, to_x, to_y, 1] = own
        x_copy(k).start()

    def pair_sum(k, to_y, i):
        return part[k, 0, to_y, i].astype(jnp.float32) + part_x[k, to_y, i].astype(jnp.float32)

    def pass_chunk(k):
        x_copy(k).wait_recv()
        for i in range(2):
            sum_send[k, i] = pair_sum(k, 1, i).astype(bf16)
        y_copy(k).start()

    def finish_chunk(k):
        y_copy(k).wait_recv()
        numer = pair_sum(k, 0, 0) + sum_recv[k, 0].astype(jnp.float32)
        denom = pair_sum(k, 0, 1) + sum_recv[k, 1].astype(jnp.float32)
        at = pl.multiple_of(k * piece, BLK)
        out_ref[:, pl.ds(at, piece)] = (numer / denom).astype(bf16)

    load_grads.wait()
    load_scales.wait()
    load_tables.wait()
    greetings = 3 + jnp.where(has_up, 1, 0) + jnp.where(has_down, 1, 0)
    pl.semaphore_wait(barrier, greetings)

    def inside(k):
        return (k >= 0) & (k < chunks)

    def step(s, carry):
        up = s - LAG * z
        down = s - LAG * (layers - 1 - z)

        @pl.when(inside(s - 1))
        def _():
            pool_copy(s - 1).wait_recv()

        @pl.when(inside(up - 1) & has_down)
        def _():
            up_mate(up - 1).wait_recv()

        @pl.when(inside(up - 1) & has_up)
        def _():
            k = up - 1
            up_out[k] = (
                dot(up_pool_sel[...], pooled(k)) + dot(up_in_sel[...], arrived(up_in, k))
            ).astype(bf16)
            up_copy(k).start()

        @pl.when(inside(down - 1) & has_up)
        def _():
            down_mate(down - 1).wait_recv()

        @pl.when(inside(down - 1) & has_down)
        def _():
            k = down - 1
            down_out[k] = (
                dot(down_pool_sel[...], pooled(k)) + dot(down_in_sel[...], arrived(down_in, k))
            ).astype(bf16)
            down_copy(k).start()

        @pl.when(s < chunks)
        def _():
            place(s)
            pool_copy(s).start()

        @pl.when(inside(up) & has_down)
        def _():
            up_copy(up).wait_recv()
            up_mate(up).start()

        @pl.when(inside(down) & has_up)
        def _():
            down_copy(down).wait_recv()
            down_mate(down).start()

        ready = jnp.minimum(up, down) - 1

        @pl.when(inside(ready))
        def _():
            weigh_chunk(ready)

        @pl.when(inside(ready - SETTLE))
        def _():
            pass_chunk(ready - SETTLE)

        @pl.when(inside(ready - 2 * SETTLE))
        def _():
            finish_chunk(ready - 2 * SETTLE)

        return carry

    lax.fori_loop(0, chunks + 1 + 2 * SETTLE + LAG * (layers - 1), step, 0)

    def drain(k, carry):
        pool_copy(k).wait_send()

        @pl.when(has_up)
        def _():
            up_copy(k).wait_send()
            down_mate(k).wait_send()

        @pl.when(has_down)
        def _():
            down_copy(k).wait_send()
            up_mate(k).wait_send()

        x_copy(k).wait_send()
        y_copy(k).wait_send()
        return carry

    lax.fori_loop(0, chunks, drain, 0)


def merge_chain(load, collective, token_ids, ids_all, grad_values, grad_scales, tables):
    groups = lax.axis_size("vocab")
    ckpts = lax.axis_size("ckpt")
    rows, width = tables.shape[1:]
    count = token_ids.shape[0]
    capacity = 2 * count // groups
    chunk_width = width // CHUNKS
    span = load * capacity // 2
    vmem = pl.BlockSpec(memory_space=pltpu.VMEM)
    hbm = pl.BlockSpec(memory_space=pl.ANY)
    bf16 = jnp.bfloat16
    dma = pltpu.SemaphoreType.DMA
    return pl.pallas_call(
        functools.partial(chain_kernel, groups, ckpts, CHUNKS, span),
        out_shape=jax.ShapeDtypeStruct((rows, width // ckpts), bf16),
        in_specs=[vmem, vmem, hbm, hbm, hbm],
        out_specs=vmem,
        scratch_shapes=[
            pltpu.VMEM((count, width), bf16),
            pltpu.VMEM((rows, width), bf16),
            pltpu.VMEM((width // BLK, count), jnp.float32),
            pltpu.VMEM((count, count), bf16),
            pltpu.VMEM((span, 2 * count), bf16),
            pltpu.VMEM((span, 2 * span), bf16),
            pltpu.VMEM((span, 2 * count), bf16),
            pltpu.VMEM((span, 2 * span), bf16),
            pltpu.VMEM((rows, 2 * count), bf16),
            pltpu.VMEM((rows, 2 * span), bf16),
            pltpu.VMEM((rows, 2 * span), bf16),
            pltpu.VMEM((CHUNKS, 2, count, chunk_width), bf16),
            pltpu.VMEM((CHUNKS, 2, span, chunk_width), bf16),
            pltpu.VMEM((CHUNKS, 2, span, chunk_width), bf16),
            pltpu.VMEM((CHUNKS, span, chunk_width), bf16),
            pltpu.VMEM((CHUNKS, span, chunk_width), bf16),
            pltpu.VMEM((CHUNKS, 2, 2, 2, rows, chunk_width // ckpts), bf16),
            pltpu.VMEM((CHUNKS, 2, 2, rows, chunk_width // ckpts), bf16),
            pltpu.VMEM((CHUNKS, 2, rows, chunk_width // ckpts), bf16),
            pltpu.VMEM((CHUNKS, 2, rows, chunk_width // ckpts), bf16),
            dma((3,)),
            dma((2, CHUNKS)),
            dma((2, CHUNKS)),
            dma((2, CHUNKS)),
            dma((2, CHUNKS)),
            dma((2, CHUNKS)),
            dma((2, CHUNKS)),
            dma((2, CHUNKS)),
        ],
        compiler_params=pltpu.CompilerParams(
            collective_id=collective, has_side_effects=True, vmem_limit_bytes=60 * 1024 * 1024
        ),
    )(token_ids.reshape(1, count), ids_all, grad_values[0], grad_scales[0], tables[0])


def merge_by_load(token_ids, grad_values, grad_scales, tables):
    groups = lax.axis_size("vocab")
    rows = tables.shape[1]
    count = token_ids.shape[0]
    capacity = 2 * count // groups
    vmem = pl.BlockSpec(memory_space=pltpu.VMEM)
    dma = pltpu.SemaphoreType.DMA
    ids_all, branch = pl.pallas_call(
        functools.partial(gather_kernel, groups, rows, capacity),
        out_shape=[
            jax.ShapeDtypeStruct((groups, count), jnp.int32),
            jax.ShapeDtypeStruct((1,), jnp.int32),
        ],
        in_specs=[vmem],
        out_specs=[vmem, pl.BlockSpec(memory_space=pltpu.SMEM)],
        scratch_shapes=[
            pltpu.VMEM((8, count), jnp.int32),
            pltpu.VMEM((groups, 8, count), jnp.int32),
            dma((groups,)),
            dma((groups,)),
        ],
        compiler_params=pltpu.CompilerParams(collective_id=0, has_side_effects=True),
    )(token_ids.reshape(1, count))
    args = (token_ids, ids_all, grad_values, grad_scales, tables)
    branches = [functools.partial(merge_chain, load, i + 1) for i, load in enumerate(LOADS)]
    branches.append(lambda ids, _, values, scales, rows: merge_rows(ids, values, scales, rows))
    return lax.switch(branch[0], branches, *args)


def merge_small_slots(token_ids, grad_values, grad_scales, tables):
    groups = lax.axis_size("vocab")
    rows = tables.shape[1]
    width = tables.shape[2]
    count = token_ids.shape[0]
    capacity = 2 * count // groups
    owner = token_ids // rows
    same = owner[:, None] == owner[None, :]
    before = lax.broadcasted_iota(jnp.int32, (count, count), 0) < lax.broadcasted_iota(
        jnp.int32, (count, count), 1
    )
    rank = jnp.sum((same & before).astype(jnp.int32), axis=0)
    slot = owner * capacity + rank
    match = lax.broadcasted_iota(jnp.int32, (groups * capacity, count), 0) == slot[None, :]
    scales = grad_scales[0].T
    grads = (
        grad_values[0].astype(jnp.float32).reshape(count, width // BLK, BLK) * scales[:, :, None]
    )
    squares = (grads * grads).reshape(count, width).astype(jnp.bfloat16)
    placed = jnp.dot(match.astype(jnp.bfloat16), squares, preferred_element_type=jnp.float32)
    buffer = placed.astype(jnp.bfloat16).reshape(groups, capacity, width)
    local_rows = token_ids % rows
    row_tags = (
        jnp.sum(jnp.where(match, local_rows[None, :], 0), axis=1)
        .astype(jnp.bfloat16)
        .reshape(groups, capacity)
    )
    arrived, arrived_rows = (
        lax.all_to_all(buffer, "vocab", split_axis=0, concat_axis=0, tiled=True),
        lax.all_to_all(row_tags, "vocab", split_axis=0, concat_axis=0, tiled=True),
    )
    flat_rows = arrived_rows.reshape(groups * capacity).astype(jnp.int32)
    selector = (
        lax.broadcasted_iota(jnp.int32, (rows, groups * capacity), 0) == flat_rows[None, :]
    ).astype(jnp.bfloat16)
    fisher = jnp.dot(
        selector, arrived.reshape(groups * capacity, width), preferred_element_type=jnp.float32
    )
    weight = (fisher + prior_weight).astype(jnp.bfloat16)
    term = (weight.astype(jnp.float32) * tables[0].astype(jnp.float32)).astype(jnp.bfloat16)
    numer, denom = (
        lax.psum_scatter(term, "ckpt", scatter_dimension=1, tiled=True).astype(jnp.float32),
        lax.psum_scatter(weight, "ckpt", scatter_dimension=1, tiled=True).astype(jnp.float32),
    )
    return (numer / denom).astype(jnp.bfloat16)


def per_device(token_ids, grad_values, grad_scales, tables):
    groups = lax.axis_size("vocab")
    ckpts = lax.axis_size("ckpt")
    count = token_ids.shape[0]
    width = tables.shape[2]
    capacity = 2 * count // groups
    if capacity % 16 == 0 and width % (ckpts * CHUNKS * BLK) == 0:
        if groups == 8 and ckpts == 4:
            return merge_by_load(token_ids, grad_values, grad_scales, tables)
        return merge_rows(token_ids, grad_values, grad_scales, tables)
    return merge_small_slots(token_ids, grad_values, grad_scales, tables)


def solution(mesh):
    return jax.shard_map(
        per_device,
        mesh=mesh,
        in_specs=(
            P("vocab"),
            P("ckpt", "vocab", None),
            P("ckpt", None, "vocab"),
            P("ckpt", "vocab", None),
        ),
        out_specs=P("vocab", "ckpt"),
        check_vma=False,
    )
```

```python
import functools

import jax
import jax.numpy as jnp
from jax import lax
from jax.experimental import pallas as pl
from jax.experimental.pallas import tpu as pltpu
from jax.sharding import PartitionSpec as P

BLK = 128
CHUNKS = 16
CHAIN_CHUNKS = 32
LAG = 4
SETTLE = 2
LOADS = (8, 9, 10, 11, 12)
MESH = pl.DeviceIdType.MESH


prior_weight = 1.0


def merge_kernel(
    groups,
    ckpts,
    chunks,
    ids_ref,
    grads_ref,
    all_scales_ref,
    tables_ref,
    out_ref,
    grads,
    tables,
    scales_ref,
    match_ref,
    select_ref,
    tag_send,
    tag_recv,
    send,
    recv,
    part_send,
    part_recv,
    load_sem,
    tag_send_sem,
    tag_recv_sem,
    send_sem,
    recv_sem,
    part_send_sem,
    part_recv_sem,
):
    c = lax.axis_index("ckpt")
    v = lax.axis_index("vocab")
    rows = tables.shape[0]
    count = grads.shape[0]
    width = grads.shape[1]
    slots = match_ref.shape[0]
    capacity = slots // groups
    quarter = width // ckpts
    piece = quarter // chunks
    blocks = piece // BLK

    def vocab_peer(j):
        return (c, lax.rem(v + j, groups))

    def ckpt_peer(j):
        return (lax.rem(c + j, ckpts), v)

    barrier = pltpu.get_barrier_semaphore()
    for j in range(1, groups):
        pl.semaphore_signal(barrier, inc=1, device_id=vocab_peer(j), device_id_type=MESH)
    for j in range(1, ckpts):
        pl.semaphore_signal(barrier, inc=1, device_id=ckpt_peer(j), device_id_type=MESH)

    load_grads = pltpu.make_async_copy(grads_ref, grads, load_sem.at[0])
    load_tables = pltpu.make_async_copy(tables_ref, tables, load_sem.at[1])
    load_scales = pltpu.make_async_copy(all_scales_ref, scales_ref, load_sem.at[2])
    load_grads.start()
    load_scales.start()
    load_tables.start()

    ids_row = ids_ref[...]
    ids_col = jnp.broadcast_to(ids_row, (count, count)).T
    near_row = lax.rem(ids_row // rows - v + groups, groups)
    near_col = lax.rem(ids_col // rows - v + groups, groups)
    same = near_row == near_col
    at0 = lax.broadcasted_iota(jnp.int32, (count, count), 0)
    at1 = lax.broadcasted_iota(jnp.int32, (count, count), 1)
    rank_row = jnp.sum(jnp.where(same & (at0 < at1), 1, 0), axis=0, keepdims=True)
    rank_col = jnp.sum(jnp.where(same & (at1 < at0), 1, 0), axis=1, keepdims=True)
    slot_row = near_row * capacity + rank_row
    slot_col = near_col * capacity + rank_col
    match_ref[...] = jnp.where(
        lax.broadcasted_iota(jnp.int32, (slots, count), 0) == slot_row, 1.0, 0.0
    ).astype(jnp.bfloat16)
    tags = jnp.sum(
        jnp.where(
            lax.broadcasted_iota(jnp.int32, (count, slots), 1) == slot_col[:, 0:1],
            lax.rem(ids_col[:, 0:1], rows),
            0,
        ),
        axis=0,
        keepdims=True,
    )
    tag_send[...] = jnp.broadcast_to(tags, tag_send.shape)

    def tag_copy(j):
        return pltpu.make_async_remote_copy(
            src_ref=tag_send,
            dst_ref=tag_recv.at[j],
            send_sem=tag_send_sem.at[j],
            recv_sem=tag_recv_sem.at[j],
            device_id=vocab_peer(j),
            device_id_type=MESH,
        )

    def row_copy(k, j):
        return pltpu.make_async_remote_copy(
            src_ref=send.at[k, j],
            dst_ref=recv.at[k, j],
            send_sem=send_sem.at[k, j],
            recv_sem=recv_sem.at[k, j],
            device_id=vocab_peer(j),
            device_id_type=MESH,
        )

    def part_copy(k, j):
        return pltpu.make_async_remote_copy(
            src_ref=part_send.at[k, j],
            dst_ref=part_recv.at[k, j],
            send_sem=part_send_sem.at[k, j],
            recv_sem=part_recv_sem.at[k, j],
            device_id=ckpt_peer(j),
            device_id_type=MESH,
        )

    order = sorted(range(1, groups), key=lambda j: -min(j, groups - j))

    def place(k):
        block_scales = jnp.concatenate(
            [
                scales_ref[pl.ds(q * (quarter // BLK) + k * blocks, blocks), :]
                for q in range(ckpts)
            ],
            axis=0,
        ).T
        squares = []
        for q in range(ckpts):
            for b in range(blocks):
                at = pl.multiple_of(q * quarter + k * piece + b * BLK, BLK)
                i = q * blocks + b
                g = grads[:, pl.ds(at, BLK)].astype(jnp.float32) * block_scales[:, i : i + 1]
                squares.append((g * g).astype(jnp.bfloat16))
        placed = jnp.dot(
            match_ref[...],
            jnp.concatenate(squares, axis=1),
            preferred_element_type=jnp.float32,
        ).astype(jnp.bfloat16)
        placed = placed.reshape(groups, capacity, ckpts * piece)
        recv[k, 0] = placed[0]
        for j in range(1, groups):
            send[k, j] = placed[j]

    def start_rows(k):
        for j in order:
            row_copy(k, j).start()

    load_grads.wait()
    load_scales.wait()
    place(0)
    pl.semaphore_wait(barrier, groups + ckpts - 2)
    for j in order:
        tag_copy(j).start()
    start_rows(0)

    def place_next(k, carry):
        place(k)
        start_rows(k)
        return carry

    lax.fori_loop(1, chunks, place_next, 0)

    lane = lax.broadcasted_iota(jnp.int32, (1, slots), 1) // capacity
    arrived_tags = jnp.where(lane == 0, tags, 0)
    for j in range(1, groups):
        tag_copy(j).wait()
        arrived_tags = jnp.where(lane == j, tag_recv[j, 0:1, :], arrived_tags)
    select_ref[...] = jnp.where(
        lax.broadcasted_iota(jnp.int32, (rows, slots), 0) == arrived_tags, 1.0, 0.0
    ).astype(jnp.bfloat16)
    load_tables.wait()

    def weigh_chunk(k):
        for j in range(1, groups):
            row_copy(k, j).wait_recv()
        fisher = jnp.dot(
            select_ref[...],
            recv[k].reshape(slots, ckpts * piece),
            preferred_element_type=jnp.float32,
        )
        weight = (fisher + prior_weight).astype(jnp.bfloat16)
        for q in range(ckpts):
            own = weight[:, q * piece : (q + 1) * piece]
            at = pl.multiple_of(q * quarter + k * piece, BLK)
            table = tables[:, pl.ds(at, piece)].astype(jnp.float32)
            j = lax.rem(q - c + ckpts, ckpts)
            part_send[k, j, 0] = (own.astype(jnp.float32) * table).astype(jnp.bfloat16)
            part_send[k, j, 1] = own
        for j in range(1, ckpts):
            part_copy(k, j).start()

    def finish_chunk(k):
        numer = part_send[k, 0, 0].astype(jnp.float32)
        denom = part_send[k, 0, 1].astype(jnp.float32)
        for j in range(1, ckpts):
            part_copy(k, j).wait_recv()
            numer += part_recv[k, j, 0].astype(jnp.float32)
            denom += part_recv[k, j, 1].astype(jnp.float32)
        at = pl.multiple_of(k * piece, BLK)
        out_ref[:, pl.ds(at, piece)] = (numer / denom).astype(jnp.bfloat16)

    weigh_chunk(0)

    def step(k, carry):
        weigh_chunk(k)
        finish_chunk(k - 1)
        return carry

    lax.fori_loop(1, chunks, step, 0)
    finish_chunk(chunks - 1)

    def drain(k, carry):
        for j in range(1, groups):
            row_copy(k, j).wait_send()
        for j in range(1, ckpts):
            part_copy(k, j).wait_send()
        return carry

    lax.fori_loop(0, chunks, drain, 0)


def merge_rows(token_ids, grad_values, grad_scales, tables):
    groups = lax.axis_size("vocab")
    ckpts = lax.axis_size("ckpt")
    rows, width = tables.shape[1:]
    count = token_ids.shape[0]
    slots = 2 * count
    capacity = slots // groups
    chunk_width = width // CHUNKS
    vmem = pl.BlockSpec(memory_space=pltpu.VMEM)
    hbm = pl.BlockSpec(memory_space=pl.ANY)
    bf16 = jnp.bfloat16
    dma = pltpu.SemaphoreType.DMA
    return pl.pallas_call(
        functools.partial(merge_kernel, groups, ckpts, CHUNKS),
        out_shape=jax.ShapeDtypeStruct((rows, width // ckpts), bf16),
        in_specs=[vmem, hbm, hbm, hbm],
        out_specs=vmem,
        scratch_shapes=[
            pltpu.VMEM((count, width), bf16),
            pltpu.VMEM((rows, width), bf16),
            pltpu.VMEM((width // BLK, count), jnp.float32),
            pltpu.VMEM((slots, count), bf16),
            pltpu.VMEM((rows, slots), bf16),
            pltpu.VMEM((8, slots), jnp.int32),
            pltpu.VMEM((groups, 8, slots), jnp.int32),
            pltpu.VMEM((CHUNKS, groups, capacity, chunk_width), bf16),
            pltpu.VMEM((CHUNKS, groups, capacity, chunk_width), bf16),
            pltpu.VMEM((CHUNKS, ckpts, 2, rows, chunk_width // ckpts), bf16),
            pltpu.VMEM((CHUNKS, ckpts, 2, rows, chunk_width // ckpts), bf16),
            dma((3,)),
            dma((groups,)),
            dma((groups,)),
            dma((CHUNKS, groups)),
            dma((CHUNKS, groups)),
            dma((CHUNKS, ckpts)),
            dma((CHUNKS, ckpts)),
        ],
        compiler_params=pltpu.CompilerParams(
            collective_id=9, has_side_effects=True, vmem_limit_bytes=60 * 1024 * 1024
        ),
        cost_estimate=pl.CostEstimate(
            flops=4 * slots * count * width,
            bytes_accessed=5 * rows * width,
            transcendentals=0,
        ),
    )(
        token_ids.reshape(1, count),
        grad_values[0],
        grad_scales[0],
        tables[0],
    )


def sort_positions(ids_row, rows):
    count = ids_row.shape[1]
    ids_col = jnp.broadcast_to(ids_row, (count, count)).T
    own_row = ids_row // rows
    own_col = ids_col // rows
    at0 = lax.broadcasted_iota(jnp.int32, (count, count), 0)
    at1 = lax.broadcasted_iota(jnp.int32, (count, count), 1)
    same = own_row == own_col
    first0 = (own_col < own_row) | (same & (at0 < at1))
    first1 = (own_row < own_col) | (same & (at1 < at0))
    pos_row = jnp.sum(jnp.where(first0, 1, 0), axis=0, keepdims=True)
    pos_col = jnp.sum(jnp.where(first1, 1, 0), axis=1, keepdims=True)
    return pos_row, pos_col, ids_col[:, 0:1]


def gather_kernel(groups, rows, capacity, ids_ref, ids_out, branch_out, mine, theirs, send_sem, recv_sem):
    c = lax.axis_index("ckpt")
    v = lax.axis_index("vocab")
    count = ids_ref.shape[1]

    def peer(j):
        return (c, lax.rem(v + j, groups))

    barrier = pltpu.get_barrier_semaphore()
    for j in range(1, groups):
        pl.semaphore_signal(barrier, inc=1, device_id=peer(j), device_id_type=MESH)
    _, pos_col, ids_col = sort_positions(ids_ref[...], rows)
    at1 = lax.broadcasted_iota(jnp.int32, (count, count), 1)
    ordered = jnp.sum(jnp.where(at1 == pos_col, ids_col, 0), axis=0, keepdims=True)
    mine[...] = jnp.broadcast_to(ordered, mine.shape)
    theirs[v] = mine[...]

    def copy(j):
        return pltpu.make_async_remote_copy(
            src_ref=mine,
            dst_ref=theirs.at[v],
            send_sem=send_sem.at[j],
            recv_sem=recv_sem.at[j],
            device_id=peer(j),
            device_id_type=MESH,
        )

    pl.semaphore_wait(barrier, groups - 1)
    for j in range(1, groups):
        copy(j).start()
    for j in range(1, groups):
        copy(j).wait()
    ids_all = jnp.concatenate([theirs[d, 0:1, :] for d in range(groups)], axis=0)
    ids_out[...] = ids_all
    layer = lax.broadcasted_iota(jnp.int32, (groups, count), 0) // 2
    owner_layer = ids_all // (2 * rows)
    most = jnp.zeros((1, 1), jnp.int32)
    for cut in range(groups // 2 - 1):
        up = jnp.where((layer <= cut) & (owner_layer > cut), 1, 0)
        down = jnp.where((layer > cut) & (owner_layer <= cut), 1, 0)
        for flow in (up, down):
            total = jnp.sum(jnp.sum(flow, axis=1, keepdims=True), axis=0, keepdims=True)
            most = jnp.maximum(most, total)
    most = jnp.max(most)
    branch_out[0] = sum(jnp.where(most > load * capacity, 1, 0) for load in LOADS)


def chain_kernel(
    groups,
    ckpts,
    chunks,
    span,
    ids_ref,
    ids_all_ref,
    grads_ref,
    all_scales_ref,
    tables_ref,
    out_ref,
    grads,
    tables,
    scales_ref,
    match_ref,
    up_pool_sel,
    up_in_sel,
    down_pool_sel,
    down_in_sel,
    rows_pool_sel,
    rows_up_sel,
    rows_down_sel,
    pool,
    up_in,
    down_in,
    up_out,
    down_out,
    part,
    part_x,
    sum_send,
    sum_recv,
    load_sem,
    pool_sems,
    up_sems,
    up_mate_sems,
    down_sems,
    down_mate_sems,
    x_sems,
    y_sems,
):
    c = lax.axis_index("ckpt")
    v = lax.axis_index("vocab")
    layers = groups // 2
    z = v // 2
    core = v % 2
    mate = v + 1 - 2 * core
    rows = tables.shape[0]
    count = grads.shape[0]
    width = grads.shape[1]
    quarter = width // ckpts
    piece = 2 * quarter // chunks
    blocks = piece // BLK
    bf16 = jnp.bfloat16
    has_up = z < layers - 1
    has_down = z > 0

    y, x = c // 2, c % 2
    x_peer = (y * 2 + 1 - x, v)
    y_peer = ((1 - y) * 2 + x, v)

    def greet(device):
        pl.semaphore_signal(barrier, inc=1, device_id=device, device_id_type=MESH)

    barrier = pltpu.get_barrier_semaphore()
    greet((c, mate))
    greet(x_peer)
    greet(y_peer)

    @pl.when(has_up)
    def _():
        greet((c, v + 2))

    @pl.when(has_down)
    def _():
        greet((c, v - 2))

    load_grads = pltpu.make_async_copy(grads_ref, grads, load_sem.at[0])
    load_tables = pltpu.make_async_copy(tables_ref, tables, load_sem.at[1])
    load_scales = pltpu.make_async_copy(all_scales_ref, scales_ref, load_sem.at[2])
    load_grads.start()
    load_scales.start()
    load_tables.start()

    pos_row, _, _ = sort_positions(ids_ref[...], rows)
    at0 = lax.broadcasted_iota(jnp.int32, (count, count), 0)
    at1 = lax.broadcasted_iota(jnp.int32, (count, count), 1)
    match_ref[...] = jnp.where(at0 == pos_row, 1.0, 0.0).astype(bf16)

    ids_all = ids_all_ref[...]
    layer = lax.broadcasted_iota(jnp.int32, (groups, count), 0) // 2
    owner_layer = ids_all // (2 * rows)
    before = jnp.where(at0 < at1, 1.0, 0.0).astype(bf16)

    def places(mask):
        flags = jnp.where(mask, 1.0, 0.0)
        inner = jnp.dot(flags.astype(bf16), before, preferred_element_type=jnp.float32)
        totals = jnp.sum(flags, axis=1, keepdims=True)
        offset = jnp.zeros((1, 1), jnp.float32)
        offsets = []
        for d in range(groups):
            offsets.append(offset)
            offset = offset + totals[d : d + 1]
        place = (inner + jnp.concatenate(offsets, axis=0)).astype(jnp.int32)
        return jnp.where(mask, place, -1)

    up_from = places((layer <= z - 1) & (owner_layer > z - 1))
    up_to = places((layer <= z) & (owner_layer > z))
    down_from = places((layer >= z + 1) & (owner_layer < z + 1))
    down_to = places((layer >= z) & (owner_layer < z))

    def one_hot(size, values):
        shape = (size, count)
        return jnp.where(
            lax.broadcasted_iota(jnp.int32, shape, 0) == values, 1.0, 0.0
        ).astype(bf16)

    def meet(a, b):
        return lax.dot_general(
            a, b, (((1,), (1,)), ((), ())), preferred_element_type=jnp.float32
        )

    up_sum = down_sum = rows_up = rows_down = 0.0
    pools = [[0.0, 0.0] for _ in range(3)]
    for d in range(groups):
        take_up = one_hot(span, up_to[d : d + 1] - core * span)
        take_down = one_hot(span, down_to[d : d + 1] - core * span)
        take_rows = one_hot(rows, ids_all[d : d + 1] - v * rows)
        at_up = one_hot(2 * span, up_from[d : d + 1])
        at_down = one_hot(2 * span, down_from[d : d + 1])
        up_sum += meet(take_up, at_up)
        down_sum += meet(take_down, at_down)
        rows_up += meet(take_rows, at_up)
        rows_down += meet(take_rows, at_down)
        here = jnp.where(z == d // 2, 1.0, 0.0).astype(bf16)
        for i, take in enumerate((take_up, take_down, take_rows)):
            pools[i][d % 2] += take * here
    up_in_sel[...] = up_sum.astype(bf16)
    down_in_sel[...] = down_sum.astype(bf16)
    rows_up_sel[...] = rows_up.astype(bf16)
    rows_down_sel[...] = rows_down.astype(bf16)
    for ref, pair in zip((up_pool_sel, down_pool_sel, rows_pool_sel), pools):
        ref[...] = jnp.concatenate(pair, axis=1).astype(bf16)

    @pl.when(z == 0)
    def _():
        def clear(k, carry):
            up_in[k] = jnp.zeros(up_in.shape[1:], bf16)
            return carry

        lax.fori_loop(0, chunks, clear, 0)

    @pl.when(z == layers - 1)
    def _():
        def clear(k, carry):
            down_in[k] = jnp.zeros(down_in.shape[1:], bf16)
            return carry

        lax.fori_loop(0, chunks, clear, 0)

    def remote(src, dst, sems, k, device):
        return pltpu.make_async_remote_copy(
            src_ref=src,
            dst_ref=dst,
            send_sem=sems.at[0, k],
            recv_sem=sems.at[1, k],
            device_id=device,
            device_id_type=MESH,
        )

    def pool_copy(k):
        return remote(pool.at[k, core], pool.at[k, core], pool_sems, k, (c, mate))

    def up_copy(k):
        return remote(up_out.at[k], up_in.at[k, core], up_sems, k, (c, lax.rem(v + 2, groups)))

    def down_copy(k):
        device = (c, lax.rem(v + groups - 2, groups))
        return remote(down_out.at[k], down_in.at[k, core], down_sems, k, device)

    def up_mate(k):
        return remote(up_in.at[k, core], up_in.at[k, core], up_mate_sems, k, (c, mate))

    def down_mate(k):
        return remote(down_in.at[k, core], down_in.at[k, core], down_mate_sems, k, (c, mate))

    def x_copy(k):
        return remote(part.at[k], part_x.at[k], x_sems, k, x_peer)

    def y_copy(k):
        return remote(sum_send.at[k], sum_recv.at[k], y_sems, k, y_peer)

    def column(k, i):
        return (i * 2 + k % 2) * quarter + (k // 2) * piece

    def place(k):
        block_scales = jnp.concatenate(
            [
                scales_ref[pl.ds(pl.multiple_of(column(k, i) // BLK, blocks), blocks), :]
                for i in range(2)
            ],
            axis=0,
        ).T
        squares = []
        for i in range(2):
            for b in range(blocks):
                at = pl.multiple_of(column(k, i) + b * BLK, BLK)
                n = i * blocks + b
                g = grads[:, pl.ds(at, BLK)].astype(jnp.float32) * block_scales[:, n : n + 1]
                squares.append((g * g).astype(bf16))
        pool[k, core] = jnp.dot(
            match_ref[...],
            jnp.concatenate(squares, axis=1),
            preferred_element_type=jnp.float32,
        ).astype(bf16)

    def pooled(k):
        return pool[k].reshape(2 * count, 2 * piece)

    def arrived(ref, k):
        return ref[k].reshape(2 * span, 2 * piece)

    def dot(a, b):
        return jnp.dot(a, b, preferred_element_type=jnp.float32)

    def weigh_chunk(k):
        fisher = (
            dot(rows_pool_sel[...], pooled(k))
            + dot(rows_up_sel[...], arrived(up_in, k))
            + dot(rows_down_sel[...], arrived(down_in, k))
        )
        weight = (fisher + prior_weight).astype(bf16)
        for i in range(2):
            own = weight[:, i * piece : (i + 1) * piece]
            at = pl.multiple_of(column(k, i), BLK)
            table = tables[:, pl.ds(at, piece)].astype(jnp.float32)
            to_y = (i + y) % 2
            part[k, to_y, 0] = (own.astype(jnp.float32) * table).astype(bf16)
            part[k, to_y, 1] = own

        @pl.when(x != k % 2)
        def _():
            x_copy(k).start()

    def pair_sum(k, to_y, i):
        return part[k, to_y, i].astype(jnp.float32) + part_x[k, to_y, i].astype(jnp.float32)

    def pass_chunk(k):
        x_copy(k).wait_recv()
        for i in range(2):
            sum_send[k, i] = pair_sum(k, 1, i).astype(bf16)
        y_copy(k).start()

    def finish_chunk(k):
        y_copy(k).wait_recv()
        numer = pair_sum(k, 0, 0) + sum_recv[k, 0].astype(jnp.float32)
        denom = pair_sum(k, 0, 1) + sum_recv[k, 1].astype(jnp.float32)
        at = pl.multiple_of((k // 2) * piece, BLK)
        out_ref[:, pl.ds(at, piece)] = (numer / denom).astype(bf16)

    load_grads.wait()
    load_scales.wait()
    load_tables.wait()
    greetings = 3 + jnp.where(has_up, 1, 0) + jnp.where(has_down, 1, 0)
    pl.semaphore_wait(barrier, greetings)

    def inside(k):
        return (k >= 0) & (k < chunks)

    def step(s, carry):
        up = s - LAG * z
        down = s - LAG * (layers - 1 - z)

        @pl.when(inside(s - 1))
        def _():
            pool_copy(s - 1).wait_recv()

        @pl.when(inside(up - 1) & has_down)
        def _():
            up_mate(up - 1).wait_recv()

        @pl.when(inside(up - 1) & has_up)
        def _():
            k = up - 1
            up_out[k] = (
                dot(up_pool_sel[...], pooled(k)) + dot(up_in_sel[...], arrived(up_in, k))
            ).astype(bf16)
            up_copy(k).start()

        @pl.when(inside(down - 1) & has_up)
        def _():
            down_mate(down - 1).wait_recv()

        @pl.when(inside(down - 1) & has_down)
        def _():
            k = down - 1
            down_out[k] = (
                dot(down_pool_sel[...], pooled(k)) + dot(down_in_sel[...], arrived(down_in, k))
            ).astype(bf16)
            down_copy(k).start()

        @pl.when(s < chunks)
        def _():
            place(s)
            pool_copy(s).start()

        @pl.when(inside(up) & has_down)
        def _():
            up_copy(up).wait_recv()
            up_mate(up).start()

        @pl.when(inside(down) & has_up)
        def _():
            down_copy(down).wait_recv()
            down_mate(down).start()

        ready = jnp.minimum(up, down) - 1

        @pl.when(inside(ready))
        def _():
            weigh_chunk(ready)

        @pl.when(inside(ready - SETTLE) & (x == (ready - SETTLE) % 2))
        def _():
            pass_chunk(ready - SETTLE)

        @pl.when(inside(ready - 2 * SETTLE) & (x == ready % 2))
        def _():
            finish_chunk(ready - 2 * SETTLE)

        return carry

    lax.fori_loop(0, chunks + 1 + 2 * SETTLE + LAG * (layers - 1), step, 0)

    def drain(k, carry):
        pool_copy(k).wait_send()

        @pl.when(has_up)
        def _():
            up_copy(k).wait_send()
            down_mate(k).wait_send()

        @pl.when(has_down)
        def _():
            down_copy(k).wait_send()
            up_mate(k).wait_send()

        @pl.when(x != k % 2)
        def _():
            x_copy(k).wait_send()

        @pl.when(x == k % 2)
        def _():
            y_copy(k).wait_send()

        return carry

    lax.fori_loop(0, chunks, drain, 0)


def merge_chain(load, collective, token_ids, ids_all, grad_values, grad_scales, tables):
    groups = lax.axis_size("vocab")
    ckpts = lax.axis_size("ckpt")
    rows, width = tables.shape[1:]
    count = token_ids.shape[0]
    capacity = 2 * count // groups
    piece = width // ckpts * 2 // CHAIN_CHUNKS
    chunk_width = 2 * piece
    span = load * capacity // 2
    vmem = pl.BlockSpec(memory_space=pltpu.VMEM)
    hbm = pl.BlockSpec(memory_space=pl.ANY)
    bf16 = jnp.bfloat16
    dma = pltpu.SemaphoreType.DMA
    return pl.pallas_call(
        functools.partial(chain_kernel, groups, ckpts, CHAIN_CHUNKS, span),
        out_shape=jax.ShapeDtypeStruct((rows, width // ckpts), bf16),
        in_specs=[vmem, vmem, hbm, hbm, hbm],
        out_specs=vmem,
        scratch_shapes=[
            pltpu.VMEM((count, width), bf16),
            pltpu.VMEM((rows, width), bf16),
            pltpu.VMEM((width // BLK, count), jnp.float32),
            pltpu.VMEM((count, count), bf16),
            pltpu.VMEM((span, 2 * count), bf16),
            pltpu.VMEM((span, 2 * span), bf16),
            pltpu.VMEM((span, 2 * count), bf16),
            pltpu.VMEM((span, 2 * span), bf16),
            pltpu.VMEM((rows, 2 * count), bf16),
            pltpu.VMEM((rows, 2 * span), bf16),
            pltpu.VMEM((rows, 2 * span), bf16),
            pltpu.VMEM((CHAIN_CHUNKS, 2, count, chunk_width), bf16),
            pltpu.VMEM((CHAIN_CHUNKS, 2, span, chunk_width), bf16),
            pltpu.VMEM((CHAIN_CHUNKS, 2, span, chunk_width), bf16),
            pltpu.VMEM((CHAIN_CHUNKS, span, chunk_width), bf16),
            pltpu.VMEM((CHAIN_CHUNKS, span, chunk_width), bf16),
            pltpu.VMEM((CHAIN_CHUNKS, 2, 2, rows, piece), bf16),
            pltpu.VMEM((CHAIN_CHUNKS, 2, 2, rows, piece), bf16),
            pltpu.VMEM((CHAIN_CHUNKS, 2, rows, piece), bf16),
            pltpu.VMEM((CHAIN_CHUNKS, 2, rows, piece), bf16),
            dma((3,)),
            dma((2, CHAIN_CHUNKS)),
            dma((2, CHAIN_CHUNKS)),
            dma((2, CHAIN_CHUNKS)),
            dma((2, CHAIN_CHUNKS)),
            dma((2, CHAIN_CHUNKS)),
            dma((2, CHAIN_CHUNKS)),
            dma((2, CHAIN_CHUNKS)),
        ],
        compiler_params=pltpu.CompilerParams(
            collective_id=collective, has_side_effects=True, vmem_limit_bytes=60 * 1024 * 1024
        ),
    )(token_ids.reshape(1, count), ids_all, grad_values[0], grad_scales[0], tables[0])


def merge_by_load(token_ids, grad_values, grad_scales, tables):
    groups = lax.axis_size("vocab")
    rows = tables.shape[1]
    count = token_ids.shape[0]
    capacity = 2 * count // groups
    vmem = pl.BlockSpec(memory_space=pltpu.VMEM)
    dma = pltpu.SemaphoreType.DMA
    ids_all, branch = pl.pallas_call(
        functools.partial(gather_kernel, groups, rows, capacity),
        out_shape=[
            jax.ShapeDtypeStruct((groups, count), jnp.int32),
            jax.ShapeDtypeStruct((1,), jnp.int32),
        ],
        in_specs=[vmem],
        out_specs=[vmem, pl.BlockSpec(memory_space=pltpu.SMEM)],
        scratch_shapes=[
            pltpu.VMEM((8, count), jnp.int32),
            pltpu.VMEM((groups, 8, count), jnp.int32),
            dma((groups,)),
            dma((groups,)),
        ],
        compiler_params=pltpu.CompilerParams(collective_id=0, has_side_effects=True),
    )(token_ids.reshape(1, count))
    args = (token_ids, ids_all, grad_values, grad_scales, tables)
    branches = [functools.partial(merge_chain, load, i + 1) for i, load in enumerate(LOADS)]
    branches.append(lambda ids, _, values, scales, rows: merge_rows(ids, values, scales, rows))
    return lax.switch(branch[0], branches, *args)


def merge_small_slots(token_ids, grad_values, grad_scales, tables):
    groups = lax.axis_size("vocab")
    rows = tables.shape[1]
    width = tables.shape[2]
    count = token_ids.shape[0]
    capacity = 2 * count // groups
    owner = token_ids // rows
    same = owner[:, None] == owner[None, :]
    before = lax.broadcasted_iota(jnp.int32, (count, count), 0) < lax.broadcasted_iota(
        jnp.int32, (count, count), 1
    )
    rank = jnp.sum((same & before).astype(jnp.int32), axis=0)
    slot = owner * capacity + rank
    match = lax.broadcasted_iota(jnp.int32, (groups * capacity, count), 0) == slot[None, :]
    scales = grad_scales[0].T
    grads = (
        grad_values[0].astype(jnp.float32).reshape(count, width // BLK, BLK) * scales[:, :, None]
    )
    squares = (grads * grads).reshape(count, width).astype(jnp.bfloat16)
    placed = jnp.dot(match.astype(jnp.bfloat16), squares, preferred_element_type=jnp.float32)
    buffer = placed.astype(jnp.bfloat16).reshape(groups, capacity, width)
    local_rows = token_ids % rows
    row_tags = (
        jnp.sum(jnp.where(match, local_rows[None, :], 0), axis=1)
        .astype(jnp.bfloat16)
        .reshape(groups, capacity)
    )
    arrived, arrived_rows = (
        lax.all_to_all(buffer, "vocab", split_axis=0, concat_axis=0, tiled=True),
        lax.all_to_all(row_tags, "vocab", split_axis=0, concat_axis=0, tiled=True),
    )
    flat_rows = arrived_rows.reshape(groups * capacity).astype(jnp.int32)
    selector = (
        lax.broadcasted_iota(jnp.int32, (rows, groups * capacity), 0) == flat_rows[None, :]
    ).astype(jnp.bfloat16)
    fisher = jnp.dot(
        selector, arrived.reshape(groups * capacity, width), preferred_element_type=jnp.float32
    )
    weight = (fisher + prior_weight).astype(jnp.bfloat16)
    term = (weight.astype(jnp.float32) * tables[0].astype(jnp.float32)).astype(jnp.bfloat16)
    numer, denom = (
        lax.psum_scatter(term, "ckpt", scatter_dimension=1, tiled=True).astype(jnp.float32),
        lax.psum_scatter(weight, "ckpt", scatter_dimension=1, tiled=True).astype(jnp.float32),
    )
    return (numer / denom).astype(jnp.bfloat16)


def per_device(token_ids, grad_values, grad_scales, tables):
    groups = lax.axis_size("vocab")
    ckpts = lax.axis_size("ckpt")
    count = token_ids.shape[0]
    width = tables.shape[2]
    capacity = 2 * count // groups
    if capacity % 16 == 0 and width % (ckpts * CHUNKS * BLK) == 0:
        if groups == 8 and ckpts == 4:
            return merge_by_load(token_ids, grad_values, grad_scales, tables)
        return merge_rows(token_ids, grad_values, grad_scales, tables)
    return merge_small_slots(token_ids, grad_values, grad_scales, tables)


def solution(mesh):
    return jax.shard_map(
        per_device,
        mesh=mesh,
        in_specs=(
            P("vocab"),
            P("ckpt", "vocab", None),
            P("ckpt", None, "vocab"),
            P("ckpt", "vocab", None),
        ),
        out_specs=P("vocab", "ckpt"),
        check_vma=False,
    )
```

```python
import functools

import jax
import jax.numpy as jnp
from jax import lax
from jax.experimental import pallas as pl
from jax.experimental.pallas import tpu as pltpu
from jax.sharding import PartitionSpec as P

BLK = 128
CHUNKS = 16
CHAIN_CHUNKS = 32
LAG = 4
SETTLE = 2
LOADS = (6, 7, 8, 9, 10)
MESH = pl.DeviceIdType.MESH


prior_weight = 1.0


def merge_kernel(
    groups,
    ckpts,
    chunks,
    ids_ref,
    grads_ref,
    all_scales_ref,
    tables_ref,
    out_ref,
    grads,
    tables,
    scales_ref,
    match_ref,
    select_ref,
    tag_send,
    tag_recv,
    send,
    recv,
    part_send,
    part_recv,
    load_sem,
    tag_send_sem,
    tag_recv_sem,
    send_sem,
    recv_sem,
    part_send_sem,
    part_recv_sem,
):
    c = lax.axis_index("ckpt")
    v = lax.axis_index("vocab")
    rows = tables.shape[0]
    count = grads.shape[0]
    width = grads.shape[1]
    slots = match_ref.shape[0]
    capacity = slots // groups
    quarter = width // ckpts
    piece = quarter // chunks
    blocks = piece // BLK

    def vocab_peer(j):
        return (c, lax.rem(v + j, groups))

    def ckpt_peer(j):
        return (lax.rem(c + j, ckpts), v)

    barrier = pltpu.get_barrier_semaphore()
    for j in range(1, groups):
        pl.semaphore_signal(barrier, inc=1, device_id=vocab_peer(j), device_id_type=MESH)
    for j in range(1, ckpts):
        pl.semaphore_signal(barrier, inc=1, device_id=ckpt_peer(j), device_id_type=MESH)

    load_grads = pltpu.make_async_copy(grads_ref, grads, load_sem.at[0])
    load_tables = pltpu.make_async_copy(tables_ref, tables, load_sem.at[1])
    load_scales = pltpu.make_async_copy(all_scales_ref, scales_ref, load_sem.at[2])
    load_grads.start()
    load_scales.start()
    load_tables.start()

    ids_row = ids_ref[...]
    ids_col = jnp.broadcast_to(ids_row, (count, count)).T
    near_row = lax.rem(ids_row // rows - v + groups, groups)
    near_col = lax.rem(ids_col // rows - v + groups, groups)
    same = near_row == near_col
    at0 = lax.broadcasted_iota(jnp.int32, (count, count), 0)
    at1 = lax.broadcasted_iota(jnp.int32, (count, count), 1)
    rank_row = jnp.sum(jnp.where(same & (at0 < at1), 1, 0), axis=0, keepdims=True)
    rank_col = jnp.sum(jnp.where(same & (at1 < at0), 1, 0), axis=1, keepdims=True)
    slot_row = near_row * capacity + rank_row
    slot_col = near_col * capacity + rank_col
    match_ref[...] = jnp.where(
        lax.broadcasted_iota(jnp.int32, (slots, count), 0) == slot_row, 1.0, 0.0
    ).astype(jnp.bfloat16)
    tags = jnp.sum(
        jnp.where(
            lax.broadcasted_iota(jnp.int32, (count, slots), 1) == slot_col[:, 0:1],
            lax.rem(ids_col[:, 0:1], rows),
            0,
        ),
        axis=0,
        keepdims=True,
    )
    tag_send[...] = jnp.broadcast_to(tags, tag_send.shape)

    def tag_copy(j):
        return pltpu.make_async_remote_copy(
            src_ref=tag_send,
            dst_ref=tag_recv.at[j],
            send_sem=tag_send_sem.at[j],
            recv_sem=tag_recv_sem.at[j],
            device_id=vocab_peer(j),
            device_id_type=MESH,
        )

    def row_copy(k, j):
        return pltpu.make_async_remote_copy(
            src_ref=send.at[k, j],
            dst_ref=recv.at[k, j],
            send_sem=send_sem.at[k, j],
            recv_sem=recv_sem.at[k, j],
            device_id=vocab_peer(j),
            device_id_type=MESH,
        )

    def part_copy(k, j):
        return pltpu.make_async_remote_copy(
            src_ref=part_send.at[k, j],
            dst_ref=part_recv.at[k, j],
            send_sem=part_send_sem.at[k, j],
            recv_sem=part_recv_sem.at[k, j],
            device_id=ckpt_peer(j),
            device_id_type=MESH,
        )

    order = sorted(range(1, groups), key=lambda j: -min(j, groups - j))

    def place(k):
        block_scales = jnp.concatenate(
            [
                scales_ref[pl.ds(q * (quarter // BLK) + k * blocks, blocks), :]
                for q in range(ckpts)
            ],
            axis=0,
        ).T
        squares = []
        for q in range(ckpts):
            for b in range(blocks):
                at = pl.multiple_of(q * quarter + k * piece + b * BLK, BLK)
                i = q * blocks + b
                g = grads[:, pl.ds(at, BLK)].astype(jnp.float32) * block_scales[:, i : i + 1]
                squares.append((g * g).astype(jnp.bfloat16))
        placed = jnp.dot(
            match_ref[...],
            jnp.concatenate(squares, axis=1),
            preferred_element_type=jnp.float32,
        ).astype(jnp.bfloat16)
        placed = placed.reshape(groups, capacity, ckpts * piece)
        recv[k, 0] = placed[0]
        for j in range(1, groups):
            send[k, j] = placed[j]

    def start_rows(k):
        for j in order:
            row_copy(k, j).start()

    load_grads.wait()
    load_scales.wait()
    place(0)
    pl.semaphore_wait(barrier, groups + ckpts - 2)
    for j in order:
        tag_copy(j).start()
    start_rows(0)

    def place_next(k, carry):
        place(k)
        start_rows(k)
        return carry

    lax.fori_loop(1, chunks, place_next, 0)

    lane = lax.broadcasted_iota(jnp.int32, (1, slots), 1) // capacity
    arrived_tags = jnp.where(lane == 0, tags, 0)
    for j in range(1, groups):
        tag_copy(j).wait()
        arrived_tags = jnp.where(lane == j, tag_recv[j, 0:1, :], arrived_tags)
    select_ref[...] = jnp.where(
        lax.broadcasted_iota(jnp.int32, (rows, slots), 0) == arrived_tags, 1.0, 0.0
    ).astype(jnp.bfloat16)
    load_tables.wait()

    def weigh_chunk(k):
        for j in range(1, groups):
            row_copy(k, j).wait_recv()
        fisher = jnp.dot(
            select_ref[...],
            recv[k].reshape(slots, ckpts * piece),
            preferred_element_type=jnp.float32,
        )
        weight = (fisher + prior_weight).astype(jnp.bfloat16)
        for q in range(ckpts):
            own = weight[:, q * piece : (q + 1) * piece]
            at = pl.multiple_of(q * quarter + k * piece, BLK)
            table = tables[:, pl.ds(at, piece)].astype(jnp.float32)
            j = lax.rem(q - c + ckpts, ckpts)
            part_send[k, j, 0] = (own.astype(jnp.float32) * table).astype(jnp.bfloat16)
            part_send[k, j, 1] = own
        for j in range(1, ckpts):
            part_copy(k, j).start()

    def finish_chunk(k):
        numer = part_send[k, 0, 0].astype(jnp.float32)
        denom = part_send[k, 0, 1].astype(jnp.float32)
        for j in range(1, ckpts):
            part_copy(k, j).wait_recv()
            numer += part_recv[k, j, 0].astype(jnp.float32)
            denom += part_recv[k, j, 1].astype(jnp.float32)
        at = pl.multiple_of(k * piece, BLK)
        out_ref[:, pl.ds(at, piece)] = (numer / denom).astype(jnp.bfloat16)

    weigh_chunk(0)

    def step(k, carry):
        weigh_chunk(k)
        finish_chunk(k - 1)
        return carry

    lax.fori_loop(1, chunks, step, 0)
    finish_chunk(chunks - 1)

    def drain(k, carry):
        for j in range(1, groups):
            row_copy(k, j).wait_send()
        for j in range(1, ckpts):
            part_copy(k, j).wait_send()
        return carry

    lax.fori_loop(0, chunks, drain, 0)


def merge_rows(token_ids, grad_values, grad_scales, tables):
    groups = lax.axis_size("vocab")
    ckpts = lax.axis_size("ckpt")
    rows, width = tables.shape[1:]
    count = token_ids.shape[0]
    slots = 2 * count
    capacity = slots // groups
    chunk_width = width // CHUNKS
    vmem = pl.BlockSpec(memory_space=pltpu.VMEM)
    hbm = pl.BlockSpec(memory_space=pl.ANY)
    bf16 = jnp.bfloat16
    dma = pltpu.SemaphoreType.DMA
    return pl.pallas_call(
        functools.partial(merge_kernel, groups, ckpts, CHUNKS),
        out_shape=jax.ShapeDtypeStruct((rows, width // ckpts), bf16),
        in_specs=[vmem, hbm, hbm, hbm],
        out_specs=vmem,
        scratch_shapes=[
            pltpu.VMEM((count, width), bf16),
            pltpu.VMEM((rows, width), bf16),
            pltpu.VMEM((width // BLK, count), jnp.float32),
            pltpu.VMEM((slots, count), bf16),
            pltpu.VMEM((rows, slots), bf16),
            pltpu.VMEM((8, slots), jnp.int32),
            pltpu.VMEM((groups, 8, slots), jnp.int32),
            pltpu.VMEM((CHUNKS, groups, capacity, chunk_width), bf16),
            pltpu.VMEM((CHUNKS, groups, capacity, chunk_width), bf16),
            pltpu.VMEM((CHUNKS, ckpts, 2, rows, chunk_width // ckpts), bf16),
            pltpu.VMEM((CHUNKS, ckpts, 2, rows, chunk_width // ckpts), bf16),
            dma((3,)),
            dma((groups,)),
            dma((groups,)),
            dma((CHUNKS, groups)),
            dma((CHUNKS, groups)),
            dma((CHUNKS, ckpts)),
            dma((CHUNKS, ckpts)),
        ],
        compiler_params=pltpu.CompilerParams(
            collective_id=9, has_side_effects=True, vmem_limit_bytes=60 * 1024 * 1024
        ),
        cost_estimate=pl.CostEstimate(
            flops=4 * slots * count * width,
            bytes_accessed=5 * rows * width,
            transcendentals=0,
        ),
    )(
        token_ids.reshape(1, count),
        grad_values[0],
        grad_scales[0],
        tables[0],
    )


def sort_positions(ids_row, rows):
    count = ids_row.shape[1]
    ids_col = jnp.broadcast_to(ids_row, (count, count)).T
    own_row = ids_row // rows
    own_col = ids_col // rows
    at0 = lax.broadcasted_iota(jnp.int32, (count, count), 0)
    at1 = lax.broadcasted_iota(jnp.int32, (count, count), 1)
    same = own_row == own_col
    first0 = (own_col < own_row) | (same & (at0 < at1))
    first1 = (own_row < own_col) | (same & (at1 < at0))
    pos_row = jnp.sum(jnp.where(first0, 1, 0), axis=0, keepdims=True)
    pos_col = jnp.sum(jnp.where(first1, 1, 0), axis=1, keepdims=True)
    return pos_row, pos_col, ids_col[:, 0:1]


def meet(a, b):
    return lax.dot_general(a, b, (((1,), (1,)), ((), ())), preferred_element_type=jnp.float32)


def id_counts(ids_all, groups, rows):
    count = ids_all.shape[1]
    owners = lax.broadcasted_iota(jnp.int32, (groups, count), 0)
    locals_ = lax.broadcasted_iota(jnp.int32, (rows, count), 0)
    counts = []
    for d in range(groups):
        ids = ids_all[d : d + 1]
        by_owner = jnp.where(owners == ids // rows, 1.0, 0.0).astype(jnp.bfloat16)
        by_row = jnp.where(locals_ == lax.rem(ids, rows), 1.0, 0.0).astype(jnp.bfloat16)
        counts.append(meet(by_owner, by_row))
    return counts


def gather_kernel(groups, rows, capacity, ids_ref, ids_out, branch_out, mine, theirs, send_sem, recv_sem):
    c = lax.axis_index("ckpt")
    v = lax.axis_index("vocab")
    count = ids_ref.shape[1]

    def peer(j):
        return (c, lax.rem(v + j, groups))

    barrier = pltpu.get_barrier_semaphore()
    for j in range(1, groups):
        pl.semaphore_signal(barrier, inc=1, device_id=peer(j), device_id_type=MESH)
    _, pos_col, ids_col = sort_positions(ids_ref[...], rows)
    at1 = lax.broadcasted_iota(jnp.int32, (count, count), 1)
    ordered = jnp.sum(jnp.where(at1 == pos_col, ids_col, 0), axis=0, keepdims=True)
    mine[...] = jnp.broadcast_to(ordered, mine.shape)
    theirs[v] = mine[...]

    def copy(j):
        return pltpu.make_async_remote_copy(
            src_ref=mine,
            dst_ref=theirs.at[v],
            send_sem=send_sem.at[j],
            recv_sem=recv_sem.at[j],
            device_id=peer(j),
            device_id_type=MESH,
        )

    pl.semaphore_wait(barrier, groups - 1)
    for j in range(1, groups):
        copy(j).start()
    for j in range(1, groups):
        copy(j).wait()
    ids_all = jnp.concatenate([theirs[d, 0:1, :] for d in range(groups)], axis=0)
    ids_out[...] = ids_all
    counts = id_counts(ids_all, groups, rows)
    owner_layer = lax.broadcasted_iota(jnp.int32, (groups, rows), 0) // 2
    most = jnp.zeros((1, 1), jnp.float32)
    for cut in range(groups // 2 - 1):
        below = sum(counts[: 2 * cut + 2])
        above = sum(counts[2 * cut + 2 :])
        up = jnp.where((below > 0.0) & (owner_layer > cut), 1.0, 0.0)
        down = jnp.where((above > 0.0) & (owner_layer <= cut), 1.0, 0.0)
        for flow in (up, down):
            total = jnp.sum(jnp.sum(flow, axis=1, keepdims=True), axis=0, keepdims=True)
            most = jnp.maximum(most, total)
    most = jnp.max(most)
    branch_out[0] = sum(jnp.where(most > load * capacity, 1, 0) for load in LOADS)


def chain_kernel(
    groups,
    ckpts,
    chunks,
    span,
    ids_ref,
    ids_all_ref,
    grads_ref,
    all_scales_ref,
    tables_ref,
    out_ref,
    grads,
    tables,
    scales_ref,
    match_ref,
    up_pool_sel,
    up_in_sel,
    down_pool_sel,
    down_in_sel,
    rows_pool_sel,
    rows_up_sel,
    rows_down_sel,
    pool,
    up_in,
    down_in,
    up_out,
    down_out,
    part,
    part_x,
    sum_send,
    sum_recv,
    load_sem,
    pool_sems,
    up_sems,
    up_mate_sems,
    down_sems,
    down_mate_sems,
    x_sems,
    y_sems,
):
    c = lax.axis_index("ckpt")
    v = lax.axis_index("vocab")
    layers = groups // 2
    z = v // 2
    core = v % 2
    mate = v + 1 - 2 * core
    rows = tables.shape[0]
    count = grads.shape[0]
    width = grads.shape[1]
    quarter = width // ckpts
    piece = 2 * quarter // chunks
    blocks = piece // BLK
    bf16 = jnp.bfloat16
    has_up = z < layers - 1
    has_down = z > 0

    y, x = c // 2, c % 2
    x_peer = (y * 2 + 1 - x, v)
    y_peer = ((1 - y) * 2 + x, v)

    def greet(device):
        pl.semaphore_signal(barrier, inc=1, device_id=device, device_id_type=MESH)

    barrier = pltpu.get_barrier_semaphore()
    greet((c, mate))
    greet(x_peer)
    greet(y_peer)

    @pl.when(has_up)
    def _():
        greet((c, v + 2))

    @pl.when(has_down)
    def _():
        greet((c, v - 2))

    load_grads = pltpu.make_async_copy(grads_ref, grads, load_sem.at[0])
    load_tables = pltpu.make_async_copy(tables_ref, tables, load_sem.at[1])
    load_scales = pltpu.make_async_copy(all_scales_ref, scales_ref, load_sem.at[2])
    load_grads.start()
    load_scales.start()
    load_tables.start()

    pos_row, _, _ = sort_positions(ids_ref[...], rows)
    at0 = lax.broadcasted_iota(jnp.int32, (count, count), 0)
    at1 = lax.broadcasted_iota(jnp.int32, (count, count), 1)
    match_ref[...] = jnp.where(at0 == pos_row, 1.0, 0.0).astype(bf16)

    ids_all = ids_all_ref[...]
    counts = id_counts(ids_all, groups, rows)
    owner_layer = lax.broadcasted_iota(jnp.int32, (groups, rows), 0) // 2
    named = lax.broadcasted_iota(jnp.int32, (groups, rows), 0) * rows + lax.broadcasted_iota(
        jnp.int32, (groups, rows), 1
    )
    before = jnp.where(at0 < at1, 1.0, 0.0).astype(bf16)

    def places(mask):
        flags = jnp.where(mask, 1.0, 0.0)
        inner = jnp.dot(flags.astype(bf16), before, preferred_element_type=jnp.float32)
        totals = jnp.sum(flags, axis=1, keepdims=True)
        offset = jnp.zeros((1, 1), jnp.float32)
        offsets = []
        for d in range(groups):
            offsets.append(offset)
            offset = offset + totals[d : d + 1]
        place = (inner + jnp.concatenate(offsets, axis=0)).astype(jnp.int32)
        return jnp.where(mask, place, -1)

    def below(last):
        return sum(jnp.where(d // 2 <= last, counts[d], 0.0) for d in range(groups)) > 0.0

    def above(first):
        return sum(jnp.where(d // 2 >= first, counts[d], 0.0) for d in range(groups)) > 0.0

    up_from = places(below(z - 1) & (owner_layer > z - 1))
    up_to = places(below(z) & (owner_layer > z))
    down_from = places(above(z + 1) & (owner_layer < z + 1))
    down_to = places(above(z) & (owner_layer < z))

    def one_hot(size, values):
        shape = (size, count)
        return jnp.where(
            lax.broadcasted_iota(jnp.int32, shape, 0) == values, 1.0, 0.0
        ).astype(bf16)

    tokens = [
        jnp.broadcast_to(ids_all_ref[pl.ds(2 * z + e, 1), :], (count, count)).T for e in range(2)
    ]
    up_sum = down_sum = rows_up = rows_down = 0.0
    pools = [[0.0, 0.0] for _ in range(3)]
    for d in range(groups):
        take_up = one_hot(span, up_to[d : d + 1] - core * span)
        take_down = one_hot(span, down_to[d : d + 1] - core * span)
        take_rows = one_hot(rows, named[d : d + 1] - v * rows)
        at_up = one_hot(2 * span, up_from[d : d + 1])
        at_down = one_hot(2 * span, down_from[d : d + 1])
        up_sum += meet(take_up, at_up)
        down_sum += meet(take_down, at_down)
        rows_up += meet(take_rows, at_up)
        rows_down += meet(take_rows, at_down)
        for e in range(2):
            at_token = jnp.where(tokens[e] - d * rows == at1, 1.0, 0.0).astype(bf16)
            for i, take in enumerate((take_up, take_down, take_rows)):
                pools[i][e] += meet(take, at_token)
    up_in_sel[...] = up_sum.astype(bf16)
    down_in_sel[...] = down_sum.astype(bf16)
    rows_up_sel[...] = rows_up.astype(bf16)
    rows_down_sel[...] = rows_down.astype(bf16)
    for ref, pair in zip((up_pool_sel, down_pool_sel, rows_pool_sel), pools):
        ref[...] = jnp.concatenate(pair, axis=1).astype(bf16)

    @pl.when(z == 0)
    def _():
        def clear(k, carry):
            up_in[k] = jnp.zeros(up_in.shape[1:], bf16)
            return carry

        lax.fori_loop(0, chunks, clear, 0)

    @pl.when(z == layers - 1)
    def _():
        def clear(k, carry):
            down_in[k] = jnp.zeros(down_in.shape[1:], bf16)
            return carry

        lax.fori_loop(0, chunks, clear, 0)

    def remote(src, dst, sems, k, device):
        return pltpu.make_async_remote_copy(
            src_ref=src,
            dst_ref=dst,
            send_sem=sems.at[0, k],
            recv_sem=sems.at[1, k],
            device_id=device,
            device_id_type=MESH,
        )

    def pool_copy(k):
        return remote(pool.at[k, core], pool.at[k, core], pool_sems, k, (c, mate))

    def up_copy(k):
        return remote(up_out.at[k], up_in.at[k, core], up_sems, k, (c, lax.rem(v + 2, groups)))

    def down_copy(k):
        device = (c, lax.rem(v + groups - 2, groups))
        return remote(down_out.at[k], down_in.at[k, core], down_sems, k, device)

    def up_mate(k):
        return remote(up_in.at[k, core], up_in.at[k, core], up_mate_sems, k, (c, mate))

    def down_mate(k):
        return remote(down_in.at[k, core], down_in.at[k, core], down_mate_sems, k, (c, mate))

    def x_copy(k):
        return remote(part.at[k], part_x.at[k], x_sems, k, x_peer)

    def y_copy(k):
        return remote(sum_send.at[k], sum_recv.at[k], y_sems, k, y_peer)

    def column(k, i):
        return (i * 2 + k % 2) * quarter + (k // 2) * piece

    def place(k):
        block_scales = jnp.concatenate(
            [
                scales_ref[pl.ds(pl.multiple_of(column(k, i) // BLK, blocks), blocks), :]
                for i in range(2)
            ],
            axis=0,
        ).T
        squares = []
        for i in range(2):
            for b in range(blocks):
                at = pl.multiple_of(column(k, i) + b * BLK, BLK)
                n = i * blocks + b
                g = grads[:, pl.ds(at, BLK)].astype(jnp.float32) * block_scales[:, n : n + 1]
                squares.append((g * g).astype(bf16))
        pool[k, core] = jnp.dot(
            match_ref[...],
            jnp.concatenate(squares, axis=1),
            preferred_element_type=jnp.float32,
        ).astype(bf16)

    def pooled(k):
        return pool[k].reshape(2 * count, 2 * piece)

    def arrived(ref, k):
        return ref[k].reshape(2 * span, 2 * piece)

    def dot(a, b):
        return jnp.dot(a, b, preferred_element_type=jnp.float32)

    def weigh_chunk(k):
        fisher = (
            dot(rows_pool_sel[...], pooled(k))
            + dot(rows_up_sel[...], arrived(up_in, k))
            + dot(rows_down_sel[...], arrived(down_in, k))
        )
        weight = (fisher + prior_weight).astype(bf16)
        for i in range(2):
            own = weight[:, i * piece : (i + 1) * piece]
            at = pl.multiple_of(column(k, i), BLK)
            table = tables[:, pl.ds(at, piece)].astype(jnp.float32)
            to_y = (i + y) % 2
            part[k, to_y, 0] = (own.astype(jnp.float32) * table).astype(bf16)
            part[k, to_y, 1] = own

        @pl.when(x != k % 2)
        def _():
            x_copy(k).start()

    def pair_sum(k, to_y, i):
        return part[k, to_y, i].astype(jnp.float32) + part_x[k, to_y, i].astype(jnp.float32)

    def pass_chunk(k):
        x_copy(k).wait_recv()
        for i in range(2):
            sum_send[k, i] = pair_sum(k, 1, i).astype(bf16)
        y_copy(k).start()

    def finish_chunk(k):
        y_copy(k).wait_recv()
        numer = pair_sum(k, 0, 0) + sum_recv[k, 0].astype(jnp.float32)
        denom = pair_sum(k, 0, 1) + sum_recv[k, 1].astype(jnp.float32)
        at = pl.multiple_of((k // 2) * piece, BLK)
        out_ref[:, pl.ds(at, piece)] = (numer / denom).astype(bf16)

    load_grads.wait()
    load_scales.wait()
    load_tables.wait()
    greetings = 3 + jnp.where(has_up, 1, 0) + jnp.where(has_down, 1, 0)
    pl.semaphore_wait(barrier, greetings)

    def inside(k):
        return (k >= 0) & (k < chunks)

    def step(s, carry):
        up = s - LAG * z
        down = s - LAG * (layers - 1 - z)

        @pl.when(inside(s - 1))
        def _():
            pool_copy(s - 1).wait_recv()

        @pl.when(inside(up - 1) & has_down)
        def _():
            up_mate(up - 1).wait_recv()

        @pl.when(inside(up - 1) & has_up)
        def _():
            k = up - 1
            up_out[k] = (
                dot(up_pool_sel[...], pooled(k)) + dot(up_in_sel[...], arrived(up_in, k))
            ).astype(bf16)
            up_copy(k).start()

        @pl.when(inside(down - 1) & has_up)
        def _():
            down_mate(down - 1).wait_recv()

        @pl.when(inside(down - 1) & has_down)
        def _():
            k = down - 1
            down_out[k] = (
                dot(down_pool_sel[...], pooled(k)) + dot(down_in_sel[...], arrived(down_in, k))
            ).astype(bf16)
            down_copy(k).start()

        @pl.when(s < chunks)
        def _():
            place(s)
            pool_copy(s).start()

        @pl.when(inside(up) & has_down)
        def _():
            up_copy(up).wait_recv()
            up_mate(up).start()

        @pl.when(inside(down) & has_up)
        def _():
            down_copy(down).wait_recv()
            down_mate(down).start()

        ready = jnp.minimum(up, down) - 1

        @pl.when(inside(ready))
        def _():
            weigh_chunk(ready)

        @pl.when(inside(ready - SETTLE) & (x == (ready - SETTLE) % 2))
        def _():
            pass_chunk(ready - SETTLE)

        @pl.when(inside(ready - 2 * SETTLE) & (x == ready % 2))
        def _():
            finish_chunk(ready - 2 * SETTLE)

        return carry

    lax.fori_loop(0, chunks + 1 + 2 * SETTLE + LAG * (layers - 1), step, 0)

    def drain(k, carry):
        pool_copy(k).wait_send()

        @pl.when(has_up)
        def _():
            up_copy(k).wait_send()
            down_mate(k).wait_send()

        @pl.when(has_down)
        def _():
            down_copy(k).wait_send()
            up_mate(k).wait_send()

        @pl.when(x != k % 2)
        def _():
            x_copy(k).wait_send()

        @pl.when(x == k % 2)
        def _():
            y_copy(k).wait_send()

        return carry

    lax.fori_loop(0, chunks, drain, 0)


def merge_chain(load, collective, token_ids, ids_all, grad_values, grad_scales, tables):
    groups = lax.axis_size("vocab")
    ckpts = lax.axis_size("ckpt")
    rows, width = tables.shape[1:]
    count = token_ids.shape[0]
    capacity = 2 * count // groups
    piece = width // ckpts * 2 // CHAIN_CHUNKS
    chunk_width = 2 * piece
    span = load * capacity // 2
    vmem = pl.BlockSpec(memory_space=pltpu.VMEM)
    hbm = pl.BlockSpec(memory_space=pl.ANY)
    bf16 = jnp.bfloat16
    dma = pltpu.SemaphoreType.DMA
    return pl.pallas_call(
        functools.partial(chain_kernel, groups, ckpts, CHAIN_CHUNKS, span),
        out_shape=jax.ShapeDtypeStruct((rows, width // ckpts), bf16),
        in_specs=[vmem, vmem, hbm, hbm, hbm],
        out_specs=vmem,
        scratch_shapes=[
            pltpu.VMEM((count, width), bf16),
            pltpu.VMEM((rows, width), bf16),
            pltpu.VMEM((width // BLK, count), jnp.float32),
            pltpu.VMEM((count, count), bf16),
            pltpu.VMEM((span, 2 * count), bf16),
            pltpu.VMEM((span, 2 * span), bf16),
            pltpu.VMEM((span, 2 * count), bf16),
            pltpu.VMEM((span, 2 * span), bf16),
            pltpu.VMEM((rows, 2 * count), bf16),
            pltpu.VMEM((rows, 2 * span), bf16),
            pltpu.VMEM((rows, 2 * span), bf16),
            pltpu.VMEM((CHAIN_CHUNKS, 2, count, chunk_width), bf16),
            pltpu.VMEM((CHAIN_CHUNKS, 2, span, chunk_width), bf16),
            pltpu.VMEM((CHAIN_CHUNKS, 2, span, chunk_width), bf16),
            pltpu.VMEM((CHAIN_CHUNKS, span, chunk_width), bf16),
            pltpu.VMEM((CHAIN_CHUNKS, span, chunk_width), bf16),
            pltpu.VMEM((CHAIN_CHUNKS, 2, 2, rows, piece), bf16),
            pltpu.VMEM((CHAIN_CHUNKS, 2, 2, rows, piece), bf16),
            pltpu.VMEM((CHAIN_CHUNKS, 2, rows, piece), bf16),
            pltpu.VMEM((CHAIN_CHUNKS, 2, rows, piece), bf16),
            dma((3,)),
            dma((2, CHAIN_CHUNKS)),
            dma((2, CHAIN_CHUNKS)),
            dma((2, CHAIN_CHUNKS)),
            dma((2, CHAIN_CHUNKS)),
            dma((2, CHAIN_CHUNKS)),
            dma((2, CHAIN_CHUNKS)),
            dma((2, CHAIN_CHUNKS)),
        ],
        compiler_params=pltpu.CompilerParams(
            collective_id=collective, has_side_effects=True, vmem_limit_bytes=60 * 1024 * 1024
        ),
    )(token_ids.reshape(1, count), ids_all, grad_values[0], grad_scales[0], tables[0])


def merge_by_load(token_ids, grad_values, grad_scales, tables):
    groups = lax.axis_size("vocab")
    rows = tables.shape[1]
    count = token_ids.shape[0]
    capacity = 2 * count // groups
    vmem = pl.BlockSpec(memory_space=pltpu.VMEM)
    dma = pltpu.SemaphoreType.DMA
    ids_all, branch = pl.pallas_call(
        functools.partial(gather_kernel, groups, rows, capacity),
        out_shape=[
            jax.ShapeDtypeStruct((groups, count), jnp.int32),
            jax.ShapeDtypeStruct((1,), jnp.int32),
        ],
        in_specs=[vmem],
        out_specs=[vmem, pl.BlockSpec(memory_space=pltpu.SMEM)],
        scratch_shapes=[
            pltpu.VMEM((8, count), jnp.int32),
            pltpu.VMEM((groups, 8, count), jnp.int32),
            dma((groups,)),
            dma((groups,)),
        ],
        compiler_params=pltpu.CompilerParams(collective_id=0, has_side_effects=True),
    )(token_ids.reshape(1, count))
    args = (token_ids, ids_all, grad_values, grad_scales, tables)
    branches = [functools.partial(merge_chain, load, i + 1) for i, load in enumerate(LOADS)]
    branches.append(lambda ids, _, values, scales, rows: merge_rows(ids, values, scales, rows))
    return lax.switch(branch[0], branches, *args)


def merge_small_slots(token_ids, grad_values, grad_scales, tables):
    groups = lax.axis_size("vocab")
    rows = tables.shape[1]
    width = tables.shape[2]
    count = token_ids.shape[0]
    capacity = 2 * count // groups
    owner = token_ids // rows
    same = owner[:, None] == owner[None, :]
    before = lax.broadcasted_iota(jnp.int32, (count, count), 0) < lax.broadcasted_iota(
        jnp.int32, (count, count), 1
    )
    rank = jnp.sum((same & before).astype(jnp.int32), axis=0)
    slot = owner * capacity + rank
    match = lax.broadcasted_iota(jnp.int32, (groups * capacity, count), 0) == slot[None, :]
    scales = grad_scales[0].T
    grads = (
        grad_values[0].astype(jnp.float32).reshape(count, width // BLK, BLK) * scales[:, :, None]
    )
    squares = (grads * grads).reshape(count, width).astype(jnp.bfloat16)
    placed = jnp.dot(match.astype(jnp.bfloat16), squares, preferred_element_type=jnp.float32)
    buffer = placed.astype(jnp.bfloat16).reshape(groups, capacity, width)
    local_rows = token_ids % rows
    row_tags = (
        jnp.sum(jnp.where(match, local_rows[None, :], 0), axis=1)
        .astype(jnp.bfloat16)
        .reshape(groups, capacity)
    )
    arrived, arrived_rows = (
        lax.all_to_all(buffer, "vocab", split_axis=0, concat_axis=0, tiled=True),
        lax.all_to_all(row_tags, "vocab", split_axis=0, concat_axis=0, tiled=True),
    )
    flat_rows = arrived_rows.reshape(groups * capacity).astype(jnp.int32)
    selector = (
        lax.broadcasted_iota(jnp.int32, (rows, groups * capacity), 0) == flat_rows[None, :]
    ).astype(jnp.bfloat16)
    fisher = jnp.dot(
        selector, arrived.reshape(groups * capacity, width), preferred_element_type=jnp.float32
    )
    weight = (fisher + prior_weight).astype(jnp.bfloat16)
    term = (weight.astype(jnp.float32) * tables[0].astype(jnp.float32)).astype(jnp.bfloat16)
    numer, denom = (
        lax.psum_scatter(term, "ckpt", scatter_dimension=1, tiled=True).astype(jnp.float32),
        lax.psum_scatter(weight, "ckpt", scatter_dimension=1, tiled=True).astype(jnp.float32),
    )
    return (numer / denom).astype(jnp.bfloat16)


def per_device(token_ids, grad_values, grad_scales, tables):
    groups = lax.axis_size("vocab")
    ckpts = lax.axis_size("ckpt")
    count = token_ids.shape[0]
    rows, width = tables.shape[1:]
    capacity = 2 * count // groups
    if capacity % 16 == 0 and width % (ckpts * CHUNKS * BLK) == 0:
        if groups == 8 and ckpts == 4 and rows == count:
            return merge_by_load(token_ids, grad_values, grad_scales, tables)
        return merge_rows(token_ids, grad_values, grad_scales, tables)
    return merge_small_slots(token_ids, grad_values, grad_scales, tables)


def solution(mesh):
    return jax.shard_map(
        per_device,
        mesh=mesh,
        in_specs=(
            P("vocab"),
            P("ckpt", "vocab", None),
            P("ckpt", None, "vocab"),
            P("ckpt", "vocab", None),
        ),
        out_specs=P("vocab", "ckpt"),
        check_vma=False,
    )
```

```python
import functools

import jax
import jax.numpy as jnp
from jax import lax
from jax.experimental import pallas as pl
from jax.experimental.pallas import tpu as pltpu
from jax.sharding import PartitionSpec as P

BLK = 128
CHUNKS = 16
CHAIN_CHUNKS = 16
LAG = 4
SETTLE = 2
LOADS = (6, 7, 8, 9, 10)
MESH = pl.DeviceIdType.MESH


prior_weight = 1.0


def merge_kernel(
    groups,
    ckpts,
    chunks,
    ids_ref,
    grads_ref,
    all_scales_ref,
    tables_ref,
    out_ref,
    grads,
    tables,
    scales_ref,
    match_ref,
    select_ref,
    tag_send,
    tag_recv,
    send,
    recv,
    part_send,
    part_recv,
    load_sem,
    tag_send_sem,
    tag_recv_sem,
    send_sem,
    recv_sem,
    part_send_sem,
    part_recv_sem,
):
    c = lax.axis_index("ckpt")
    v = lax.axis_index("vocab")
    rows = tables.shape[0]
    count = grads.shape[0]
    width = grads.shape[1]
    slots = match_ref.shape[0]
    capacity = slots // groups
    quarter = width // ckpts
    piece = quarter // chunks
    blocks = piece // BLK

    def vocab_peer(j):
        return (c, lax.rem(v + j, groups))

    def ckpt_peer(j):
        return (lax.rem(c + j, ckpts), v)

    barrier = pltpu.get_barrier_semaphore()
    for j in range(1, groups):
        pl.semaphore_signal(barrier, inc=1, device_id=vocab_peer(j), device_id_type=MESH)
    for j in range(1, ckpts):
        pl.semaphore_signal(barrier, inc=1, device_id=ckpt_peer(j), device_id_type=MESH)

    load_grads = pltpu.make_async_copy(grads_ref, grads, load_sem.at[0])
    load_tables = pltpu.make_async_copy(tables_ref, tables, load_sem.at[1])
    load_scales = pltpu.make_async_copy(all_scales_ref, scales_ref, load_sem.at[2])
    load_grads.start()
    load_scales.start()
    load_tables.start()

    ids_row = ids_ref[...]
    ids_col = jnp.broadcast_to(ids_row, (count, count)).T
    near_row = lax.rem(ids_row // rows - v + groups, groups)
    near_col = lax.rem(ids_col // rows - v + groups, groups)
    same = near_row == near_col
    at0 = lax.broadcasted_iota(jnp.int32, (count, count), 0)
    at1 = lax.broadcasted_iota(jnp.int32, (count, count), 1)
    rank_row = jnp.sum(jnp.where(same & (at0 < at1), 1, 0), axis=0, keepdims=True)
    rank_col = jnp.sum(jnp.where(same & (at1 < at0), 1, 0), axis=1, keepdims=True)
    slot_row = near_row * capacity + rank_row
    slot_col = near_col * capacity + rank_col
    match_ref[...] = jnp.where(
        lax.broadcasted_iota(jnp.int32, (slots, count), 0) == slot_row, 1.0, 0.0
    ).astype(jnp.bfloat16)
    tags = jnp.sum(
        jnp.where(
            lax.broadcasted_iota(jnp.int32, (count, slots), 1) == slot_col[:, 0:1],
            lax.rem(ids_col[:, 0:1], rows),
            0,
        ),
        axis=0,
        keepdims=True,
    )
    tag_send[...] = jnp.broadcast_to(tags, tag_send.shape)

    def tag_copy(j):
        return pltpu.make_async_remote_copy(
            src_ref=tag_send,
            dst_ref=tag_recv.at[j],
            send_sem=tag_send_sem.at[j],
            recv_sem=tag_recv_sem.at[j],
            device_id=vocab_peer(j),
            device_id_type=MESH,
        )

    def row_copy(k, j):
        return pltpu.make_async_remote_copy(
            src_ref=send.at[k, j],
            dst_ref=recv.at[k, j],
            send_sem=send_sem.at[k, j],
            recv_sem=recv_sem.at[k, j],
            device_id=vocab_peer(j),
            device_id_type=MESH,
        )

    def part_copy(k, j):
        return pltpu.make_async_remote_copy(
            src_ref=part_send.at[k, j],
            dst_ref=part_recv.at[k, j],
            send_sem=part_send_sem.at[k, j],
            recv_sem=part_recv_sem.at[k, j],
            device_id=ckpt_peer(j),
            device_id_type=MESH,
        )

    order = sorted(range(1, groups), key=lambda j: -min(j, groups - j))

    def place(k):
        block_scales = jnp.concatenate(
            [
                scales_ref[pl.ds(q * (quarter // BLK) + k * blocks, blocks), :]
                for q in range(ckpts)
            ],
            axis=0,
        ).T
        squares = []
        for q in range(ckpts):
            for b in range(blocks):
                at = pl.multiple_of(q * quarter + k * piece + b * BLK, BLK)
                i = q * blocks + b
                g = grads[:, pl.ds(at, BLK)].astype(jnp.float32) * block_scales[:, i : i + 1]
                squares.append((g * g).astype(jnp.bfloat16))
        placed = jnp.dot(
            match_ref[...],
            jnp.concatenate(squares, axis=1),
            preferred_element_type=jnp.float32,
        ).astype(jnp.bfloat16)
        placed = placed.reshape(groups, capacity, ckpts * piece)
        recv[k, 0] = placed[0]
        for j in range(1, groups):
            send[k, j] = placed[j]

    def start_rows(k):
        for j in order:
            row_copy(k, j).start()

    load_grads.wait()
    load_scales.wait()
    place(0)
    pl.semaphore_wait(barrier, groups + ckpts - 2)
    for j in order:
        tag_copy(j).start()
    start_rows(0)

    def place_next(k, carry):
        place(k)
        start_rows(k)
        return carry

    lax.fori_loop(1, chunks, place_next, 0)

    lane = lax.broadcasted_iota(jnp.int32, (1, slots), 1) // capacity
    arrived_tags = jnp.where(lane == 0, tags, 0)
    for j in range(1, groups):
        tag_copy(j).wait()
        arrived_tags = jnp.where(lane == j, tag_recv[j, 0:1, :], arrived_tags)
    select_ref[...] = jnp.where(
        lax.broadcasted_iota(jnp.int32, (rows, slots), 0) == arrived_tags, 1.0, 0.0
    ).astype(jnp.bfloat16)
    load_tables.wait()

    def weigh_chunk(k):
        for j in range(1, groups):
            row_copy(k, j).wait_recv()
        fisher = jnp.dot(
            select_ref[...],
            recv[k].reshape(slots, ckpts * piece),
            preferred_element_type=jnp.float32,
        )
        weight = (fisher + prior_weight).astype(jnp.bfloat16)
        for q in range(ckpts):
            own = weight[:, q * piece : (q + 1) * piece]
            at = pl.multiple_of(q * quarter + k * piece, BLK)
            table = tables[:, pl.ds(at, piece)].astype(jnp.float32)
            j = lax.rem(q - c + ckpts, ckpts)
            part_send[k, j, 0] = (own.astype(jnp.float32) * table).astype(jnp.bfloat16)
            part_send[k, j, 1] = own
        for j in range(1, ckpts):
            part_copy(k, j).start()

    def finish_chunk(k):
        numer = part_send[k, 0, 0].astype(jnp.float32)
        denom = part_send[k, 0, 1].astype(jnp.float32)
        for j in range(1, ckpts):
            part_copy(k, j).wait_recv()
            numer += part_recv[k, j, 0].astype(jnp.float32)
            denom += part_recv[k, j, 1].astype(jnp.float32)
        at = pl.multiple_of(k * piece, BLK)
        out_ref[:, pl.ds(at, piece)] = (numer / denom).astype(jnp.bfloat16)

    weigh_chunk(0)

    def step(k, carry):
        weigh_chunk(k)
        finish_chunk(k - 1)
        return carry

    lax.fori_loop(1, chunks, step, 0)
    finish_chunk(chunks - 1)

    def drain(k, carry):
        for j in range(1, groups):
            row_copy(k, j).wait_send()
        for j in range(1, ckpts):
            part_copy(k, j).wait_send()
        return carry

    lax.fori_loop(0, chunks, drain, 0)


def merge_rows(token_ids, grad_values, grad_scales, tables):
    groups = lax.axis_size("vocab")
    ckpts = lax.axis_size("ckpt")
    rows, width = tables.shape[1:]
    count = token_ids.shape[0]
    slots = 2 * count
    capacity = slots // groups
    chunk_width = width // CHUNKS
    vmem = pl.BlockSpec(memory_space=pltpu.VMEM)
    hbm = pl.BlockSpec(memory_space=pl.ANY)
    bf16 = jnp.bfloat16
    dma = pltpu.SemaphoreType.DMA
    return pl.pallas_call(
        functools.partial(merge_kernel, groups, ckpts, CHUNKS),
        out_shape=jax.ShapeDtypeStruct((rows, width // ckpts), bf16),
        in_specs=[vmem, hbm, hbm, hbm],
        out_specs=vmem,
        scratch_shapes=[
            pltpu.VMEM((count, width), bf16),
            pltpu.VMEM((rows, width), bf16),
            pltpu.VMEM((width // BLK, count), jnp.float32),
            pltpu.VMEM((slots, count), bf16),
            pltpu.VMEM((rows, slots), bf16),
            pltpu.VMEM((8, slots), jnp.int32),
            pltpu.VMEM((groups, 8, slots), jnp.int32),
            pltpu.VMEM((CHUNKS, groups, capacity, chunk_width), bf16),
            pltpu.VMEM((CHUNKS, groups, capacity, chunk_width), bf16),
            pltpu.VMEM((CHUNKS, ckpts, 2, rows, chunk_width // ckpts), bf16),
            pltpu.VMEM((CHUNKS, ckpts, 2, rows, chunk_width // ckpts), bf16),
            dma((3,)),
            dma((groups,)),
            dma((groups,)),
            dma((CHUNKS, groups)),
            dma((CHUNKS, groups)),
            dma((CHUNKS, ckpts)),
            dma((CHUNKS, ckpts)),
        ],
        compiler_params=pltpu.CompilerParams(
            collective_id=9, has_side_effects=True, vmem_limit_bytes=60 * 1024 * 1024
        ),
        cost_estimate=pl.CostEstimate(
            flops=4 * slots * count * width,
            bytes_accessed=5 * rows * width,
            transcendentals=0,
        ),
    )(
        token_ids.reshape(1, count),
        grad_values[0],
        grad_scales[0],
        tables[0],
    )


def sort_positions(ids_row, rows):
    count = ids_row.shape[1]
    ids_col = jnp.broadcast_to(ids_row, (count, count)).T
    own_row = ids_row // rows
    own_col = ids_col // rows
    at0 = lax.broadcasted_iota(jnp.int32, (count, count), 0)
    at1 = lax.broadcasted_iota(jnp.int32, (count, count), 1)
    same = own_row == own_col
    first0 = (own_col < own_row) | (same & (at0 < at1))
    first1 = (own_row < own_col) | (same & (at1 < at0))
    pos_row = jnp.sum(jnp.where(first0, 1, 0), axis=0, keepdims=True)
    pos_col = jnp.sum(jnp.where(first1, 1, 0), axis=1, keepdims=True)
    return pos_row, pos_col, ids_col[:, 0:1]


def meet(a, b):
    return lax.dot_general(a, b, (((1,), (1,)), ((), ())), preferred_element_type=jnp.float32)


def id_counts(ids_all, groups, rows):
    count = ids_all.shape[1]
    owners = lax.broadcasted_iota(jnp.int32, (groups, count), 0)
    locals_ = lax.broadcasted_iota(jnp.int32, (rows, count), 0)
    counts = []
    for d in range(groups):
        ids = ids_all[d : d + 1]
        by_owner = jnp.where(owners == ids // rows, 1.0, 0.0).astype(jnp.bfloat16)
        by_row = jnp.where(locals_ == lax.rem(ids, rows), 1.0, 0.0).astype(jnp.bfloat16)
        counts.append(meet(by_owner, by_row))
    return counts


def gather_kernel(groups, rows, capacity, ids_ref, ids_out, branch_out, mine, theirs, send_sem, recv_sem):
    c = lax.axis_index("ckpt")
    v = lax.axis_index("vocab")
    count = ids_ref.shape[1]

    def peer(j):
        return (c, lax.rem(v + j, groups))

    barrier = pltpu.get_barrier_semaphore()
    for j in range(1, groups):
        pl.semaphore_signal(barrier, inc=1, device_id=peer(j), device_id_type=MESH)
    _, pos_col, ids_col = sort_positions(ids_ref[...], rows)
    at1 = lax.broadcasted_iota(jnp.int32, (count, count), 1)
    ordered = jnp.sum(jnp.where(at1 == pos_col, ids_col, 0), axis=0, keepdims=True)
    mine[...] = jnp.broadcast_to(ordered, mine.shape)
    theirs[v] = mine[...]

    def copy(j):
        return pltpu.make_async_remote_copy(
            src_ref=mine,
            dst_ref=theirs.at[v],
            send_sem=send_sem.at[j],
            recv_sem=recv_sem.at[j],
            device_id=peer(j),
            device_id_type=MESH,
        )

    pl.semaphore_wait(barrier, groups - 1)
    for j in range(1, groups):
        copy(j).start()
    for j in range(1, groups):
        copy(j).wait()
    ids_all = jnp.concatenate([theirs[d, 0:1, :] for d in range(groups)], axis=0)
    ids_out[...] = ids_all
    counts = id_counts(ids_all, groups, rows)
    owner_layer = lax.broadcasted_iota(jnp.int32, (groups, rows), 0) // 2
    most = jnp.zeros((1, 1), jnp.float32)
    for cut in range(groups // 2 - 1):
        below = sum(counts[: 2 * cut + 2])
        above = sum(counts[2 * cut + 2 :])
        up = jnp.where((below > 0.0) & (owner_layer > cut), 1.0, 0.0)
        down = jnp.where((above > 0.0) & (owner_layer <= cut), 1.0, 0.0)
        for flow in (up, down):
            total = jnp.sum(jnp.sum(flow, axis=1, keepdims=True), axis=0, keepdims=True)
            most = jnp.maximum(most, total)
    most = jnp.max(most)
    branch_out[0] = sum(jnp.where(most > load * capacity, 1, 0) for load in LOADS)


def chain_kernel(
    groups,
    ckpts,
    chunks,
    span,
    ids_ref,
    ids_all_ref,
    grads_ref,
    all_scales_ref,
    tables_ref,
    out_ref,
    grads,
    tables,
    scales_ref,
    match_ref,
    up_pool_sel,
    up_in_sel,
    down_pool_sel,
    down_in_sel,
    rows_pool_sel,
    rows_up_sel,
    rows_down_sel,
    pool,
    up_in,
    down_in,
    up_out,
    down_out,
    part,
    part_x,
    sum_send,
    sum_recv,
    load_sem,
    pool_sems,
    up_sems,
    up_mate_sems,
    down_sems,
    down_mate_sems,
    x_sems,
    y_sems,
):
    c = lax.axis_index("ckpt")
    v = lax.axis_index("vocab")
    layers = groups // 2
    z = v // 2
    core = v % 2
    mate = v + 1 - 2 * core
    rows = tables.shape[0]
    count = grads.shape[0]
    width = grads.shape[1]
    quarter = width // ckpts
    piece = 2 * quarter // chunks
    blocks = piece // BLK
    bf16 = jnp.bfloat16
    has_up = z < layers - 1
    has_down = z > 0

    y, x = c // 2, c % 2
    x_peer = (y * 2 + 1 - x, v)
    y_peer = ((1 - y) * 2 + x, v)

    def greet(device):
        pl.semaphore_signal(barrier, inc=1, device_id=device, device_id_type=MESH)

    barrier = pltpu.get_barrier_semaphore()
    greet((c, mate))
    greet(x_peer)
    greet(y_peer)

    @pl.when(has_up)
    def _():
        greet((c, v + 2))

    @pl.when(has_down)
    def _():
        greet((c, v - 2))

    load_grads = pltpu.make_async_copy(grads_ref, grads, load_sem.at[0])
    load_tables = pltpu.make_async_copy(tables_ref, tables, load_sem.at[1])
    load_scales = pltpu.make_async_copy(all_scales_ref, scales_ref, load_sem.at[2])
    load_grads.start()
    load_scales.start()
    load_tables.start()

    pos_row, _, _ = sort_positions(ids_ref[...], rows)
    at0 = lax.broadcasted_iota(jnp.int32, (count, count), 0)
    at1 = lax.broadcasted_iota(jnp.int32, (count, count), 1)
    match_ref[...] = jnp.where(at0 == pos_row, 1.0, 0.0).astype(bf16)

    ids_all = ids_all_ref[...]
    counts = id_counts(ids_all, groups, rows)
    owner_layer = lax.broadcasted_iota(jnp.int32, (groups, rows), 0) // 2
    named = lax.broadcasted_iota(jnp.int32, (groups, rows), 0) * rows + lax.broadcasted_iota(
        jnp.int32, (groups, rows), 1
    )
    before = jnp.where(at0 < at1, 1.0, 0.0).astype(bf16)

    def places(mask):
        flags = jnp.where(mask, 1.0, 0.0)
        inner = jnp.dot(flags.astype(bf16), before, preferred_element_type=jnp.float32)
        totals = jnp.sum(flags, axis=1, keepdims=True)
        offset = jnp.zeros((1, 1), jnp.float32)
        offsets = []
        for d in range(groups):
            offsets.append(offset)
            offset = offset + totals[d : d + 1]
        place = (inner + jnp.concatenate(offsets, axis=0)).astype(jnp.int32)
        return jnp.where(mask, place, -1)

    def below(last):
        return sum(jnp.where(d // 2 <= last, counts[d], 0.0) for d in range(groups)) > 0.0

    def above(first):
        return sum(jnp.where(d // 2 >= first, counts[d], 0.0) for d in range(groups)) > 0.0

    up_from = places(below(z - 1) & (owner_layer > z - 1))
    up_to = places(below(z) & (owner_layer > z))
    down_from = places(above(z + 1) & (owner_layer < z + 1))
    down_to = places(above(z) & (owner_layer < z))

    def one_hot(size, values):
        shape = (size, count)
        return jnp.where(
            lax.broadcasted_iota(jnp.int32, shape, 0) == values, 1.0, 0.0
        ).astype(bf16)

    tokens = [
        jnp.broadcast_to(ids_all_ref[pl.ds(2 * z + e, 1), :], (count, count)).T for e in range(2)
    ]
    up_sum = down_sum = rows_up = rows_down = 0.0
    pools = [[0.0, 0.0] for _ in range(3)]
    for d in range(groups):
        take_up = one_hot(span, up_to[d : d + 1] - core * span)
        take_down = one_hot(span, down_to[d : d + 1] - core * span)
        take_rows = one_hot(rows, named[d : d + 1] - v * rows)
        at_up = one_hot(2 * span, up_from[d : d + 1])
        at_down = one_hot(2 * span, down_from[d : d + 1])
        up_sum += meet(take_up, at_up)
        down_sum += meet(take_down, at_down)
        rows_up += meet(take_rows, at_up)
        rows_down += meet(take_rows, at_down)
        for e in range(2):
            at_token = jnp.where(tokens[e] - d * rows == at1, 1.0, 0.0).astype(bf16)
            for i, take in enumerate((take_up, take_down, take_rows)):
                pools[i][e] += meet(take, at_token)
    up_in_sel[...] = up_sum.astype(bf16)
    down_in_sel[...] = down_sum.astype(bf16)
    rows_up_sel[...] = rows_up.astype(bf16)
    rows_down_sel[...] = rows_down.astype(bf16)
    for ref, pair in zip((up_pool_sel, down_pool_sel, rows_pool_sel), pools):
        ref[...] = jnp.concatenate(pair, axis=1).astype(bf16)

    @pl.when(z == 0)
    def _():
        def clear(k, carry):
            up_in[k] = jnp.zeros(up_in.shape[1:], bf16)
            return carry

        lax.fori_loop(0, chunks, clear, 0)

    @pl.when(z == layers - 1)
    def _():
        def clear(k, carry):
            down_in[k] = jnp.zeros(down_in.shape[1:], bf16)
            return carry

        lax.fori_loop(0, chunks, clear, 0)

    def remote(src, dst, sems, k, device):
        return pltpu.make_async_remote_copy(
            src_ref=src,
            dst_ref=dst,
            send_sem=sems.at[0, k],
            recv_sem=sems.at[1, k],
            device_id=device,
            device_id_type=MESH,
        )

    def pool_copy(k):
        return remote(pool.at[k, core], pool.at[k, core], pool_sems, k, (c, mate))

    def up_copy(k):
        return remote(up_out.at[k], up_in.at[k, core], up_sems, k, (c, lax.rem(v + 2, groups)))

    def down_copy(k):
        device = (c, lax.rem(v + groups - 2, groups))
        return remote(down_out.at[k], down_in.at[k, core], down_sems, k, device)

    def up_mate(k):
        return remote(up_in.at[k, core], up_in.at[k, core], up_mate_sems, k, (c, mate))

    def down_mate(k):
        return remote(down_in.at[k, core], down_in.at[k, core], down_mate_sems, k, (c, mate))

    def x_copy(k):
        return remote(part.at[k], part_x.at[k], x_sems, k, x_peer)

    def y_copy(k):
        return remote(sum_send.at[k], sum_recv.at[k], y_sems, k, y_peer)

    def column(k, i):
        return (i * 2 + k % 2) * quarter + (k // 2) * piece

    def place(k):
        block_scales = jnp.concatenate(
            [
                scales_ref[pl.ds(pl.multiple_of(column(k, i) // BLK, blocks), blocks), :]
                for i in range(2)
            ],
            axis=0,
        ).T
        squares = []
        for i in range(2):
            for b in range(blocks):
                at = pl.multiple_of(column(k, i) + b * BLK, BLK)
                n = i * blocks + b
                g = grads[:, pl.ds(at, BLK)].astype(jnp.float32) * block_scales[:, n : n + 1]
                squares.append((g * g).astype(bf16))
        pool[k, core] = jnp.dot(
            match_ref[...],
            jnp.concatenate(squares, axis=1),
            preferred_element_type=jnp.float32,
        ).astype(bf16)

    def pooled(k):
        return pool[k].reshape(2 * count, 2 * piece)

    def arrived(ref, k):
        return ref[k].reshape(2 * span, 2 * piece)

    def dot(a, b):
        return jnp.dot(a, b, preferred_element_type=jnp.float32)

    def weigh_chunk(k):
        fisher = (
            dot(rows_pool_sel[...], pooled(k))
            + dot(rows_up_sel[...], arrived(up_in, k))
            + dot(rows_down_sel[...], arrived(down_in, k))
        )
        weight = (fisher + prior_weight).astype(bf16)
        for i in range(2):
            own = weight[:, i * piece : (i + 1) * piece]
            at = pl.multiple_of(column(k, i), BLK)
            table = tables[:, pl.ds(at, piece)].astype(jnp.float32)
            to_y = (i + y) % 2
            part[k, to_y, 0] = (own.astype(jnp.float32) * table).astype(bf16)
            part[k, to_y, 1] = own

        @pl.when(x != k % 2)
        def _():
            x_copy(k).start()

    def pair_sum(k, to_y, i):
        return part[k, to_y, i].astype(jnp.float32) + part_x[k, to_y, i].astype(jnp.float32)

    def pass_chunk(k):
        x_copy(k).wait_recv()
        for i in range(2):
            sum_send[k, i] = pair_sum(k, 1, i).astype(bf16)
        y_copy(k).start()

    def finish_chunk(k):
        y_copy(k).wait_recv()
        numer = pair_sum(k, 0, 0) + sum_recv[k, 0].astype(jnp.float32)
        denom = pair_sum(k, 0, 1) + sum_recv[k, 1].astype(jnp.float32)
        at = pl.multiple_of((k // 2) * piece, BLK)
        out_ref[:, pl.ds(at, piece)] = (numer / denom).astype(bf16)

    load_grads.wait()
    load_scales.wait()
    load_tables.wait()
    greetings = 3 + jnp.where(has_up, 1, 0) + jnp.where(has_down, 1, 0)
    pl.semaphore_wait(barrier, greetings)

    def inside(k):
        return (k >= 0) & (k < chunks)

    def step(s, carry):
        up = s - LAG * z
        down = s - LAG * (layers - 1 - z)

        @pl.when(inside(s - 1))
        def _():
            pool_copy(s - 1).wait_recv()

        @pl.when(inside(up - 1) & has_down)
        def _():
            up_mate(up - 1).wait_recv()

        @pl.when(inside(up - 1) & has_up)
        def _():
            k = up - 1
            up_out[k] = (
                dot(up_pool_sel[...], pooled(k)) + dot(up_in_sel[...], arrived(up_in, k))
            ).astype(bf16)
            up_copy(k).start()

        @pl.when(inside(down - 1) & has_up)
        def _():
            down_mate(down - 1).wait_recv()

        @pl.when(inside(down - 1) & has_down)
        def _():
            k = down - 1
            down_out[k] = (
                dot(down_pool_sel[...], pooled(k)) + dot(down_in_sel[...], arrived(down_in, k))
            ).astype(bf16)
            down_copy(k).start()

        @pl.when(s < chunks)
        def _():
            place(s)
            pool_copy(s).start()

        @pl.when(inside(up) & has_down)
        def _():
            up_copy(up).wait_recv()
            up_mate(up).start()

        @pl.when(inside(down) & has_up)
        def _():
            down_copy(down).wait_recv()
            down_mate(down).start()

        ready = jnp.minimum(up, down) - 1

        @pl.when(inside(ready))
        def _():
            weigh_chunk(ready)

        @pl.when(inside(ready - SETTLE) & (x == (ready - SETTLE) % 2))
        def _():
            pass_chunk(ready - SETTLE)

        @pl.when(inside(ready - 2 * SETTLE) & (x == ready % 2))
        def _():
            finish_chunk(ready - 2 * SETTLE)

        return carry

    lax.fori_loop(0, chunks + 1 + 2 * SETTLE + LAG * (layers - 1), step, 0)

    def drain(k, carry):
        pool_copy(k).wait_send()

        @pl.when(has_up)
        def _():
            up_copy(k).wait_send()
            down_mate(k).wait_send()

        @pl.when(has_down)
        def _():
            down_copy(k).wait_send()
            up_mate(k).wait_send()

        @pl.when(x != k % 2)
        def _():
            x_copy(k).wait_send()

        @pl.when(x == k % 2)
        def _():
            y_copy(k).wait_send()

        return carry

    lax.fori_loop(0, chunks, drain, 0)


def merge_chain(load, collective, token_ids, ids_all, grad_values, grad_scales, tables):
    groups = lax.axis_size("vocab")
    ckpts = lax.axis_size("ckpt")
    rows, width = tables.shape[1:]
    count = token_ids.shape[0]
    capacity = 2 * count // groups
    piece = width // ckpts * 2 // CHAIN_CHUNKS
    chunk_width = 2 * piece
    span = load * capacity // 2
    vmem = pl.BlockSpec(memory_space=pltpu.VMEM)
    hbm = pl.BlockSpec(memory_space=pl.ANY)
    bf16 = jnp.bfloat16
    dma = pltpu.SemaphoreType.DMA
    return pl.pallas_call(
        functools.partial(chain_kernel, groups, ckpts, CHAIN_CHUNKS, span),
        out_shape=jax.ShapeDtypeStruct((rows, width // ckpts), bf16),
        in_specs=[vmem, vmem, hbm, hbm, hbm],
        out_specs=vmem,
        scratch_shapes=[
            pltpu.VMEM((count, width), bf16),
            pltpu.VMEM((rows, width), bf16),
            pltpu.VMEM((width // BLK, count), jnp.float32),
            pltpu.VMEM((count, count), bf16),
            pltpu.VMEM((span, 2 * count), bf16),
            pltpu.VMEM((span, 2 * span), bf16),
            pltpu.VMEM((span, 2 * count), bf16),
            pltpu.VMEM((span, 2 * span), bf16),
            pltpu.VMEM((rows, 2 * count), bf16),
            pltpu.VMEM((rows, 2 * span), bf16),
            pltpu.VMEM((rows, 2 * span), bf16),
            pltpu.VMEM((CHAIN_CHUNKS, 2, count, chunk_width), bf16),
            pltpu.VMEM((CHAIN_CHUNKS, 2, span, chunk_width), bf16),
            pltpu.VMEM((CHAIN_CHUNKS, 2, span, chunk_width), bf16),
            pltpu.VMEM((CHAIN_CHUNKS, span, chunk_width), bf16),
            pltpu.VMEM((CHAIN_CHUNKS, span, chunk_width), bf16),
            pltpu.VMEM((CHAIN_CHUNKS, 2, 2, rows, piece), bf16),
            pltpu.VMEM((CHAIN_CHUNKS, 2, 2, rows, piece), bf16),
            pltpu.VMEM((CHAIN_CHUNKS, 2, rows, piece), bf16),
            pltpu.VMEM((CHAIN_CHUNKS, 2, rows, piece), bf16),
            dma((3,)),
            dma((2, CHAIN_CHUNKS)),
            dma((2, CHAIN_CHUNKS)),
            dma((2, CHAIN_CHUNKS)),
            dma((2, CHAIN_CHUNKS)),
            dma((2, CHAIN_CHUNKS)),
            dma((2, CHAIN_CHUNKS)),
            dma((2, CHAIN_CHUNKS)),
        ],
        compiler_params=pltpu.CompilerParams(
            collective_id=collective, has_side_effects=True, vmem_limit_bytes=60 * 1024 * 1024
        ),
    )(token_ids.reshape(1, count), ids_all, grad_values[0], grad_scales[0], tables[0])


def merge_by_load(token_ids, grad_values, grad_scales, tables):
    groups = lax.axis_size("vocab")
    rows = tables.shape[1]
    count = token_ids.shape[0]
    capacity = 2 * count // groups
    vmem = pl.BlockSpec(memory_space=pltpu.VMEM)
    dma = pltpu.SemaphoreType.DMA
    ids_all, branch = pl.pallas_call(
        functools.partial(gather_kernel, groups, rows, capacity),
        out_shape=[
            jax.ShapeDtypeStruct((groups, count), jnp.int32),
            jax.ShapeDtypeStruct((1,), jnp.int32),
        ],
        in_specs=[vmem],
        out_specs=[vmem, pl.BlockSpec(memory_space=pltpu.SMEM)],
        scratch_shapes=[
            pltpu.VMEM((8, count), jnp.int32),
            pltpu.VMEM((groups, 8, count), jnp.int32),
            dma((groups,)),
            dma((groups,)),
        ],
        compiler_params=pltpu.CompilerParams(collective_id=0, has_side_effects=True),
    )(token_ids.reshape(1, count))
    args = (token_ids, ids_all, grad_values, grad_scales, tables)
    branches = [functools.partial(merge_chain, load, i + 1) for i, load in enumerate(LOADS)]
    branches.append(lambda ids, _, values, scales, rows: merge_rows(ids, values, scales, rows))
    return lax.switch(branch[0], branches, *args)


def merge_small_slots(token_ids, grad_values, grad_scales, tables):
    groups = lax.axis_size("vocab")
    rows = tables.shape[1]
    width = tables.shape[2]
    count = token_ids.shape[0]
    capacity = 2 * count // groups
    owner = token_ids // rows
    same = owner[:, None] == owner[None, :]
    before = lax.broadcasted_iota(jnp.int32, (count, count), 0) < lax.broadcasted_iota(
        jnp.int32, (count, count), 1
    )
    rank = jnp.sum((same & before).astype(jnp.int32), axis=0)
    slot = owner * capacity + rank
    match = lax.broadcasted_iota(jnp.int32, (groups * capacity, count), 0) == slot[None, :]
    scales = grad_scales[0].T
    grads = (
        grad_values[0].astype(jnp.float32).reshape(count, width // BLK, BLK) * scales[:, :, None]
    )
    squares = (grads * grads).reshape(count, width).astype(jnp.bfloat16)
    placed = jnp.dot(match.astype(jnp.bfloat16), squares, preferred_element_type=jnp.float32)
    buffer = placed.astype(jnp.bfloat16).reshape(groups, capacity, width)
    local_rows = token_ids % rows
    row_tags = (
        jnp.sum(jnp.where(match, local_rows[None, :], 0), axis=1)
        .astype(jnp.bfloat16)
        .reshape(groups, capacity)
    )
    arrived, arrived_rows = (
        lax.all_to_all(buffer, "vocab", split_axis=0, concat_axis=0, tiled=True),
        lax.all_to_all(row_tags, "vocab", split_axis=0, concat_axis=0, tiled=True),
    )
    flat_rows = arrived_rows.reshape(groups * capacity).astype(jnp.int32)
    selector = (
        lax.broadcasted_iota(jnp.int32, (rows, groups * capacity), 0) == flat_rows[None, :]
    ).astype(jnp.bfloat16)
    fisher = jnp.dot(
        selector, arrived.reshape(groups * capacity, width), preferred_element_type=jnp.float32
    )
    weight = (fisher + prior_weight).astype(jnp.bfloat16)
    term = (weight.astype(jnp.float32) * tables[0].astype(jnp.float32)).astype(jnp.bfloat16)
    numer, denom = (
        lax.psum_scatter(term, "ckpt", scatter_dimension=1, tiled=True).astype(jnp.float32),
        lax.psum_scatter(weight, "ckpt", scatter_dimension=1, tiled=True).astype(jnp.float32),
    )
    return (numer / denom).astype(jnp.bfloat16)


def per_device(token_ids, grad_values, grad_scales, tables):
    groups = lax.axis_size("vocab")
    ckpts = lax.axis_size("ckpt")
    count = token_ids.shape[0]
    rows, width = tables.shape[1:]
    capacity = 2 * count // groups
    if capacity % 16 == 0 and width % (ckpts * CHUNKS * BLK) == 0:
        if groups == 8 and ckpts == 4 and rows == count:
            return merge_by_load(token_ids, grad_values, grad_scales, tables)
        return merge_rows(token_ids, grad_values, grad_scales, tables)
    return merge_small_slots(token_ids, grad_values, grad_scales, tables)


def solution(mesh):
    return jax.shard_map(
        per_device,
        mesh=mesh,
        in_specs=(
            P("vocab"),
            P("ckpt", "vocab", None),
            P("ckpt", None, "vocab"),
            P("ckpt", "vocab", None),
        ),
        out_specs=P("vocab", "ckpt"),
        check_vma=False,
    )
```
